128 devices in a mesh: lat: 4 (over z_hi, core), lon: 32 (over x, y, z_lo).
Axes of the slice: x: 4, y: 4, z: 4 (z_hi: 2, z_lo: 2; z = z_hi * 2 + z_lo), core: 2. Of those that a mesh axis runs over, the one named last changes fastest.
Arguments:
- terrain_surface: float32 [1024, 32768], P('lat', 'lon')
- azimuth_lag_tallies: int32 [8, 8], replicated, may hold values from 1 to 128, as said below
- holder_devices: int32 [524288, 1], P(('lat', 'lon')), may hold values from 0 to 127; in each aligned block of 4096 rows (0 to 4095, 4096 to 8191, ...) at most 128 rows name the same one
- holder_region_slot: int32 [524288], P(('lat', 'lon')), may hold values from 0 to 511
- footprint_weight: int32 [524288], P(('lat', 'lon')), may hold values from 1 to 64
Outputs:
- fine_svf: float32 [1024, 32768], P('lat', 'lon')
- cell_horizon: float32 [8, 65536], P(None, ('lat', 'lon'))
- cell_svf: float32 [65536], P(('lat', 'lon'))
The draws below stay inside these ranges and needn't reach their ends.
Inputs may be any that keep to these rules, and one draw needn't show every extreme that they name: `holder_devices`: in the blocks of one device no owner is named by more than 128 blocks, a bound that some block reaches. `azimuth_lag_tallies`: every azimuth has a distance of 128.
All inputs are finite; a program needn't handle non-finite values.
Results may differ from the reference program's by a relative error of at most 0.0003.
Values sent between devices are 32-bit elements; how exact they have to be, the bound alone decides.
No kernel may reach another device: no remote copies, remote signals or barrier semaphores. Data moves between devices by JAX's collectives and lax.ppermute only.
A program may use at most 192 MiB of HBM per device.

```python
import math
import jax
import jax.numpy as jnp
import numpy as np
from jax import lax

RY = 256
CX = 1024
FARTHEST_LAG = 128
AZ = 8
KS = 8
BY = 8
BX = 8
CELLS_DEV = 512
NY = 1024
NX = 32768
NB = 4096
CAP = 128
BLOCKS = 524288
CELLS = 65536
N_LAT = 4
N_LON = 32


def draw_terrain_surface(key, part):
    key = jax.random.fold_in(key, 11)
    keys = jax.random.split(key, 16)
    rows = jnp.arange(NY, dtype=jnp.float32)[:, None]
    cols = jnp.arange(NX, dtype=jnp.float32)[None, :]
    total = jnp.zeros((NY, NX), jnp.float32)
    for number, factor in enumerate((1.0, 0.6, 0.35)):
        span_y = jax.random.uniform(keys[4 * number], (), jnp.float32, FARTHEST_LAG * 1.0, FARTHEST_LAG * 3.0) * factor
        span_x = jax.random.uniform(keys[4 * number + 1], (), jnp.float32, FARTHEST_LAG * 1.0, FARTHEST_LAG * 3.0) * factor
        phase_y = jax.random.uniform(keys[4 * number + 2], (), jnp.float32, 0.0, 1.0)
        phase_x = jax.random.uniform(keys[4 * number + 3], (), jnp.float32, 0.0, 1.0)
        wave_y = jnp.cos(2.0 * jnp.pi * jnp.mod(rows / span_y + phase_y, 1.0))
        wave_x = jnp.sin(2.0 * jnp.pi * jnp.mod(cols / span_x + phase_x, 1.0))
        total = total + factor * wave_y * wave_x
    rough = 20.0 * jax.random.normal(keys[13], (NY, NX), jnp.float32)
    relief = 1000.0
    return (1500.0 + relief * total + rough).astype(jnp.float32)


def draw_azimuth_lag_tallies(key, part):
    key = jax.random.fold_in(key, 12)
    first, second = jax.random.split(key)
    steps = jax.random.randint(first, (AZ, KS), 1, FARTHEST_LAG + 1)
    where_top = jax.random.randint(second, (AZ, 1), 0, KS)
    return jnp.where(jnp.arange(KS)[None, :] == where_top, FARTHEST_LAG, steps).astype(jnp.int32)


def place_ends(entries, rng, least, high):
    extent = entries.shape
    spot = [jax.random.randint(jax.random.fold_in(rng, axis), (), 0, extent[axis]) for axis in range(len(extent))]
    entries = entries.at[tuple(spot)].set(least)
    longest = extent.index(max(extent))
    spot[longest] = (spot[longest] + 1) % extent[longest]
    return entries.at[tuple(spot)].set(high)


def routed_block(own_key, own, number, rows, count, top, bound, skew):
    sequence = jax.random.permutation(own_key, count)
    packed, ordinary = shares(count, rows * top, bound, skew, True), shares(count, rows * top, bound, skew, False)
    places = jnp.arange(count)

    def named(tallies, turn):
        used = int((tallies > 0).sum())
        fixed = max(1, used // 4)
        shifted = fixed + (places - fixed + turn * (used - fixed)) % max(1, count - fixed)
        return jnp.zeros((count,), jnp.int32).at[sequence[jnp.where(places < fixed, places, shifted)]].set(jnp.asarray(tallies, jnp.int32))

    tallies = jnp.where(number % 4 == 0, named(packed, number // 4), named(ordinary, number - number // 4 - 1))
    mixed = jax.random.permutation(jax.random.fold_in(own, 3), count)
    giver, sink = mixed[0:count // 2 * 2:2], mixed[1:count // 2 * 2:2]
    margin = jnp.minimum(tallies[giver] - 1, bound - tallies[sink]) // 2
    margin = jnp.where((giver == sequence[0]) | (sink == sequence[0]) | (tallies[sink] == 0), 0, jnp.maximum(margin, 0))
    shifted = jax.random.randint(jax.random.fold_in(own, 4), (count // 2,), 0, 1 << 20) % (margin + 1)
    tallies = tallies.at[giver].add(-shifted).at[sink].add(shifted)
    labels = jnp.searchsorted(jnp.cumsum(tallies), jnp.arange(rows * top), side="right").astype(jnp.int32)
    grid = labels.reshape(top, rows).T
    grid = grid[jax.random.permutation(jax.random.fold_in(own, 1), rows)]
    turn = jax.random.randint(jax.random.fold_in(own, 2), (rows, 1), 0, top)
    return jnp.take_along_axis(grid, (jnp.arange(top)[None, :] + turn) % top, axis=1)


def shares(amount, total, most, skew, full):
    weights = [(1 << 20) // math.isqrt(grade ** skew) + 1 for grade in range(1, amount + 1)]
    largest = most if full else min(most, max(-(-total // amount), total * weights[0] // sum(weights)))
    least = 1 if total - largest >= amount - 1 else 0
    counts, surplus = [largest] + [least] * (amount - 1), total - largest - least * (amount - 1)
    while surplus > 0:
        movable = [i for i in range(1, amount) if counts[i] < largest] or [i for i in range(1, amount) if counts[i] < most]
        pool, left = sum([weights[i] for i in movable]), surplus
        for i in movable:
            addition = min(most - counts[i], max(1, left * weights[i] // pool), surplus)
            counts[i] = counts[i] + addition
            surplus = surplus - addition
    return np.array(counts)


def setup_inputs(seed: int = 0) -> dict:
    key_of = jax.random.split(jax.random.key(seed), 6)
    terrain_surface = draw_terrain_surface(jax.random.fold_in(key_of[5], 71), 0)
    azimuth_lag_tallies = draw_azimuth_lag_tallies(jax.random.fold_in(key_of[5], 71), 0)
    holder_devices_keys = jax.random.split(jax.random.fold_in(key_of[2], 1), BLOCKS // NB)
    holder_devices_turns = jax.random.permutation(jax.random.fold_in(key_of[2], 3), BLOCKS // NB)
    holder_devices = jax.vmap(lambda own, number: routed_block(jax.random.fold_in(key_of[2], 2), own, number, NB, N_LAT * N_LON, 1, CAP, 2))(holder_devices_keys, holder_devices_turns).reshape((BLOCKS, 1))
    holder_region_slot = place_ends(jax.random.randint(key_of[3], (BLOCKS,), 0, CELLS_DEV), jax.random.fold_in(key_of[3], 1), 0, CELLS_DEV - 1).astype(jnp.int32)
    footprint_weight = place_ends(jax.random.randint(key_of[4], (BLOCKS,), 1, 65), jax.random.fold_in(key_of[4], 1), 1, 64).astype(jnp.int32)
    return dict(terrain_surface=terrain_surface, azimuth_lag_tallies=azimuth_lag_tallies, holder_devices=holder_devices, holder_region_slot=holder_region_slot, footprint_weight=footprint_weight)


directions = ((0, 1), (1, 1), (1, 0), (1, -1), (0, -1), (-1, -1), (-1, 0), (-1, 1))
pixel_size = 92.6

def block_means(field):
    shaped = field.reshape(N_LAT, RY // BY, BY, N_LON, CX // BX, BX)
    summed = shaped.sum(axis=(2, 5)) / (BY * BX)
    return summed.transpose(0, 2, 1, 3).reshape(-1)

def reference(terrain_surface, azimuth_lag_tallies, holder_devices, holder_region_slot, footprint_weight):
    haloed_altitude = jnp.pad(terrain_surface, ((0, 0), (FARTHEST_LAG, FARTHEST_LAG)), mode='wrap')
    haloed_altitude = jnp.pad(haloed_altitude, ((FARTHEST_LAG, FARTHEST_LAG), (0, 0)), mode='edge')
    rows_global = jnp.arange(NY, dtype=jnp.float32)
    latitude = 47.0 - (rows_global + 0.5) / 1200.0
    coslat = jnp.cos(latitude * jnp.pi / 180.0)[:, None]
    weight = footprint_weight.astype(jnp.float32) / 64.0
    gid = (holder_devices[:, 0] * CELLS_DEV + holder_region_slot).astype(jnp.int32)
    svf_total = jnp.zeros((NY, NX), jnp.float32)
    horizon_rows = []
    opening_total = jnp.zeros((CELLS,), jnp.float32)
    for azimuth in range(AZ):
        step_y, step_x = directions[azimuth]
        observer_altitude = jnp.sqrt((step_y * pixel_size) ** 2 + (step_x * pixel_size * coslat) ** 2)

        def sample(best, walking_offset):
            start_y = (FARTHEST_LAG + step_y * walking_offset).astype(jnp.int32)
            start_x = (FARTHEST_LAG + step_x * walking_offset).astype(jnp.int32)
            device_subgrid = lax.dynamic_slice(haloed_altitude, (start_y, start_x), (NY, NX))
            ascent_slope = (device_subgrid - terrain_surface) / (walking_offset.astype(jnp.float32) * observer_altitude)
            return (jnp.maximum(best, ascent_slope), None)
        best, unused = lax.scan(sample, jnp.full((NY, NX), -jnp.inf, jnp.float32), azimuth_lag_tallies[azimuth])
        rise = jnp.maximum(best, 0.0)
        angle = jnp.arctan(rise)
        opening = 1.0 / (1.0 + rise * rise)
        svf_total = svf_total + opening
        horizon_rows.append(jax.ops.segment_sum(weight * block_means(angle), gid, CELLS))
        opening_total = opening_total + jax.ops.segment_sum(weight * block_means(opening), gid, CELLS)
    area_sum = jax.ops.segment_sum(weight, gid, CELLS)
    floor_area = jnp.maximum(area_sum, 1.0)
    fine_svf = svf_total / AZ
    cell_horizon = jnp.stack(horizon_rows) / floor_area[None, :]
    cell_svf = opening_total / (AZ * floor_area)
    return (fine_svf, cell_horizon, cell_svf)
```

```python
import jax
import jax.numpy as jnp
from jax import lax
from jax.experimental import pallas as pl
from jax.experimental.pallas import tpu as pltpu

FARTHEST_LAG = 128
AZ = 8
KS = 8
directions = ((0, 1), (1, 1), (1, 0), (1, -1), (0, -1), (-1, -1), (-1, 0), (-1, 1))
pixel_size = 92.6
ATAN = (0.9999999, -0.33331991, 0.19969724, -0.14019481, 0.09914293, -0.05948639, 0.0242524, -0.00469327)
HALF_PI = 1.5707963267948966


def recip(v):
    g = pl.reciprocal(v, approx=True)
    return g * (2.0 - v * g)


def quad_angle(r):
    x0, y0 = 1.0 - r[0] * r[1], r[0] + r[1]
    x1, y1 = 1.0 - r[2] * r[3], r[2] + r[3]
    x = x0 * x1 - y0 * y1
    y = x0 * y1 + x1 * y0
    ax, ay = jnp.abs(x), jnp.abs(y)
    z = jnp.minimum(ax, ay) * recip(jnp.maximum(ax, ay))
    u = z * z
    p = ATAN[7]
    for c in ATAN[6::-1]:
        p = p * u + c
    p = p * z
    p = jnp.where(ay > ax, HALF_PI - p, p)
    p = jnp.where(x < 0.0, 2.0 * HALF_PI - p, p)
    return jnp.where(y < 0.0, 4.0 * HALF_PI - p, p)


def sample_body(lags, inv_lags, invb, H, svf_ref, S, V, JW=4, PW=4):
    lane = lax.broadcasted_iota(jnp.int32, (8, 128), 1)
    nj = 8 // JW
    nph = 8 // PW

    def step(it, carry):
        rc = it // nj
        j0 = it % nj
        r0 = rc * 64
        jb = j0 * JW
        for ph in range(nph):
            ps = [ph * PW + p for p in range(PW)]
            t = [[H[jb + 1 + j, pl.ds(128 + r0 + p, 8, stride=8), :] for j in range(JW)] for p in ps]
            acc = [[None] * JW for _ in ps]
            for a in range(AZ):
                sy, sx = directions[a]
                best = [[None] * JW for _ in ps]
                for k in range(KS):
                    s = lags[a, k]
                    il = inv_lags[a, k]
                    row = 128 + r0 + sy * s
                    if sx == 1:
                        amount = 128 - s
                        keep = lane < amount
                    elif sx == -1:
                        amount = lax.bitwise_and(s, 127)
                        keep = lane < s
                    for pi, p in enumerate(ps):
                        if sx == 0:
                            got = [H[jb + 1 + j, pl.ds(row + p, 8, stride=8), :] for j in range(JW)]
                        else:
                            off = 1 if sx == 1 else 0
                            rolled = [
                                pltpu.roll(H[jb + j + off, pl.ds(row + p, 8, stride=8), :], amount, 1)
                                for j in range(JW + 1)
                            ]
                            got = [jnp.where(keep, rolled[j], rolled[j + 1]) for j in range(JW)]
                        for j in range(JW):
                            v = (got[j] - t[pi][j]) * il
                            best[pi][j] = v if k == 0 else jnp.maximum(best[pi][j], v)
                for pi, p in enumerate(ps):
                    if sx == 0:
                        ib = 1.0 / pixel_size
                    else:
                        ib = invb[0 if sy != 0 else 1, pl.ds(r0 + p, 8, stride=8), :]
                    for j in range(JW):
                        rise = jnp.minimum(jnp.maximum(best[pi][j] * ib, 0.0), 1e8)
                        best[pi][j] = rise
                        op = recip(1.0 + rise * rise)
                        acc[pi][j] = op if a == 0 else acc[pi][j] + op
                for j in range(JW):
                    th = None
                    for q in range(0, PW, 4):
                        th_q = quad_angle([best[q + i][j] for i in range(4)])
                        th = th_q if th is None else th + th_q
                    if ph == 0:
                        S[rc, a, jb + j] = th
                    else:
                        S[rc, a, jb + j] += th
            for j in range(JW):
                tot = None
                for pi, p in enumerate(ps):
                    sv = acc[pi][j] * (1.0 / AZ)
                    V[jb + j, pl.ds(r0 + p, 8, stride=8), :] = sv
                    tot = sv if tot is None else tot + sv
                if ph == 0:
                    S[rc, 8, jb + j] = tot
                else:
                    S[rc, 8, jb + j] += tot
        return carry

    lax.fori_loop(0, 4 * nj, step, 0)

N_DEV = 128
NBR = 32
CELLS_DEV = 512
F32 = jnp.float32
BF16 = jnp.bfloat16
VMEM = pl.BlockSpec(memory_space=pltpu.VMEM)
SMEM = pl.BlockSpec(memory_space=pltpu.SMEM)
NT = (((1,), (1,)), ((), ()))


def split2(v):
    hi = v.astype(BF16)
    return hi, (v - hi.astype(F32)).astype(BF16)


def iota(shape, dim):
    return lax.broadcasted_iota(jnp.int32, shape, dim)


def route_kernel(owner_ref, slot_ref, weight_ref, start_ref, index_ref, meta_ref, rank_ref):
    sub = iota((N_DEV, 128), 0)
    lane_row = iota((1, 128), 1)
    upper = (iota((128, 128), 0) < iota((128, 128), 1)).astype(BF16)
    right = jnp.concatenate([upper, jnp.ones((128, 128), BF16)], axis=1)
    count = jnp.zeros((N_DEV, 128), F32)
    for i in range(NBR):
        mine = sub == owner_ref[i : i + 1, :]
        both = jnp.dot(mine.astype(BF16), right, preferred_element_type=F32)
        rank = jnp.sum(jnp.where(mine, both[:, :128] + count, 0.0), axis=0, keepdims=True)
        rank_ref[i : i + 1, :] = rank
        count = count + both[:, 128:]
    lower = (iota((128, 128), 0) > iota((128, 128), 1)).astype(BF16)
    start = jnp.dot(lower, count.astype(BF16), preferred_element_type=F32)
    start_row = lax.dot_general(count[:, :8].T.astype(BF16), upper, (((1,), (0,)), ((), ())), preferred_element_type=F32)
    start_ref[...] = start_row[:1].astype(jnp.int32)
    inv = jnp.zeros((64, 128), F32)
    meta = jnp.zeros((3 * N_DEV, 128), F32)
    sub32 = iota((NBR, 128), 0)
    for i in range(NBR):
        mine = sub == owner_ref[i : i + 1, :]
        rank = rank_ref[i : i + 1, :]
        place = (rank + jnp.sum(jnp.where(mine, start, 0.0), axis=0, keepdims=True)).astype(jnp.int32)
        mine_hi = sub32 == lax.shift_right_logical(place, 7)
        lo_hot = (sub == lax.bitwise_and(place, 127)).astype(BF16)
        left = jnp.concatenate(
            [jnp.where(mine_hi, float(i), 0.0), jnp.where(mine_hi, lane_row.astype(F32), 0.0)], axis=0
        ).astype(BF16)
        inv = inv + lax.dot_general(left, lo_hot, NT, preferred_element_type=F32)
        rank_hot = (sub == rank.astype(jnp.int32)).astype(BF16)
        slot = slot_ref[i : i + 1, :] + 1
        parts = (lax.shift_right_logical(slot, 4), lax.bitwise_and(slot, 15), weight_ref[i : i + 1, :])
        left = jnp.concatenate([jnp.where(mine, v.astype(F32), 0.0) for v in parts], axis=0).astype(BF16)
        meta = meta + lax.dot_general(left, rank_hot, NT, preferred_element_type=F32)
    index_ref[...] = inv.astype(jnp.int32)
    meta_ref[0] = meta[:N_DEV] * 16.0 + meta[N_DEV : 2 * N_DEV]
    meta_ref[1] = meta[2 * N_DEV :]


def route(owner, slot, weight):
    return pl.pallas_call(
        route_kernel,
        name="route",
        out_shape=(
            jax.ShapeDtypeStruct((1, N_DEV), jnp.int32),
            jax.ShapeDtypeStruct((64, 128), jnp.int32),
            jax.ShapeDtypeStruct((2, N_DEV, 128), F32),
        ),
        in_specs=[VMEM] * 3,
        out_specs=[VMEM] * 3,
        scratch_shapes=[pltpu.VMEM((NBR, 128), F32)],
        cost_estimate=pl.CostEstimate(flops=int(4e8), bytes_accessed=200000, transcendentals=0),
    )(owner, slot, weight)


def main_kernel(
    lags, inv_lags, starts, lat, own, north, south, west, east, nw, ne, sw, se, invb, weight, index,
    svf_ref, feat_ref, open_ref, H, S, V, R, Z, Y,
):
    for j in range(8):
        c = slice(j * 128, (j + 1) * 128)
        H[1 + j, 0:128, :] = north[:, c]
        H[1 + j, 128:384, :] = own[:, c]
        H[1 + j, 384:512, :] = south[:, c]
    for c, parts in ((0, (nw, west, sw)), (9, (ne, east, se))):
        H[c, 0:128, :] = parts[0][...]
        H[c, 128:384, :] = parts[1][...]
        H[c, 384:512, :] = parts[2][...]

    @pl.when(lat[0] == 0)
    def _():
        for c in range(10):
            H[c, 0:128, :] = jnp.broadcast_to(H[c, 128:129, :], (128, 128))

    @pl.when(lat[0] == lat[1] - 1)
    def _():
        for c in range(10):
            H[c, 384:512, :] = jnp.broadcast_to(H[c, 383:384, :], (128, 128))

    sample_body(lags, inv_lags, invb, H, svf_ref, S, V)
    for j in range(8):
        svf_ref[:, j * 128 : (j + 1) * 128] = V[j]

    total = jnp.zeros((288, 128), F32)
    for j in range(8):
        pool = (iota((128, 128), 1) == j * 16 + lax.shift_right_logical(iota((128, 128), 0), 3)).astype(BF16)
        field = jnp.concatenate([S[rc, f, j] for rc in range(4) for f in range(9)], axis=0)
        hi, lo = split2(field)
        total = total + jnp.dot(hi, pool, preferred_element_type=F32) + jnp.dot(lo, pool, preferred_element_type=F32)
    R[...] = total
    sub = iota((8, 128), 0)
    lane = iota((8, 128), 1)
    scale = 1.0 / 4096.0
    for rc in range(4):
        for i in range(8):
            b = rc * 8 + i
            Y[b] = R[pl.ds(rc * 72 + i, 8, stride=8), :] * (weight[b : b + 1, :].astype(F32) * scale)
        Y[32 + rc] = R[rc * 72 + 64 : rc * 72 + 72, :] * (weight[rc * 8 : rc * 8 + 8, :].astype(F32) * scale)

    def gather(t, carry):
        hi = jnp.broadcast_to(index[pl.ds(t, 1), :], (8, 128))
        lo = jnp.broadcast_to(index[pl.ds(32 + t, 1), :], (8, 128))
        acc = jnp.zeros((8, 128), F32)
        for i in range(NBR):
            g = jnp.take_along_axis(Y[i], lo, axis=1, mode="promise_in_bounds")
            acc = jnp.where(hi == i, g, acc)
        Z[t, 0:8, :] = acc
        acc = jnp.zeros((8, 128), F32)
        for rc in range(4):
            g = jnp.take_along_axis(Y[32 + rc], lo, axis=1, mode="promise_in_bounds")
            acc = jnp.where(hi == rc * 8 + sub, g, acc)
        Z[t, 8:16, :] = jnp.broadcast_to(jnp.sum(acc, axis=0, keepdims=True), (8, 128))
        return carry

    lax.fori_loop(0, NBR, gather, 0)
    Z[32] = jnp.zeros((16, 128), F32)

    def expand(o, carry):
        st = starts[0, o]
        tile = lax.shift_right_logical(st, 7)
        q = 128 - lax.bitwise_and(st, 127)
        amount = lax.bitwise_and(q, 127)
        after = jnp.minimum(tile + 1, 32)
        tile = jnp.minimum(tile, 32)
        keep = lane < q
        for half in range(2):
            a = pltpu.roll(Z[tile, half * 8 : half * 8 + 8, :], amount, 1)
            b = pltpu.roll(Z[after, half * 8 : half * 8 + 8, :], amount, 1)
            got = jnp.where(keep, a, b)
            if half == 0:
                feat_ref[o] = got
            else:
                open_ref[pl.ds(o, 1), :] = got[0:1]
        return carry

    lax.fori_loop(0, N_DEV, expand, 0, unroll=4)


def main(*args):
    return pl.pallas_call(
        main_kernel,
        name="horizon",
        out_shape=(
            jax.ShapeDtypeStruct((256, 1024), F32),
            jax.ShapeDtypeStruct((N_DEV, 8, 128), F32),
            jax.ShapeDtypeStruct((N_DEV, 128), F32),
        ),
        in_specs=[SMEM] * 4 + [VMEM] * 12,
        out_specs=[VMEM] * 3,
        scratch_shapes=[
            pltpu.VMEM((10, 512, 128), F32),
            pltpu.VMEM((4, 9, 8, 8, 128), F32),
            pltpu.VMEM((8, 256, 128), F32),
            pltpu.VMEM((288, 128), F32),
            pltpu.VMEM((33, 16, 128), F32),
            pltpu.VMEM((36, 8, 128), F32),
        ],
        compiler_params=pltpu.CompilerParams(vmem_limit_bytes=40 * 1024 * 1024),
        cost_estimate=pl.CostEstimate(flops=int(1e10), bytes_accessed=6000000, transcendentals=0),
    )(*args)


def places_kernel(meta_ref, places_ref):
    valid = (meta_ref[0] > 0.0).astype(BF16)
    count = lax.dot_general(jnp.ones((8, 128), BF16), valid, NT, preferred_element_type=F32)
    upper = (iota((128, 128), 0) < iota((128, 128), 1)).astype(BF16)
    start = jnp.dot(count.astype(BF16), upper, preferred_element_type=F32)
    places_ref[0:1, :] = count[0:1].astype(jnp.int32)
    places_ref[1:2, :] = start[0:1].astype(jnp.int32)


def places(meta):
    return pl.pallas_call(
        places_kernel,
        name="places",
        out_shape=jax.ShapeDtypeStruct((2, N_DEV), jnp.int32),
        in_specs=[VMEM],
        out_specs=VMEM,
    )(meta)


def reduce_kernel(places_ref, meta_ref, feat_ref, open_ref, horizon_ref, svf_ref, C, M):
    lane = iota((8, 128), 1)
    M[pl.ds(0, N_DEV, stride=8), :] = open_ref[...]
    M[pl.ds(1, N_DEV, stride=8), :] = meta_ref[0]
    M[pl.ds(2, N_DEV, stride=8), :] = meta_ref[1]
    for r in range(3, 8):
        M[pl.ds(r, N_DEV, stride=8), :] = jnp.zeros((N_DEV, 128), F32)
    total = places_ref[1, N_DEV - 1] + places_ref[0, N_DEV - 1]
    chunks = lax.shift_right_logical(total + 255, 8)

    def clear(t, carry):
        C[2 * t] = jnp.zeros((16, 128), F32)
        C[2 * t + 1] = jnp.zeros((16, 128), F32)
        return carry

    lax.fori_loop(0, chunks + 1, clear, 0)

    def compact(src, carry):
        n = places_ref[0, src]
        st = places_ref[1, src]
        tile = lax.shift_right_logical(st, 7)
        q = lax.bitwise_and(st, 127)
        filled = lane < n
        first = lane >= q
        for half in range(2):
            v = feat_ref[src] if half == 0 else M[pl.ds(pl.multiple_of(src * 8, 8), 8), :]
            v = pltpu.roll(jnp.where(filled, v, 0.0), q, 1)
            rows = slice(half * 8, half * 8 + 8)
            C[tile, rows, :] += jnp.where(first, v, 0.0)
            C[tile + 1, rows, :] += jnp.where(first, 0.0, v)
        return carry

    lax.fori_loop(0, N_DEV, compact, 0)
    cell = (iota((CELLS_DEV, 256), 0) + 1).astype(F32)

    def accumulate(t, acc):
        pair = jnp.concatenate([C[2 * t], C[2 * t + 1]], axis=1)
        hi, lo = split2(pair)
        hot = (cell == pair[9:10, :]).astype(BF16)
        left = jnp.concatenate([hi, lo], axis=0)
        return acc + lax.dot_general(left, hot, NT, preferred_element_type=F32)

    acc = lax.fori_loop(0, chunks, accumulate, jnp.zeros((32, CELLS_DEV), F32))
    sums = acc[0:16] + acc[16:32]
    area = jnp.maximum(sums[10:11, :] * (1.0 / 64.0), 1.0)
    horizon_ref[...] = sums[0:8] / area
    svf_ref[...] = sums[8:9] / area


def reduce(*args):
    return pl.pallas_call(
        reduce_kernel,
        name="cells",
        out_shape=(jax.ShapeDtypeStruct((AZ, CELLS_DEV), F32), jax.ShapeDtypeStruct((1, CELLS_DEV), F32)),
        in_specs=[SMEM] + [VMEM] * 3,
        out_specs=[VMEM] * 2,
        scratch_shapes=[pltpu.VMEM((132, 16, 128), F32), pltpu.VMEM((8 * N_DEV, 128), F32)],
        compiler_params=pltpu.CompilerParams(vmem_limit_bytes=40 * 1024 * 1024),
    )(*args)


def shards(terrain_surface, azimuth_lag_tallies, holder_devices, holder_region_slot, footprint_weight):
    rows, cols = terrain_surface.shape
    n_lat = lax.axis_size("lat")
    n_lon = lax.axis_size("lon")
    W = FARTHEST_LAG

    def from_neighbour(block, dy, dx):
        pairs = []
        for la in range(n_lat):
            for lo in range(n_lon):
                if 0 <= la + dy < n_lat:
                    pairs.append(((la + dy) * n_lon + (lo + dx) % n_lon, la * n_lon + lo))
        return lax.ppermute(block, ("lat", "lon"), pairs)

    top, bottom = terrain_surface[:W], terrain_surface[rows - W :]
    north = from_neighbour(bottom, -1, 0)
    south = from_neighbour(top, 1, 0)
    west = from_neighbour(terrain_surface[:, cols - W :], 0, -1)
    east = from_neighbour(terrain_surface[:, :W], 0, 1)
    nw = from_neighbour(bottom[:, cols - W :], -1, -1)
    ne = from_neighbour(bottom[:, :W], -1, 1)
    sw = from_neighbour(top[:, cols - W :], 1, -1)
    se = from_neighbour(top[:, :W], 1, 1)

    start, index, meta = route(
        holder_devices.reshape(NBR, 128), holder_region_slot.reshape(NBR, 128), footprint_weight.reshape(NBR, 128)
    )
    meta = lax.all_to_all(meta, ("lat", "lon"), split_axis=1, concat_axis=1, tiled=True)

    rows_global = (lax.axis_index("lat") * rows + jnp.arange(rows, dtype=jnp.int32)).astype(F32)
    latitude = 47.0 - (rows_global + 0.5) / 1200.0
    coslat = jnp.cos(latitude * jnp.pi / 180.0)
    across = (pixel_size * coslat) ** 2
    inv_base = 1.0 / jnp.sqrt(jnp.stack([pixel_size**2 + across, across]))
    inv_base = jnp.broadcast_to(inv_base[:, :, None], (2, rows, 128))
    lat = jnp.stack([lax.axis_index("lat").astype(jnp.int32), jnp.int32(n_lat)])
    fine_svf, feats, opens = main(
        azimuth_lag_tallies, 1.0 / azimuth_lag_tallies.astype(F32), start, lat, terrain_surface,
        north, south, west, east, nw, ne, sw, se, inv_base, footprint_weight.reshape(NBR, 128), index,
    )
    where = places(meta)
    feats = lax.all_to_all(feats, ("lat", "lon"), split_axis=0, concat_axis=0, tiled=True)
    opens = lax.all_to_all(opens, ("lat", "lon"), split_axis=0, concat_axis=0, tiled=True)
    cell_horizon, cell_svf = reduce(where, meta, feats, opens)
    return fine_svf, cell_horizon, cell_svf.reshape(CELLS_DEV)


def solution(mesh):
    P = jax.sharding.PartitionSpec
    in_specs = (P("lat", "lon"), P(), P(("lat", "lon"), None), P(("lat", "lon")), P(("lat", "lon")))
    out_specs = (P("lat", "lon"), P(None, ("lat", "lon")), P(("lat", "lon")))
    return jax.shard_map(shards, mesh=mesh, in_specs=in_specs, out_specs=out_specs, check_vma=False)
```

```python
import jax
import jax.numpy as jnp
from jax import lax
from jax.experimental import pallas as pl
from jax.experimental.pallas import tpu as pltpu

FARTHEST_LAG = 128
AZ = 8
KS = 8
pixel_size = 92.6
ATAN = (0.9999999, -0.33331991, 0.19969724, -0.14019481, 0.09914293, -0.05948639, 0.0242524, -0.00469327)
HALF_PI = 1.5707963267948966


def recip(v):
    g = pl.reciprocal(v, approx=True)
    return g * (2.0 - v * g)


def quad_angle(r):
    x0, y0 = 1.0 - r[0] * r[1], r[0] + r[1]
    x1, y1 = 1.0 - r[2] * r[3], r[2] + r[3]
    x = x0 * x1 - y0 * y1
    y = x0 * y1 + x1 * y0
    ax, ay = jnp.abs(x), jnp.abs(y)
    z = jnp.minimum(ax, ay) * recip(jnp.maximum(ax, ay))
    u = z * z
    p = ATAN[7]
    for c in ATAN[6::-1]:
        p = p * u + c
    p = p * z
    p = jnp.where(ay > ax, HALF_PI - p, p)
    p = jnp.where(x < 0.0, 2.0 * HALF_PI - p, p)
    return jnp.where(y < 0.0, 4.0 * HALF_PI - p, p)


N_DEV = 128
NBR = 32
CELLS_DEV = 512
F32 = jnp.float32
BF16 = jnp.bfloat16
VMEM = pl.BlockSpec(memory_space=pltpu.VMEM)
SMEM = pl.BlockSpec(memory_space=pltpu.SMEM)
ANY = pl.BlockSpec(memory_space=pl.ANY)
NT = (((1,), (1,)), ((), ()))


def split2(v):
    hi = v.astype(BF16)
    return hi, (v - hi.astype(F32)).astype(BF16)


def iota(shape, dim):
    return lax.broadcasted_iota(jnp.int32, shape, dim)


def route_kernel(owner_ref, slot_ref, weight_ref, start_ref, index_ref, meta_ref, rank_ref):
    sub = iota((N_DEV, 128), 0)
    lane_row = iota((1, 128), 1)
    upper = (iota((128, 128), 0) < iota((128, 128), 1)).astype(BF16)
    right = jnp.concatenate([upper, jnp.ones((128, 128), BF16)], axis=1)
    count = jnp.zeros((N_DEV, 128), F32)
    for i in range(NBR):
        mine = sub == owner_ref[i : i + 1, :]
        both = jnp.dot(mine.astype(BF16), right, preferred_element_type=F32)
        rank = jnp.sum(jnp.where(mine, both[:, :128] + count, 0.0), axis=0, keepdims=True)
        rank_ref[i : i + 1, :] = rank
        count = count + both[:, 128:]
    lower = (iota((128, 128), 0) > iota((128, 128), 1)).astype(BF16)
    start = jnp.dot(lower, count.astype(BF16), preferred_element_type=F32)
    start_row = lax.dot_general(count[:, :8].T.astype(BF16), upper, (((1,), (0,)), ((), ())), preferred_element_type=F32)
    start_ref[...] = start_row[:1].astype(jnp.int32)
    inv = jnp.zeros((64, 128), F32)
    meta = jnp.zeros((3 * N_DEV, 128), F32)
    sub32 = iota((NBR, 128), 0)
    for i in range(NBR):
        mine = sub == owner_ref[i : i + 1, :]
        rank = rank_ref[i : i + 1, :]
        place = (rank + jnp.sum(jnp.where(mine, start, 0.0), axis=0, keepdims=True)).astype(jnp.int32)
        mine_hi = sub32 == lax.shift_right_logical(place, 7)
        lo_hot = (sub == lax.bitwise_and(place, 127)).astype(BF16)
        left = jnp.concatenate(
            [jnp.where(mine_hi, float(i), 0.0), jnp.where(mine_hi, lane_row.astype(F32), 0.0)], axis=0
        ).astype(BF16)
        inv = inv + lax.dot_general(left, lo_hot, NT, preferred_element_type=F32)
        rank_hot = (sub == rank.astype(jnp.int32)).astype(BF16)
        slot = slot_ref[i : i + 1, :] + 1
        parts = (lax.shift_right_logical(slot, 4), lax.bitwise_and(slot, 15), weight_ref[i : i + 1, :])
        left = jnp.concatenate([jnp.where(mine, v.astype(F32), 0.0) for v in parts], axis=0).astype(BF16)
        meta = meta + lax.dot_general(left, rank_hot, NT, preferred_element_type=F32)
    index_ref[...] = inv.astype(jnp.int32)
    meta_ref[0] = meta[:N_DEV] * 16.0 + meta[N_DEV : 2 * N_DEV]
    meta_ref[1] = meta[2 * N_DEV :]


def route(owner, slot, weight):
    return pl.pallas_call(
        route_kernel,
        name="route",
        out_shape=(
            jax.ShapeDtypeStruct((1, N_DEV), jnp.int32),
            jax.ShapeDtypeStruct((64, 128), jnp.int32),
            jax.ShapeDtypeStruct((2, N_DEV, 128), F32),
        ),
        in_specs=[VMEM] * 3,
        out_specs=[VMEM] * 3,
        scratch_shapes=[pltpu.VMEM((NBR, 128), F32)],
        cost_estimate=pl.CostEstimate(flops=int(4e8), bytes_accessed=200000, transcendentals=0),
    )(owner, slot, weight)


def sample(lags, inv_lags, invb, H, h0, r0, jb, rays, S_ref, rc, svf_in, svf_out, JW=4):
    lane = iota((8, 128), 1)
    for ph in range(2):
        ps = [ph * 4 + p for p in range(4)]
        t = [[H[jb + 1 + j, pl.ds(h0 + r0 + p, 8, stride=8), :] for j in range(JW)] for p in ps]
        acc = [[svf_in[jb + j, pl.ds(r0 + p, 8, stride=8), :] if svf_in is not None else None for j in range(JW)] for p in ps]
        for f, (a, sy, sx) in enumerate(rays):
            best = [[None] * JW for _ in ps]
            for k in range(KS):
                s = lags[a, k]
                il = inv_lags[a, k]
                row = h0 + r0 + sy * s
                if sx == 1:
                    amount = 128 - s
                    keep = lane < amount
                elif sx == -1:
                    amount = lax.bitwise_and(s, 127)
                    keep = lane < s
                for pi, p in enumerate(ps):
                    if sx == 0:
                        got = [H[jb + 1 + j, pl.ds(row + p, 8, stride=8), :] for j in range(JW)]
                    else:
                        off = 1 if sx == 1 else 0
                        rolled = [
                            pltpu.roll(H[jb + j + off, pl.ds(row + p, 8, stride=8), :], amount, 1)
                            for j in range(JW + 1)
                        ]
                        got = [jnp.where(keep, rolled[j], rolled[j + 1]) for j in range(JW)]
                    for j in range(JW):
                        v = (got[j] - t[pi][j]) * il
                        best[pi][j] = v if k == 0 else jnp.maximum(best[pi][j], v)
            for pi, p in enumerate(ps):
                if sx == 0:
                    ib = 1.0 / pixel_size
                else:
                    flat = isinstance(sy, int) and sy == 0
                    ib = invb[1 if flat else 0, pl.ds(r0 + p, 8, stride=8), :]
                for j in range(JW):
                    rise = jnp.minimum(jnp.maximum(best[pi][j] * ib, 0.0), 1e8)
                    best[pi][j] = rise
                    opening = recip(1.0 + rise * rise)
                    acc[pi][j] = opening if acc[pi][j] is None else acc[pi][j] + opening
            for j in range(JW):
                th = quad_angle([best[i][j] for i in range(4)])
                if ph == 0:
                    S_ref[rc, f, jb + j] = th
                else:
                    S_ref[rc, f, jb + j] += th
        f = len(rays)
        for j in range(JW):
            tot = None
            for pi, p in enumerate(ps):
                svf_out[jb + j, pl.ds(r0 + p, 8, stride=8), :] = acc[pi][j]
                tot = acc[pi][j] if tot is None else tot + acc[pi][j]
            if ph == 0:
                S_ref[rc, f, jb + j] = tot
            else:
                S_ref[rc, f, jb + j] += tot


def slanted(southward):
    sy = jnp.where(southward, 1, -1)
    return [(jnp.where(southward, 3, 5), sy, -1), (jnp.where(southward, 2, 6), sy, 0), (jnp.where(southward, 1, 7), sy, 1)]


def copies(pairs, sems):
    made = [pltpu.make_async_copy(a, b, sems.at[i]) for i, (a, b) in enumerate(pairs)]
    for c in made:
        c.start()
    for c in made:
        c.wait()


def cols(j):
    return pl.ds(j * 128, 128)


def inner_kernel(lags, inv_lags, own, west, east, invb, V_ref, S_ref, H, sems):
    copies(
        [(own.at[:, cols(j)], H.at[1 + j]) for j in range(8)] + [(west, H.at[0]), (east, H.at[9])], sems
    )

    def step(it, carry):
        rc = lax.shift_right_logical(it, 1)
        jb = lax.bitwise_and(it, 1) * 4
        rays = [(0, 0, 1), (4, 0, -1)] + slanted(rc < 2)
        sample(lags, inv_lags, invb, H, 0, rc * 64, jb, rays, S_ref, rc, None, V_ref)
        return carry

    lax.fori_loop(0, 8, step, 0)


def inner(*args):
    return pl.pallas_call(
        inner_kernel,
        name="inner",
        out_shape=(jax.ShapeDtypeStruct((8, 256, 128), F32), jax.ShapeDtypeStruct((4, 6, 8, 8, 128), F32)),
        in_specs=[SMEM] * 2 + [ANY] * 3 + [VMEM],
        out_specs=[VMEM] * 2,
        scratch_shapes=[pltpu.VMEM((10, 256, 128), F32), pltpu.SemaphoreType.DMA((10,))],
        compiler_params=pltpu.CompilerParams(vmem_limit_bytes=24 * 1024 * 1024),
        cost_estimate=pl.CostEstimate(flops=int(4e8), bytes_accessed=30000000, transcendentals=0),
    )(*args)


def outer_kernel(
    lags, inv_lags, starts, lat, own, north, south, west, east, invb, V_in, S_in, weight, index, meta,
    svf_ref, out_ref, H, S, V, R, Z, Y, F, sems,
):
    pairs = [(own.at[:, cols(j)], H.at[1 + j, pl.ds(128, 256)]) for j in range(8)]
    pairs += [(west, H.at[0, pl.ds(128, 256)]), (east, H.at[9, pl.ds(128, 256)])]
    pairs += [(north.at[:, cols(j)], H.at[j, pl.ds(0, 128)]) for j in range(10)]
    pairs += [(south.at[:, cols(j)], H.at[j, pl.ds(384, 128)]) for j in range(10)]
    copies(pairs, sems)

    @pl.when(lat[0] == 0)
    def _():
        for c in range(10):
            H[c, 0:128, :] = jnp.broadcast_to(H[c, 128:129, :], (128, 128))

    @pl.when(lat[0] == lat[1] - 1)
    def _():
        for c in range(10):
            H[c, 384:512, :] = jnp.broadcast_to(H[c, 383:384, :], (128, 128))

    def step(it, carry):
        rc = lax.shift_right_logical(it, 1)
        jb = lax.bitwise_and(it, 1) * 4
        sample(lags, inv_lags, invb, H, 128, rc * 64, jb, slanted(rc >= 2), S, rc, V_in, V)
        return carry

    lax.fori_loop(0, 8, step, 0)
    for j in range(8):
        svf_ref[:, j * 128 : (j + 1) * 128] = V[j] * (1.0 / AZ)

    total = jnp.zeros((288, 128), F32)
    for j in range(8):
        pool = (iota((128, 128), 1) == j * 16 + lax.shift_right_logical(iota((128, 128), 0), 3)).astype(BF16)
        field = []
        for rc in range(4):
            here, there = ((S_in, 2), (S, 0)) if rc < 2 else ((S, 0), (S_in, 2))
            where = [(S_in, 0), (here[0], here[1] + 2), (here[0], here[1] + 1), (here[0], here[1])]
            where += [(S_in, 1), (there[0], there[1]), (there[0], there[1] + 1), (there[0], there[1] + 2), (S, 3)]
            field += [ref[rc, f, j] for ref, f in where]
        hi, lo = split2(jnp.concatenate(field, axis=0))
        total = total + jnp.dot(hi, pool, preferred_element_type=F32) + jnp.dot(lo, pool, preferred_element_type=F32)
    R[...] = total
    sub = iota((8, 128), 0)
    lane = iota((8, 128), 1)
    scale = 1.0 / 4096.0
    for rc in range(4):
        for i in range(8):
            b = rc * 8 + i
            Y[b] = R[pl.ds(rc * 72 + i, 8, stride=8), :] * (weight[b : b + 1, :].astype(F32) * scale)
        Y[32 + rc] = R[rc * 72 + 64 : rc * 72 + 72, :] * (weight[rc * 8 : rc * 8 + 8, :].astype(F32) * (scale / AZ))

    def gather(t, carry):
        hi = jnp.broadcast_to(index[pl.ds(t, 1), :], (8, 128))
        lo = jnp.broadcast_to(index[pl.ds(32 + t, 1), :], (8, 128))
        acc = jnp.zeros((8, 128), F32)
        for i in range(NBR):
            g = jnp.take_along_axis(Y[i], lo, axis=1, mode="promise_in_bounds")
            acc = jnp.where(hi == i, g, acc)
        Z[t, 0:8, :] = acc
        acc = jnp.zeros((8, 128), F32)
        for rc in range(4):
            g = jnp.take_along_axis(Y[32 + rc], lo, axis=1, mode="promise_in_bounds")
            acc = jnp.where(hi == rc * 8 + sub, g, acc)
        Z[t, 8:16, :] = jnp.broadcast_to(jnp.sum(acc, axis=0, keepdims=True), (8, 128))
        return carry

    lax.fori_loop(0, NBR, gather, 0)
    Z[32] = jnp.zeros((16, 128), F32)

    def expand(o, carry):
        st = starts[0, o]
        tile = lax.shift_right_logical(st, 7)
        q = 128 - lax.bitwise_and(st, 127)
        amount = lax.bitwise_and(q, 127)
        after = jnp.minimum(tile + 1, 32)
        tile = jnp.minimum(tile, 32)
        keep = lane < q
        for half in range(2):
            a = pltpu.roll(Z[tile, half * 8 : half * 8 + 8, :], amount, 1)
            b = pltpu.roll(Z[after, half * 8 : half * 8 + 8, :], amount, 1)
            got = jnp.where(keep, a, b)
            if half == 0:
                F[pl.ds(o, 8, stride=N_DEV), :] = got
            else:
                F[pl.ds(o + 8 * N_DEV, 1), :] = got[0:1]
        return carry

    lax.fori_loop(0, N_DEV, expand, 0, unroll=4)
    for f in range(9):
        out_ref[:, f * 128 : (f + 1) * 128] = F[f * N_DEV : (f + 1) * N_DEV, :]
    out_ref[:, 9 * 128 : 10 * 128] = meta[0]
    out_ref[:, 10 * 128 : 11 * 128] = meta[1]


def outer(*args):
    return pl.pallas_call(
        outer_kernel,
        name="outer",
        out_shape=(jax.ShapeDtypeStruct((256, 1024), F32), jax.ShapeDtypeStruct((N_DEV, 11 * 128), F32)),
        in_specs=[SMEM] * 4 + [ANY] * 5 + [VMEM] * 6,
        out_specs=[VMEM] * 2,
        scratch_shapes=[
            pltpu.VMEM((10, 512, 128), F32),
            pltpu.VMEM((4, 4, 8, 8, 128), F32),
            pltpu.VMEM((8, 256, 128), F32),
            pltpu.VMEM((288, 128), F32),
            pltpu.VMEM((33, 16, 128), F32),
            pltpu.VMEM((36, 8, 128), F32),
            pltpu.VMEM((9 * N_DEV, 128), F32),
            pltpu.SemaphoreType.DMA((30,)),
        ],
        compiler_params=pltpu.CompilerParams(vmem_limit_bytes=32 * 1024 * 1024),
        cost_estimate=pl.CostEstimate(flops=int(4e8), bytes_accessed=20000000, transcendentals=0),
    )(*args)


def cells_kernel(got_ref, horizon_ref, svf_ref, G, C, A, Pv, Ps, sem):
    lane = iota((8, 128), 1)
    slots = got_ref[:, 9 * 128 : 10 * 128]
    valid = (slots > 0.0).astype(BF16)
    count = lax.dot_general(jnp.ones((8, 128), BF16), valid, NT, preferred_element_type=F32)
    upper = (iota((128, 128), 0) < iota((128, 128), 1)).astype(BF16)
    start = jnp.dot(count.astype(BF16), upper, preferred_element_type=F32)
    Pv[...] = jnp.where(lane >= 0, jnp.where(iota((8, 128), 0) == 0, count, start), 0.0).astype(jnp.int32)
    copy = pltpu.make_async_copy(Pv, Ps, sem)
    copy.start()
    for f in range(11):
        G[pl.ds(f, N_DEV, stride=16), :] = got_ref[:, f * 128 : (f + 1) * 128]
    for f in range(11, 16):
        G[pl.ds(f, N_DEV, stride=16), :] = jnp.zeros((N_DEV, 128), F32)
    A[...] = jnp.zeros((CELLS_DEV, 32), F32)
    copy.wait()
    total = Ps[1, N_DEV - 1] + Ps[0, N_DEV - 1]
    chunks = lax.shift_right_logical(total + 255, 8)

    def compact(src, cur):
        n = Ps[0, src]
        st = Ps[1, src]
        tile = lax.shift_right_logical(st, 7)
        q = lax.bitwise_and(st, 127)
        held = lane < q
        crossed = q + n >= 128
        out = []
        for half in range(2):
            v = pltpu.roll(G[pl.ds(pl.multiple_of(src * 16 + half * 8, 8), 8), :], q, 1)
            merged = jnp.where(held, cur[half], v)
            C[tile, half * 8 : half * 8 + 8, :] = merged
            C[tile + 1, half * 8 : half * 8 + 8, :] = v
            out.append(jnp.where(crossed, v, merged))
        return tuple(out)

    zero = jnp.zeros((8, 128), F32)
    lax.fori_loop(0, N_DEV, compact, (zero, zero), unroll=4)
    last = lax.shift_right_logical(total, 7)
    C[last + 1] = jnp.zeros((16, 128), F32)
    cell = (iota((CELLS_DEV, 256), 0) + 1).astype(F32)
    place = iota((1, 256), 1)

    def accumulate(t, carry):
        pair = jnp.concatenate([C[2 * t], C[2 * t + 1]], axis=1)
        hi, lo = split2(pair)
        slot = jnp.where(t * 256 + place < total, pair[9:10, :], 0.0)
        hot = (cell == slot).astype(BF16)
        A[...] += lax.dot_general(hot, jnp.concatenate([hi, lo], axis=0), NT, preferred_element_type=F32)
        return carry

    lax.fori_loop(0, chunks, accumulate, 0)
    acc = A[...].T
    sums = acc[0:16] + acc[16:32]
    area = jnp.maximum(sums[10:11, :] * (1.0 / 64.0), 1.0)
    horizon_ref[...] = sums[0:8] / area
    svf_ref[...] = sums[8:9] / area


def cells(got):
    return pl.pallas_call(
        cells_kernel,
        name="cells",
        out_shape=(jax.ShapeDtypeStruct((AZ, CELLS_DEV), F32), jax.ShapeDtypeStruct((1, CELLS_DEV), F32)),
        in_specs=[VMEM],
        out_specs=[VMEM] * 2,
        scratch_shapes=[
            pltpu.VMEM((16 * N_DEV, 128), F32),
            pltpu.VMEM((132, 16, 128), F32),
            pltpu.VMEM((CELLS_DEV, 32), F32),
            pltpu.VMEM((8, 128), jnp.int32),
            pltpu.SMEM((8, 128), jnp.int32),
            pltpu.SemaphoreType.DMA,
        ],
        compiler_params=pltpu.CompilerParams(vmem_limit_bytes=24 * 1024 * 1024),
    )(got)


def shards(terrain_surface, azimuth_lag_tallies, holder_devices, holder_region_slot, footprint_weight):
    rows, width = terrain_surface.shape
    n_lat = lax.axis_size("lat")
    n_lon = lax.axis_size("lon")
    W = FARTHEST_LAG
    own = terrain_surface
    east_pairs = [((i + 1) % n_lon, i) for i in range(n_lon)]
    west = lax.ppermute(own[:, width - W :], "lon", [(j, i) for i, j in east_pairs])
    east = lax.ppermute(own[:, :W], "lon", east_pairs)
    wide = jnp.concatenate([west, own, east], axis=1)
    down = [(i, i + 1) for i in range(n_lat - 1)]
    north = lax.ppermute(wide[rows - W :], "lat", down)
    south = lax.ppermute(wide[:W], "lat", [(j, i) for i, j in down])

    weight = footprint_weight.reshape(NBR, 128)
    start, index, meta = route(holder_devices.reshape(NBR, 128), holder_region_slot.reshape(NBR, 128), weight)

    rows_global = (lax.axis_index("lat") * rows + jnp.arange(rows, dtype=jnp.int32)).astype(F32)
    latitude = 47.0 - (rows_global + 0.5) / 1200.0
    coslat = jnp.cos(latitude * jnp.pi / 180.0)
    across = (pixel_size * coslat) ** 2
    inv_base = 1.0 / jnp.sqrt(jnp.stack([pixel_size**2 + across, across]))
    inv_base = jnp.broadcast_to(inv_base[:, :, None], (2, rows, 128))
    lat = jnp.stack([lax.axis_index("lat").astype(jnp.int32), jnp.int32(n_lat)])
    inv_lags = 1.0 / azimuth_lag_tallies.astype(F32)
    part, sums = inner(azimuth_lag_tallies, inv_lags, own, west, east, inv_base)
    fine_svf, packed = outer(
        azimuth_lag_tallies, inv_lags, start, lat, own, north, south, west, east, inv_base, part, sums, weight, index, meta
    )
    got = lax.all_to_all(packed, ("lat", "lon"), split_axis=0, concat_axis=0, tiled=True)
    cell_horizon, cell_svf = cells(got)
    return fine_svf, cell_horizon, cell_svf.reshape(CELLS_DEV)


def solution(mesh):
    P = jax.sharding.PartitionSpec
    in_specs = (P("lat", "lon"), P(), P(("lat", "lon"), None), P(("lat", "lon")), P(("lat", "lon")))
    out_specs = (P("lat", "lon"), P(None, ("lat", "lon")), P(("lat", "lon")))
    return jax.shard_map(shards, mesh=mesh, in_specs=in_specs, out_specs=out_specs, check_vma=False)
```

```python
import jax
import jax.numpy as jnp
from jax import lax
from jax.experimental import pallas as pl
from jax.experimental.pallas import tpu as pltpu

FARTHEST_LAG = 128
AZ = 8
KS = 8
pixel_size = 92.6
ATAN = (0.9999999, -0.33331991, 0.19969724, -0.14019481, 0.09914293, -0.05948639, 0.0242524, -0.00469327)
HALF_PI = 1.5707963267948966


def recip(v):
    g = pl.reciprocal(v, approx=True)
    return g * (2.0 - v * g)


def angle(x, y):
    ax, ay = jnp.abs(x), jnp.abs(y)
    z = jnp.minimum(ax, ay) * recip(jnp.maximum(ax, ay))
    u = z * z
    p = ATAN[7]
    for c in ATAN[6::-1]:
        p = p * u + c
    p = p * z
    p = jnp.where(ay > ax, HALF_PI - p, p)
    p = jnp.where(x < 0.0, 2.0 * HALF_PI - p, p)
    return jnp.where(y < 0.0, 4.0 * HALF_PI - p, p)


N_DEV = 128
NBR = 32
CELLS_DEV = 512
F32 = jnp.float32
BF16 = jnp.bfloat16
VMEM = pl.BlockSpec(memory_space=pltpu.VMEM)
SMEM = pl.BlockSpec(memory_space=pltpu.SMEM)
ANY = pl.BlockSpec(memory_space=pl.ANY)
NT = (((1,), (1,)), ((), ()))


def split2(v):
    hi = v.astype(BF16)
    return hi, (v - hi.astype(F32)).astype(BF16)


def iota(shape, dim):
    return lax.broadcasted_iota(jnp.int32, shape, dim)


def route_kernel(owner_ref, slot_ref, weight_ref, start_ref, index_ref, meta_ref, rank_ref):
    sub = iota((N_DEV, 128), 0)
    upper = (iota((128, 128), 0) < iota((128, 128), 1)).astype(BF16)
    right = jnp.concatenate([upper, jnp.ones((128, 128), BF16)], axis=1)
    count = jnp.zeros((N_DEV, 128), F32)
    for i in range(NBR):
        mine = sub == owner_ref[i : i + 1, :]
        both = jnp.dot(mine.astype(BF16), right, preferred_element_type=F32)
        rank = jnp.sum(jnp.where(mine, both[:, :128] + count, 0.0), axis=0, keepdims=True)
        rank_ref[i : i + 1, :] = rank
        count = count + both[:, 128:]
    lower = (iota((128, 128), 0) > iota((128, 128), 1)).astype(BF16)
    start = jnp.dot(lower, count.astype(BF16), preferred_element_type=F32)
    start_row = lax.dot_general(count[:, :8].T.astype(BF16), upper, (((1,), (0,)), ((), ())), preferred_element_type=F32)
    start_ref[...] = start_row[:1].astype(jnp.int32)
    meta = jnp.zeros((3 * N_DEV, 128), F32)
    for i in range(NBR):
        mine = sub == owner_ref[i : i + 1, :]
        rank = rank_ref[i : i + 1, :]
        place = (rank + jnp.sum(jnp.where(mine, start, 0.0), axis=0, keepdims=True)).astype(jnp.int32)
        rank = rank.astype(jnp.int32)
        index_ref[i : i + 1, :] = lax.shift_right_logical(place, 7)
        index_ref[NBR + i : NBR + i + 1, :] = lax.bitwise_and(place, 127)
        index_ref[2 * NBR + i : 2 * NBR + i + 1, :] = rank
        rank_hot = (sub == rank).astype(BF16)
        slot = slot_ref[i : i + 1, :] + 1
        parts = (lax.shift_right_logical(slot, 4), lax.bitwise_and(slot, 15), weight_ref[i : i + 1, :])
        left = jnp.concatenate([jnp.where(mine, v.astype(F32), 0.0) for v in parts], axis=0).astype(BF16)
        meta = meta + lax.dot_general(left, rank_hot, NT, preferred_element_type=F32)
    meta_ref[0] = meta[:N_DEV] * 16.0 + meta[N_DEV : 2 * N_DEV]
    meta_ref[1] = meta[2 * N_DEV :]


def route(owner, slot, weight):
    return pl.pallas_call(
        route_kernel,
        name="route",
        out_shape=(
            jax.ShapeDtypeStruct((1, N_DEV), jnp.int32),
            jax.ShapeDtypeStruct((96, 128), jnp.int32),
            jax.ShapeDtypeStruct((2, N_DEV, 128), F32),
        ),
        in_specs=[VMEM] * 3,
        out_specs=[VMEM] * 3,
        scratch_shapes=[pltpu.VMEM((NBR, 128), F32)],
        cost_estimate=pl.CostEstimate(flops=int(4e8), bytes_accessed=200000, transcendentals=0),
    )(owner, slot, weight)


def turned(z, r):
    if z is None:
        return (None, r)
    x, y = z
    if x is None:
        return (1.0 - y * r, y + r)
    return (x - y * r, y + x * r)


def sample(lags, inv_lags, invb, H, h0, it, rays, S_ref, svf_in, svf_out):
    lane = iota((8, 128), 1)
    rc = lax.shift_right_logical(it, 1)
    r0 = rc * 64 + lax.bitwise_and(it, 1) * 4
    for f, (a, sy, sx) in enumerate(rays):
        flat = isinstance(sy, int) and sy == 0
        z = [None] * 8
        off = 1 if sx >= 0 else 0
        count = 8 if sx == 0 else 9
        for p in range(4):
            here = r0 + p
            t = [H[1 + j, pl.ds(h0 + here, 8, stride=8), :] for j in range(8)]
            best = [None] * 8
            if flat:
                far = [H[off + j, pl.ds(h0 + here, 8, stride=8), :] for j in range(count)]
            for k in range(KS):
                s = lags[a, k]
                il = inv_lags[a, k]
                if not flat:
                    row = h0 + here + sy * s
                    far = [H[off + j, pl.ds(row, 8, stride=8), :] for j in range(count)]
                if sx == 0:
                    got = far
                else:
                    amount = 128 - s if sx == 1 else lax.bitwise_and(s, 127)
                    keep = lane < (amount if sx == 1 else s)
                    rolled = [pltpu.roll(v, amount, 1) for v in far]
                    got = [jnp.where(keep, rolled[j], rolled[j + 1]) for j in range(8)]
                for j in range(8):
                    v = (got[j] - t[j]) * il
                    best[j] = v if k == 0 else jnp.maximum(best[j], v)
            ib = 1.0 / pixel_size if sx == 0 else invb[1 if flat else 0, pl.ds(here, 8, stride=8), :]
            for j in range(8):
                rise = jnp.minimum(jnp.maximum(best[j] * ib, 0.0), 1e8)
                z[j] = turned(z[j], rise)
                opening = recip(1.0 + rise * rise)
                if f == 0 and svf_in is not None:
                    opening = opening + svf_in[j, pl.ds(here, 8, stride=8), :]
                if f > 0:
                    opening = opening + svf_out[j, pl.ds(here, 8, stride=8), :]
                svf_out[j, pl.ds(here, 8, stride=8), :] = opening
        for j in range(8):
            S_ref[rc, f, j] += angle(*z[j])
    for j in range(8):
        v = [svf_out[j, pl.ds(r0 + p, 8, stride=8), :] for p in range(4)]
        S_ref[rc, len(rays), j] += (v[0] + v[1]) + (v[2] + v[3])


def slanted(southward):
    sy = jnp.where(southward, 1, -1)
    return [(jnp.where(southward, 3, 5), sy, -1), (jnp.where(southward, 2, 6), sy, 0), (jnp.where(southward, 1, 7), sy, 1)]


def copies(pairs, sems):
    made = [pltpu.make_async_copy(a, b, sems.at[i]) for i, (a, b) in enumerate(pairs)]
    for c in made:
        c.start()
    for c in made:
        c.wait()


def cols(j):
    return pl.ds(j * 128, 128)


def inner_kernel(lags, inv_lags, own, west, east, invb, V_ref, S_ref, H, sems):
    copies(
        [(own.at[:, cols(j)], H.at[1 + j]) for j in range(8)] + [(west, H.at[0]), (east, H.at[9])], sems
    )

    S_ref[...] = jnp.zeros(S_ref.shape, F32)

    def step(it, carry):
        rays = [(0, 0, 1), (4, 0, -1)] + slanted(it < 4)
        sample(lags, inv_lags, invb, H, 0, it, rays, S_ref, None, V_ref)
        return carry

    lax.fori_loop(0, 8, step, 0)


def inner(*args):
    return pl.pallas_call(
        inner_kernel,
        name="inner",
        out_shape=(jax.ShapeDtypeStruct((8, 256, 128), F32), jax.ShapeDtypeStruct((4, 6, 8, 8, 128), F32)),
        in_specs=[SMEM] * 2 + [ANY] * 3 + [VMEM],
        out_specs=[VMEM] * 2,
        scratch_shapes=[pltpu.VMEM((10, 256, 128), F32), pltpu.SemaphoreType.DMA((10,))],
        compiler_params=pltpu.CompilerParams(vmem_limit_bytes=24 * 1024 * 1024),
        cost_estimate=pl.CostEstimate(flops=int(4e8), bytes_accessed=30000000, transcendentals=0),
    )(*args)


def outer_kernel(
    lags, inv_lags, starts, lat, own, north, south, west, east, invb, V_in, S_in, weight, owner, index, meta,
    svf_ref, out_ref, H, S, V, R, Z, Y, O, F, acc, sems,
):
    pairs = [(own.at[:, cols(j)], H.at[1 + j, pl.ds(128, 256)]) for j in range(8)]
    pairs += [(west, H.at[0, pl.ds(128, 256)]), (east, H.at[9, pl.ds(128, 256)])]
    pairs += [(north.at[:, cols(j)], H.at[j, pl.ds(0, 128)]) for j in range(10)]
    pairs += [(south.at[:, cols(j)], H.at[j, pl.ds(384, 128)]) for j in range(10)]
    copies(pairs, sems)

    @pl.when(lat[0] == 0)
    def _():
        for c in range(10):
            H[c, 0:128, :] = jnp.broadcast_to(H[c, 128:129, :], (128, 128))

    @pl.when(lat[0] == lat[1] - 1)
    def _():
        for c in range(10):
            H[c, 384:512, :] = jnp.broadcast_to(H[c, 383:384, :], (128, 128))

    S[...] = jnp.zeros(S.shape, F32)

    def step(it, carry):
        sample(lags, inv_lags, invb, H, 128, it, slanted(it >= 4), S, V_in, V)
        return carry

    lax.fori_loop(0, 8, step, 0)
    for j in range(8):
        svf_ref[:, j * 128 : (j + 1) * 128] = V[j] * (1.0 / AZ)

    total = jnp.zeros((288, 128), F32)
    for j in range(8):
        pool = (iota((128, 128), 1) == j * 16 + lax.shift_right_logical(iota((128, 128), 0), 3)).astype(BF16)
        field = []
        for rc in range(4):
            here, there = ((S_in, 2), (S, 0)) if rc < 2 else ((S, 0), (S_in, 2))
            where = [(S_in, 0), (here[0], here[1] + 2), (here[0], here[1] + 1), (here[0], here[1])]
            where += [(S_in, 1), (there[0], there[1]), (there[0], there[1] + 1), (there[0], there[1] + 2), (S, 3)]
            field += [ref[rc, f, j] for ref, f in where]
        hi, lo = split2(jnp.concatenate(field, axis=0))
        total = total + jnp.dot(hi, pool, preferred_element_type=F32) + jnp.dot(lo, pool, preferred_element_type=F32)
    R[...] = total
    lane = iota((8, 128), 1)
    scale = 1.0 / 4096.0
    for rc in range(4):
        for i in range(8):
            b = rc * 8 + i
            Y[b] = R[pl.ds(rc * 72 + i, 8, stride=8), :] * (weight[b : b + 1, :].astype(F32) * scale)
        O[rc * 8 : rc * 8 + 8, :] = R[rc * 72 + 64 : rc * 72 + 72, :] * (weight[rc * 8 : rc * 8 + 8, :].astype(F32) * (scale / AZ))

    acc[...] = jnp.zeros(acc.shape, F32)
    low = iota((128, 512), 0).astype(F32).astype(BF16)
    zero = jnp.zeros((16, 512), BF16)

    def wide(ref, row):
        return jnp.concatenate([ref[pl.ds(row + i, 1), :] for i in range(4)], axis=1)

    def sort(g, carry):
        b = g * 4
        v = jnp.concatenate([Y[b + i] for i in range(4)], axis=1)
        v = jnp.concatenate(split2(v), axis=0)
        o_hi, o_lo = split2(jnp.broadcast_to(wide(O, b), (128, 512)))
        tile = jnp.broadcast_to(wide(index, b).astype(F32), (16, 512)).astype(BF16)
        left = [jnp.where(tile == BF16(t), v, zero) for t in range(NBR)]
        hot = (low == jnp.broadcast_to(wide(index, 32 + b).astype(F32), (128, 512)).astype(BF16)).astype(BF16)
        acc[0:512, :] += lax.dot_general(jnp.concatenate(left, axis=0), hot, NT, preferred_element_type=F32)
        mine = low == jnp.broadcast_to(wide(owner, b).astype(F32), (128, 512)).astype(BF16)
        hot = (low == jnp.broadcast_to(wide(index, 64 + b).astype(F32), (128, 512)).astype(BF16)).astype(BF16)
        left = [jnp.where(mine, o_hi, jnp.zeros_like(o_hi)), jnp.where(mine, o_lo, jnp.zeros_like(o_lo))]
        acc[512:768, :] += lax.dot_general(jnp.concatenate(left, axis=0), hot, NT, preferred_element_type=F32)
        return carry

    lax.fori_loop(0, NBR // 4, sort, 0, unroll=2)
    for t in range(NBR):
        Z[t] = acc[t * 16 : t * 16 + 8, :] + acc[t * 16 + 8 : t * 16 + 16, :]
    Z[32] = jnp.zeros((8, 128), F32)
    out_ref[:, 8 * 128 : 9 * 128] = acc[512:640, :] + acc[640:768, :]

    def expand(o, carry):
        st = starts[0, o]
        tile = lax.shift_right_logical(st, 7)
        q = 128 - lax.bitwise_and(st, 127)
        amount = lax.bitwise_and(q, 127)
        after = jnp.minimum(tile + 1, 32)
        tile = jnp.minimum(tile, 32)
        keep = lane < q
        a = pltpu.roll(Z[tile], amount, 1)
        b = pltpu.roll(Z[after], amount, 1)
        F[pl.ds(o, 8, stride=N_DEV), :] = jnp.where(keep, a, b)
        return carry

    lax.fori_loop(0, N_DEV, expand, 0, unroll=8)
    for f in range(8):
        out_ref[:, f * 128 : (f + 1) * 128] = F[f * N_DEV : (f + 1) * N_DEV, :]
    out_ref[:, 9 * 128 : 10 * 128] = meta[0]
    out_ref[:, 10 * 128 : 11 * 128] = meta[1]


def outer(*args):
    return pl.pallas_call(
        outer_kernel,
        name="outer",
        out_shape=(jax.ShapeDtypeStruct((256, 1024), F32), jax.ShapeDtypeStruct((N_DEV, 11 * 128), F32)),
        in_specs=[SMEM] * 4 + [ANY] * 5 + [VMEM] * 7,
        out_specs=[VMEM] * 2,
        scratch_shapes=[
            pltpu.VMEM((10, 512, 128), F32),
            pltpu.VMEM((4, 4, 8, 8, 128), F32),
            pltpu.VMEM((8, 256, 128), F32),
            pltpu.VMEM((288, 128), F32),
            pltpu.VMEM((33, 8, 128), F32),
            pltpu.VMEM((32, 8, 128), F32),
            pltpu.VMEM((32, 128), F32),
            pltpu.VMEM((8 * N_DEV, 128), F32),
            pltpu.VMEM((768, 128), F32),
            pltpu.SemaphoreType.DMA((30,)),
        ],
        compiler_params=pltpu.CompilerParams(vmem_limit_bytes=32 * 1024 * 1024),
        cost_estimate=pl.CostEstimate(flops=int(4e8), bytes_accessed=20000000, transcendentals=0),
    )(*args)


def cells_kernel(got_ref, horizon_ref, svf_ref, G):
    for f in range(9):
        G[pl.ds(f, N_DEV, stride=16), :] = got_ref[:, f * 128 : (f + 1) * 128]
    cell = got_ref[:, 9 * 128 : 10 * 128].astype(jnp.int32) - 1
    G[pl.ds(9, N_DEV, stride=16), :] = lax.shift_right_arithmetic(cell, 7).astype(F32)
    G[pl.ds(10, N_DEV, stride=16), :] = got_ref[:, 10 * 128 : 11 * 128]
    G[pl.ds(11, N_DEV, stride=16), :] = lax.bitwise_and(cell, 127).astype(F32)
    for f in range(12, 16):
        G[pl.ds(f, N_DEV, stride=16), :] = jnp.zeros((N_DEV, 128), F32)
    low = iota((128, 512), 0).astype(F32).astype(BF16)

    def accumulate(t, acc):
        base = pl.multiple_of(t * 64, 64)
        v = jnp.concatenate([G[pl.ds(base + 16 * i, 16), :] for i in range(4)], axis=1)
        hi, lo = split2(v)
        high = jnp.broadcast_to(v[9:10, :], (16, 512)).astype(BF16)
        zero = jnp.zeros((16, 512), BF16)
        left = []
        for h in range(4):
            mine = high == BF16(h)
            left += [jnp.where(mine, hi, zero), jnp.where(mine, lo, zero)]
        hot = (low == jnp.broadcast_to(v[11:12, :], (128, 512)).astype(BF16)).astype(BF16)
        return acc + lax.dot_general(jnp.concatenate(left, axis=0), hot, NT, preferred_element_type=F32)

    acc = lax.fori_loop(0, N_DEV // 4, accumulate, jnp.zeros((128, 128), F32), unroll=8)
    sums = jnp.concatenate([acc[h * 32 : h * 32 + 16] + acc[h * 32 + 16 : h * 32 + 32] for h in range(4)], axis=1)
    area = jnp.maximum(sums[10:11, :] * (1.0 / 64.0), 1.0)
    horizon_ref[...] = sums[0:8] / area
    svf_ref[...] = sums[8:9] / area


def cells(got):
    return pl.pallas_call(
        cells_kernel,
        name="cells",
        out_shape=(jax.ShapeDtypeStruct((AZ, CELLS_DEV), F32), jax.ShapeDtypeStruct((1, CELLS_DEV), F32)),
        in_specs=[VMEM],
        out_specs=[VMEM] * 2,
        scratch_shapes=[pltpu.VMEM((16 * N_DEV, 128), F32)],
        compiler_params=pltpu.CompilerParams(vmem_limit_bytes=24 * 1024 * 1024),
    )(got)


def shards(terrain_surface, azimuth_lag_tallies, holder_devices, holder_region_slot, footprint_weight):
    rows, width = terrain_surface.shape
    n_lat = lax.axis_size("lat")
    n_lon = lax.axis_size("lon")
    W = FARTHEST_LAG
    own = terrain_surface
    east_pairs = [((i + 1) % n_lon, i) for i in range(n_lon)]
    west = lax.ppermute(own[:, width - W :], "lon", [(j, i) for i, j in east_pairs])
    east = lax.ppermute(own[:, :W], "lon", east_pairs)
    weight = footprint_weight.reshape(NBR, 128)
    owner = holder_devices.reshape(NBR, 128)
    start, index, meta = route(owner, holder_region_slot.reshape(NBR, 128), weight)
    west, east, start, index, meta = lax.optimization_barrier((west, east, start, index, meta))
    wide = jnp.concatenate([west, own, east], axis=1)
    down = [(i, i + 1) for i in range(n_lat - 1)]
    north = lax.ppermute(wide[rows - W :], "lat", down)
    south = lax.ppermute(wide[:W], "lat", [(j, i) for i, j in down])

    rows_global = (lax.axis_index("lat") * rows + jnp.arange(rows, dtype=jnp.int32)).astype(F32)
    latitude = 47.0 - (rows_global + 0.5) / 1200.0
    coslat = jnp.cos(latitude * jnp.pi / 180.0)
    across = (pixel_size * coslat) ** 2
    inv_base = 1.0 / jnp.sqrt(jnp.stack([pixel_size**2 + across, across]))
    inv_base = jnp.broadcast_to(inv_base[:, :, None], (2, rows, 128))
    lat = jnp.stack([lax.axis_index("lat").astype(jnp.int32), jnp.int32(n_lat)])
    inv_lags = 1.0 / azimuth_lag_tallies.astype(F32)
    part, sums = inner(azimuth_lag_tallies, inv_lags, own, west, east, inv_base)
    fine_svf, packed = outer(
        azimuth_lag_tallies, inv_lags, start, lat, own, north, south, west, east, inv_base, part, sums, weight, owner, index, meta
    )
    got = lax.all_to_all(packed, ("lat", "lon"), split_axis=0, concat_axis=0, tiled=True)
    cell_horizon, cell_svf = cells(got)
    return fine_svf, cell_horizon, cell_svf.reshape(CELLS_DEV)


def solution(mesh):
    P = jax.sharding.PartitionSpec
    in_specs = (P("lat", "lon"), P(), P(("lat", "lon"), None), P(("lat", "lon")), P(("lat", "lon")))
    out_specs = (P("lat", "lon"), P(None, ("lat", "lon")), P(("lat", "lon")))
    return jax.shard_map(shards, mesh=mesh, in_specs=in_specs, out_specs=out_specs, check_vma=False)
```

```python
import jax
import jax.numpy as jnp
from jax import lax
from jax.experimental import pallas as pl
from jax.experimental.pallas import tpu as pltpu

FARTHEST_LAG = 128
AZ = 8
KS = 8
pixel_size = 92.6
ATAN = (0.9999999, -0.33331991, 0.19969724, -0.14019481, 0.09914293, -0.05948639, 0.0242524, -0.00469327)
HALF_PI = 1.5707963267948966


def recip(v):
    g = pl.reciprocal(v, approx=True)
    return g * (2.0 - v * g)


def angle(x, y):
    ax, ay = jnp.abs(x), jnp.abs(y)
    z = jnp.minimum(ax, ay) * recip(jnp.maximum(ax, ay))
    u = z * z
    p = ATAN[7]
    for c in ATAN[6::-1]:
        p = p * u + c
    p = p * z
    p = jnp.where(ay > ax, HALF_PI - p, p)
    p = jnp.where(x < 0.0, 2.0 * HALF_PI - p, p)
    return jnp.where(y < 0.0, 4.0 * HALF_PI - p, p)


N_DEV = 128
NBR = 32
CELLS_DEV = 512
F32 = jnp.float32
BF16 = jnp.bfloat16
VMEM = pl.BlockSpec(memory_space=pltpu.VMEM)
SMEM = pl.BlockSpec(memory_space=pltpu.SMEM)
ANY = pl.BlockSpec(memory_space=pl.ANY)
NT = (((1,), (1,)), ((), ()))


def split2(v):
    hi = v.astype(BF16)
    return hi, (v - hi.astype(F32)).astype(BF16)


def iota(shape, dim):
    return lax.broadcasted_iota(jnp.int32, shape, dim)


def route_kernel(owner_ref, slot_ref, weight_ref, start_ref, index_ref, meta_ref, rank_ref):
    sub = iota((N_DEV, 128), 0)
    upper = (iota((128, 128), 0) < iota((128, 128), 1)).astype(BF16)
    right = jnp.concatenate([upper, jnp.ones((128, 128), BF16)], axis=1)
    count = jnp.zeros((N_DEV, 128), F32)
    for i in range(NBR):
        mine = sub == owner_ref[i : i + 1, :]
        both = jnp.dot(mine.astype(BF16), right, preferred_element_type=F32)
        rank = jnp.sum(jnp.where(mine, both[:, :128] + count, 0.0), axis=0, keepdims=True)
        rank_ref[i : i + 1, :] = rank
        count = count + both[:, 128:]
    lower = (iota((128, 128), 0) > iota((128, 128), 1)).astype(BF16)
    start = jnp.dot(lower, count.astype(BF16), preferred_element_type=F32)
    start_row = lax.dot_general(count[:, :8].T.astype(BF16), upper, (((1,), (0,)), ((), ())), preferred_element_type=F32)
    start_ref[...] = start_row[:1].astype(jnp.int32)
    meta = jnp.zeros((3 * N_DEV, 128), F32)
    for i in range(NBR):
        mine = sub == owner_ref[i : i + 1, :]
        rank = rank_ref[i : i + 1, :]
        place = (rank + jnp.sum(jnp.where(mine, start, 0.0), axis=0, keepdims=True)).astype(jnp.int32)
        rank = rank.astype(jnp.int32)
        index_ref[i : i + 1, :] = lax.shift_right_logical(place, 7)
        index_ref[NBR + i : NBR + i + 1, :] = lax.bitwise_and(place, 127)
        index_ref[2 * NBR + i : 2 * NBR + i + 1, :] = rank
        rank_hot = (sub == rank).astype(BF16)
        slot = slot_ref[i : i + 1, :] + 1
        parts = (lax.shift_right_logical(slot, 4), lax.bitwise_and(slot, 15), weight_ref[i : i + 1, :])
        left = jnp.concatenate([jnp.where(mine, v.astype(F32), 0.0) for v in parts], axis=0).astype(BF16)
        meta = meta + lax.dot_general(left, rank_hot, NT, preferred_element_type=F32)
    meta_ref[0] = meta[:N_DEV] * 16.0 + meta[N_DEV : 2 * N_DEV]
    meta_ref[1] = meta[2 * N_DEV :]


def route(owner, slot, weight):
    return pl.pallas_call(
        route_kernel,
        name="route",
        out_shape=(
            jax.ShapeDtypeStruct((1, N_DEV), jnp.int32),
            jax.ShapeDtypeStruct((96, 128), jnp.int32),
            jax.ShapeDtypeStruct((2, N_DEV, 128), F32),
        ),
        in_specs=[VMEM] * 3,
        out_specs=[VMEM] * 3,
        scratch_shapes=[pltpu.VMEM((NBR, 128), F32)],
        cost_estimate=pl.CostEstimate(flops=int(4e8), bytes_accessed=200000, transcendentals=0),
    )(owner, slot, weight)


def quad(r):
    x0, y0 = 1.0 - r[0] * r[1], r[0] + r[1]
    x1, y1 = 1.0 - r[2] * r[3], r[2] + r[3]
    return angle(x0 * x1 - y0 * y1, x0 * y1 + x1 * y0)


class Ray:
    def __init__(self, azimuth, step, near, far, inv_base, opening, put):
        self.azimuth, self.step, self.near, self.far = azimuth, step, near, far
        self.inv_base, self.opening, self.put = inv_base, opening, put


def plane_rays(H, it, h0, rays, inv_base, V_old, V, S_ref):
    lane = iota((8, 128), 1)
    rc = lax.shift_right_logical(it, 1)
    p0 = lax.bitwise_and(it, 1) * 4
    block = pl.multiple_of(rc * 8, 8)
    made = []
    for f, (a, sy, sx) in enumerate(rays):
        off = 1 if sx >= 0 else 0
        count = 8 if sx == 0 else 9

        def near(p):
            rows = pl.ds(pl.multiple_of(h0 // 8 + rc * 8, 8), 8)
            return [H[1 + j, p0 + p, rows, :] for j in range(8)]

        def far(p, s, sy=sy, sx=sx, off=off, count=count):
            y = h0 + rc * 64 + p0 + p + sy * s
            plane, i0 = lax.bitwise_and(y, 7), lax.shift_right_logical(y, 3)
            tiles = [H[off + j, plane, pl.ds(i0, 8), :] for j in range(count)]
            if sx == 0:
                return tiles
            amount = 128 - s if sx == 1 else lax.bitwise_and(s, 127)
            keep = lane < (amount if sx == 1 else s)
            rolled = [pltpu.roll(v, amount, 1) for v in tiles]
            return [jnp.where(keep, rolled[j], rolled[j + 1]) for j in range(8)]

        def base(p, sx=sx):
            return 1.0 / pixel_size if sx == 0 else inv_base[p0 + p, pl.ds(block, 8), :]

        def opening(p, j, v, f=f):
            old = V_old if f == 0 else V
            at = (j, p0 + p, pl.ds(block, 8))
            V[at] = v if old is None else old[at] + v

        def put(j, v, f=f):
            S_ref[rc, f, j] += v

        made.append(Ray(a, sy, near, far, base, opening, put))
    return made


def turned_rays(H, it, inv_row, V, S_ref):
    rt = lax.shift_right_logical(it, 2)
    half = lax.bitwise_and(lax.shift_right_logical(it, 1), 1)
    p0 = lax.bitwise_and(it, 1) * 4
    made = []
    for f, (a, sx) in enumerate(((0, 1), (4, -1))):

        def near(p):
            return [H[rt, p0 + p, pl.ds(pl.multiple_of(16 + half * 64 + 8 * j, 8), 8), :] for j in range(8)]

        def far(p, s, sx=sx):
            x = 128 + half * 512 + p0 + p + sx * s
            plane, i0 = lax.bitwise_and(x, 7), lax.shift_right_logical(x, 3)
            return [H[rt, plane, pl.ds(i0 + 8 * j, 8), :] for j in range(8)]

        def base(p):
            return jnp.broadcast_to(inv_row[pl.ds(rt, 1), :], (8, 128))

        def rows(j):
            return pl.ds(pl.multiple_of(half * 64 + 8 * j, 8), 8)

        def opening(p, j, v, f=f):
            at = (rt, p0 + p, rows(j))
            V[at] = v if f == 0 else V[at] + v

        def put(j, v, f=f):
            S_ref[rt, f, rows(j), :] += v

        made.append(Ray(a, sx, near, far, base, opening, put))
    return made


def march(lags, inv_lags, group, rise):
    for p in range(4):
        t = [ray.near(p) for ray in group]
        best = [[None] * 8 for ray in group]
        for k in range(KS):
            for i, ray in enumerate(group):
                inv_lag = inv_lags[ray.azimuth, k]
                got = ray.far(p, lags[ray.azimuth, k])
                for j in range(8):
                    v = (got[j] - t[i][j]) * inv_lag
                    best[i][j] = v if k == 0 else jnp.maximum(best[i][j], v)
        for i, ray in enumerate(group):
            ib = ray.inv_base(p)
            for j in range(8):
                rise[i, p, j] = jnp.minimum(jnp.maximum(best[i][j] * ib, 0.0), 1e8)


def finish(group, rise):
    for i, ray in enumerate(group):
        for j in range(8):
            r = [rise[i, p, j] for p in range(4)]
            for p in range(4):
                ray.opening(p, j, recip(1.0 + r[p] * r[p]))
            ray.put(j, quad(r))


def slanted(southward):
    sy = jnp.where(southward, 1, -1)
    return [(jnp.where(southward, 3, 5), sy, -1), (jnp.where(southward, 2, 6), sy, 0), (jnp.where(southward, 1, 7), sy, 1)]


def copies(pairs, sems):
    made = [pltpu.make_async_copy(a, b, sems.at[i]) for i, (a, b) in enumerate(pairs)]
    for c in made:
        c.start()
    for c in made:
        c.wait()


def cols(j):
    return pl.ds(j * 128, 128)


def inner_kernel(
    lags, inv_lags, own, west, east, inv_base, inv_row, V_ref, S_ref, pooled_ref, Hn, H, Tn, T, VT, ST, X, Xn, rise, sems
):
    copies(
        [(own.at[:, cols(j)], Hn.at[1 + j]) for j in range(8)] + [(west, Hn.at[0]), (east, Hn.at[9])], sems
    )
    for c in range(10):
        for p in range(8):
            H[c, p] = Hn[c, pl.ds(p, 32, stride=8), :]
        for rt in range(2):
            Tn[rt, c * 128 : (c + 1) * 128, :] = Hn[c, rt * 128 : (rt + 1) * 128, :].T
    for rt in range(2):
        for p in range(8):
            T[rt, p] = Tn[rt, pl.ds(p, 160, stride=8), :]
    S_ref[...] = jnp.zeros(S_ref.shape, F32)
    ST[...] = jnp.zeros(ST.shape, F32)

    def step(it, carry):
        left, up, right = plane_rays(H, it, 0, slanted(it < 4), inv_base, None, V_ref, S_ref)
        along, against = turned_rays(T, it, inv_row, VT, ST)
        groups = ((left, along), (right, against), (up,))
        order = (0, 2, 1)
        for n, g in enumerate(groups):
            march(lags, inv_lags, g, rise.at[n])
        for n in order:
            finish(groups[n], rise.at[n])
        return carry

    lax.fori_loop(0, 8, step, 0)
    pool = (iota((16, 128), 0) == lax.shift_right_logical(iota((16, 128), 1), 3)).astype(BF16)
    for rt in range(2):
        for f in range(2):
            hi, lo = split2(ST[rt, f])
            total = lax.dot_general(pool, hi, NT, preferred_element_type=F32)
            pooled_ref[f, rt * 16 : rt * 16 + 16, :] = total + lax.dot_general(pool, lo, NT, preferred_element_type=F32)
        for c in range(8):
            for p in range(8):
                X[rt, c, pl.ds(p, 16, stride=8), :] = VT[rt, p, c * 16 : (c + 1) * 16, :]
    for rt in range(2):
        for c in range(8):
            Xn[rt, c] = X[rt, c].T
    for rt in range(2):
        for c in range(8):
            for p in range(8):
                V_ref[c, p, rt * 16 : rt * 16 + 16, :] += Xn[rt, c, pl.ds(p, 16, stride=8), :]


def inner(*args):
    return pl.pallas_call(
        inner_kernel,
        name="inner",
        out_shape=(
            jax.ShapeDtypeStruct((8, 8, 32, 128), F32),
            jax.ShapeDtypeStruct((4, 3, 8, 8, 128), F32),
            jax.ShapeDtypeStruct((2, NBR, 128), F32),
        ),
        in_specs=[SMEM] * 2 + [ANY] * 3 + [VMEM] * 2,
        out_specs=[VMEM] * 3,
        scratch_shapes=[
            pltpu.VMEM((10, 256, 128), F32),
            pltpu.VMEM((10, 8, 32, 128), F32),
            pltpu.VMEM((2, 1280, 128), F32),
            pltpu.VMEM((2, 8, 160, 128), F32),
            pltpu.VMEM((2, 8, 128, 128), F32),
            pltpu.VMEM((2, 2, 128, 128), F32),
            pltpu.VMEM((2, 8, 128, 128), F32),
            pltpu.VMEM((2, 8, 128, 128), F32),
            pltpu.VMEM((3, 2, 4, 8, 8, 128), F32),
            pltpu.SemaphoreType.DMA((10,)),
        ],
        compiler_params=pltpu.CompilerParams(vmem_limit_bytes=32 * 1024 * 1024),
        cost_estimate=pl.CostEstimate(flops=int(4e8), bytes_accessed=30000000, transcendentals=0),
    )(*args)


def outer_kernel(
    lags, inv_lags, starts, lat, own, north, south, west, east, inv_base, V_in, S_in, pooled, weight, owner, index, meta,
    svf_ref, out_ref, Hn, H, S, V, Vn, R, Z, Y, O, acc, rise, sems,
):
    pairs = [(own.at[:, cols(j)], Hn.at[1 + j, pl.ds(128, 256)]) for j in range(8)]
    pairs += [(west, Hn.at[0, pl.ds(128, 256)]), (east, Hn.at[9, pl.ds(128, 256)])]
    pairs += [(north.at[:, cols(j)], Hn.at[j, pl.ds(0, 128)]) for j in range(10)]
    pairs += [(south.at[:, cols(j)], Hn.at[j, pl.ds(384, 128)]) for j in range(10)]
    copies(pairs, sems)

    @pl.when(lat[0] == 0)
    def _():
        for c in range(10):
            Hn[c, 0:128, :] = jnp.broadcast_to(Hn[c, 128:129, :], (128, 128))

    @pl.when(lat[0] == lat[1] - 1)
    def _():
        for c in range(10):
            Hn[c, 384:512, :] = jnp.broadcast_to(Hn[c, 383:384, :], (128, 128))

    for c in range(10):
        for p in range(8):
            H[c, p] = Hn[c, pl.ds(p, 64, stride=8), :]
    S[...] = jnp.zeros(S.shape, F32)

    def step(it, carry):
        left, up, right = plane_rays(H, it, 128, slanted(it >= 4), inv_base, V_in, V, S)
        groups = ((left, up), (right,))
        for n, g in enumerate(groups):
            march(lags, inv_lags, g, rise.at[n])
        for n, g in enumerate(groups):
            finish(g, rise.at[n])
        return carry

    lax.fori_loop(0, 8, step, 0)
    svf_rows = []
    for j in range(8):
        rows = V[j, 0]
        for p in range(8):
            Vn[j, pl.ds(p, 32, stride=8), :] = V[j, p] * (1.0 / AZ)
            rows = rows if p == 0 else rows + V[j, p]
        svf_rows.append(rows)
    for j in range(8):
        svf_ref[:, j * 128 : (j + 1) * 128] = Vn[j]

    total = jnp.zeros((224, 128), F32)
    for j in range(8):
        pool = (iota((128, 128), 1) == j * 16 + lax.shift_right_logical(iota((128, 128), 0), 3)).astype(BF16)
        field = []
        for rc in range(4):
            south, north_ = (S_in, S) if rc < 2 else (S, S_in)
            field += [south[rc, 2, j], south[rc, 1, j], south[rc, 0, j], north_[rc, 0, j], north_[rc, 1, j], north_[rc, 2, j]]
            field.append(svf_rows[j][rc * 8 : rc * 8 + 8, :])
        hi, lo = split2(jnp.concatenate(field, axis=0))
        total = total + jnp.dot(hi, pool, preferred_element_type=F32) + jnp.dot(lo, pool, preferred_element_type=F32)
    for rc in range(4):
        part = [total[rc * 56 + 8 * i : rc * 56 + 8 * i + 8] for i in range(7)]
        flat = [pooled[f, rc * 8 : rc * 8 + 8, :] for f in range(2)]
        R[rc * 72 : rc * 72 + 72, :] = jnp.concatenate([flat[0]] + part[:3] + [flat[1]] + part[3:], axis=0)
    lane = iota((8, 128), 1)
    scale = 1.0 / 4096.0
    for rc in range(4):
        for i in range(8):
            b = rc * 8 + i
            Y[b] = R[pl.ds(rc * 72 + i, 8, stride=8), :] * (weight[b : b + 1, :].astype(F32) * scale)
        O[rc * 8 : rc * 8 + 8, :] = R[rc * 72 + 64 : rc * 72 + 72, :] * (weight[rc * 8 : rc * 8 + 8, :].astype(F32) * (scale / AZ))

    acc[...] = jnp.zeros(acc.shape, F32)
    low = iota((128, 512), 0).astype(F32).astype(BF16)
    zero = jnp.zeros((16, 512), BF16)

    def wide(ref, row):
        return jnp.concatenate([ref[pl.ds(row + i, 1), :] for i in range(4)], axis=1)

    def sort(g, carry):
        b = g * 4
        v = jnp.concatenate([Y[b + i] for i in range(4)], axis=1)
        v = jnp.concatenate(split2(v), axis=0)
        o_hi, o_lo = split2(jnp.broadcast_to(wide(O, b), (128, 512)))
        tile = jnp.broadcast_to(wide(index, b).astype(F32), (16, 512)).astype(BF16)
        left = [jnp.where(tile == BF16(t), v, zero) for t in range(NBR)]
        hot = (low == jnp.broadcast_to(wide(index, 32 + b).astype(F32), (128, 512)).astype(BF16)).astype(BF16)
        acc[0:512, :] += lax.dot_general(jnp.concatenate(left, axis=0), hot, NT, preferred_element_type=F32)
        mine = low == jnp.broadcast_to(wide(owner, b).astype(F32), (128, 512)).astype(BF16)
        hot = (low == jnp.broadcast_to(wide(index, 64 + b).astype(F32), (128, 512)).astype(BF16)).astype(BF16)
        left = [jnp.where(mine, o_hi, jnp.zeros_like(o_hi)), jnp.where(mine, o_lo, jnp.zeros_like(o_lo))]
        acc[512:768, :] += lax.dot_general(jnp.concatenate(left, axis=0), hot, NT, preferred_element_type=F32)
        return carry

    lax.fori_loop(0, NBR // 4, sort, 0, unroll=2)
    for t in range(NBR):
        Z[t] = acc[t * 16 : t * 16 + 8, :] + acc[t * 16 + 8 : t * 16 + 16, :]
    Z[32] = jnp.zeros((8, 128), F32)
    out_ref[pl.ds(8, N_DEV, stride=11), :] = acc[512:640, :] + acc[640:768, :]
    out_ref[pl.ds(9, N_DEV, stride=11), :] = meta[0]
    out_ref[pl.ds(10, N_DEV, stride=11), :] = meta[1]

    def expand(o, carry):
        st = starts[0, o]
        tile = lax.shift_right_logical(st, 7)
        q = 128 - lax.bitwise_and(st, 127)
        amount = lax.bitwise_and(q, 127)
        after = jnp.minimum(tile + 1, 32)
        tile = jnp.minimum(tile, 32)
        keep = lane < q
        a = pltpu.roll(Z[tile], amount, 1)
        b = pltpu.roll(Z[after], amount, 1)
        out_ref[pl.ds(o * 11, 8), :] = jnp.where(keep, a, b)
        return carry

    lax.fori_loop(0, N_DEV, expand, 0, unroll=8)


def outer(*args):
    return pl.pallas_call(
        outer_kernel,
        name="outer",
        out_shape=(jax.ShapeDtypeStruct((256, 1024), F32), jax.ShapeDtypeStruct((N_DEV * 11, 128), F32)),
        in_specs=[SMEM] * 4 + [ANY] * 5 + [VMEM] * 8,
        out_specs=[VMEM] * 2,
        scratch_shapes=[
            pltpu.VMEM((10, 512, 128), F32),
            pltpu.VMEM((10, 8, 64, 128), F32),
            pltpu.VMEM((4, 3, 8, 8, 128), F32),
            pltpu.VMEM((8, 8, 32, 128), F32),
            pltpu.VMEM((8, 256, 128), F32),
            pltpu.VMEM((288, 128), F32),
            pltpu.VMEM((33, 8, 128), F32),
            pltpu.VMEM((32, 8, 128), F32),
            pltpu.VMEM((32, 128), F32),
            pltpu.VMEM((768, 128), F32),
            pltpu.VMEM((2, 2, 4, 8, 8, 128), F32),
            pltpu.SemaphoreType.DMA((30,)),
        ],
        compiler_params=pltpu.CompilerParams(vmem_limit_bytes=32 * 1024 * 1024),
        cost_estimate=pl.CostEstimate(flops=int(4e8), bytes_accessed=20000000, transcendentals=0),
    )(*args)


def cells_kernel(got_ref, horizon_ref, svf_ref):
    low = iota((128, 512), 0).astype(F32).astype(BF16)

    def accumulate(t, acc):
        first = jnp.concatenate([got_ref[pl.ds(t * 44 + 11 * i, 8), :] for i in range(4)], axis=1)
        second = jnp.concatenate([got_ref[pl.ds(t * 44 + 11 * i + 3, 8), :] for i in range(4)], axis=1)
        hi, lo = split2(jnp.concatenate([first, second], axis=0))
        cell = second[6:7, :] - 1.0
        upper = jnp.floor(cell * (1.0 / 128.0))
        high = jnp.broadcast_to(upper, (16, 512)).astype(BF16)
        zero = jnp.zeros((16, 512), BF16)
        left = []
        for h in range(4):
            mine = high == BF16(h)
            left += [jnp.where(mine, hi, zero), jnp.where(mine, lo, zero)]
        hot = (low == jnp.broadcast_to(cell - 128.0 * upper, (128, 512)).astype(BF16)).astype(BF16)
        return acc + lax.dot_general(jnp.concatenate(left, axis=0), hot, NT, preferred_element_type=F32)

    acc = lax.fori_loop(0, N_DEV // 4, accumulate, jnp.zeros((128, 128), F32), unroll=8)
    sums = jnp.concatenate([acc[h * 32 : h * 32 + 16] + acc[h * 32 + 16 : h * 32 + 32] for h in range(4)], axis=1)
    area = jnp.maximum(sums[15:16, :] * (1.0 / 64.0), 1.0)
    horizon_ref[...] = sums[0:8] / area
    svf_ref[...] = sums[13:14] / area


def cells(got):
    return pl.pallas_call(
        cells_kernel,
        name="cells",
        out_shape=(jax.ShapeDtypeStruct((AZ, CELLS_DEV), F32), jax.ShapeDtypeStruct((1, CELLS_DEV), F32)),
        in_specs=[VMEM],
        out_specs=[VMEM] * 2,
        compiler_params=pltpu.CompilerParams(vmem_limit_bytes=24 * 1024 * 1024),
    )(got)


def shards(terrain_surface, azimuth_lag_tallies, holder_devices, holder_region_slot, footprint_weight):
    rows, width = terrain_surface.shape
    n_lat = lax.axis_size("lat")
    n_lon = lax.axis_size("lon")
    W = FARTHEST_LAG
    own = terrain_surface
    east_pairs = [((i + 1) % n_lon, i) for i in range(n_lon)]
    west = lax.ppermute(own[:, width - W :], "lon", [(j, i) for i, j in east_pairs])
    east = lax.ppermute(own[:, :W], "lon", east_pairs)
    weight = footprint_weight.reshape(NBR, 128)
    owner = holder_devices.reshape(NBR, 128)
    start, index, meta = route(owner, holder_region_slot.reshape(NBR, 128), weight)
    west, east, start, index, meta = lax.optimization_barrier((west, east, start, index, meta))
    wide = jnp.concatenate([west, own, east], axis=1)
    down = [(i, i + 1) for i in range(n_lat - 1)]
    north = lax.ppermute(wide[rows - W :], "lat", down)
    south = lax.ppermute(wide[:W], "lat", [(j, i) for i, j in down])

    rows_global = (lax.axis_index("lat") * rows + jnp.arange(rows, dtype=jnp.int32)).astype(F32)
    latitude = 47.0 - (rows_global + 0.5) / 1200.0
    coslat = jnp.cos(latitude * jnp.pi / 180.0)
    across = (pixel_size * coslat) ** 2
    inv_row = (1.0 / jnp.sqrt(across)).reshape(2, 128)
    inv_base = 1.0 / jnp.sqrt(pixel_size**2 + across)
    inv_base = jnp.broadcast_to(inv_base.reshape(32, 8).T[:, :, None], (8, 32, 128))
    lat = jnp.stack([lax.axis_index("lat").astype(jnp.int32), jnp.int32(n_lat)])
    inv_lags = 1.0 / azimuth_lag_tallies.astype(F32)
    part, sums, pooled = inner(azimuth_lag_tallies, inv_lags, own, west, east, inv_base, inv_row)
    fine_svf, packed = outer(
        azimuth_lag_tallies, inv_lags, start, lat, own, north, south, west, east, inv_base, part, sums, pooled,
        weight, owner, index, meta,
    )
    packed = packed.reshape(N_DEV, 1, 11 * 128)
    got = lax.all_to_all(packed, ("lat", "lon"), split_axis=0, concat_axis=0, tiled=True)
    got = got.reshape(N_DEV * 11, 128)
    cell_horizon, cell_svf = cells(got)
    return fine_svf, cell_horizon, cell_svf.reshape(CELLS_DEV)


def solution(mesh):
    P = jax.sharding.PartitionSpec
    in_specs = (P("lat", "lon"), P(), P(("lat", "lon"), None), P(("lat", "lon")), P(("lat", "lon")))
    out_specs = (P("lat", "lon"), P(None, ("lat", "lon")), P(("lat", "lon")))
    return jax.shard_map(shards, mesh=mesh, in_specs=in_specs, out_specs=out_specs, check_vma=False)
```

```python
import jax
import jax.numpy as jnp
from jax import lax
from jax.experimental import pallas as pl
from jax.experimental.pallas import tpu as pltpu

FARTHEST_LAG = 128
AZ = 8
KS = 8
pixel_size = 92.6
ATAN = (0.9999999, -0.33331991, 0.19969724, -0.14019481, 0.09914293, -0.05948639, 0.0242524, -0.00469327)
HALF_PI = 1.5707963267948966


def recip(v):
    return pl.reciprocal(v, approx=True)


def angle(x, y):
    ax, ay = jnp.abs(x), jnp.abs(y)
    z = jnp.minimum(ax, ay) * recip(jnp.maximum(ax, ay))
    u = z * z
    p = ATAN[7]
    for c in ATAN[6::-1]:
        p = p * u + c
    p = p * z
    p = jnp.where(ay > ax, HALF_PI - p, p)
    p = jnp.where(x < 0.0, 2.0 * HALF_PI - p, p)
    return jnp.where(y < 0.0, 4.0 * HALF_PI - p, p)


N_DEV = 128
NBR = 32
CELLS_DEV = 512
F32 = jnp.float32
BF16 = jnp.bfloat16
VMEM = pl.BlockSpec(memory_space=pltpu.VMEM)
SMEM = pl.BlockSpec(memory_space=pltpu.SMEM)
ANY = pl.BlockSpec(memory_space=pl.ANY)
NT = (((1,), (1,)), ((), ()))


def split2(v):
    hi = v.astype(BF16)
    return hi, (v - hi.astype(F32)).astype(BF16)


def iota(shape, dim):
    return lax.broadcasted_iota(jnp.int32, shape, dim)


def route_kernel(owner_ref, slot_ref, weight_ref, start_ref, index_ref, meta_ref, rank_ref):
    sub = iota((N_DEV, 128), 0)
    upper = (iota((128, 128), 0) < iota((128, 128), 1)).astype(BF16)
    right = jnp.concatenate([upper, jnp.ones((128, 128), BF16)], axis=1)
    count = jnp.zeros((N_DEV, 128), F32)
    for i in range(NBR):
        mine = sub == owner_ref[i : i + 1, :]
        both = jnp.dot(mine.astype(BF16), right, preferred_element_type=F32)
        rank = jnp.sum(jnp.where(mine, both[:, :128] + count, 0.0), axis=0, keepdims=True)
        rank_ref[i : i + 1, :] = rank
        count = count + both[:, 128:]
    lower = (iota((128, 128), 0) > iota((128, 128), 1)).astype(BF16)
    start = jnp.dot(lower, count.astype(BF16), preferred_element_type=F32)
    start_row = lax.dot_general(count[:, :8].T.astype(BF16), upper, (((1,), (0,)), ((), ())), preferred_element_type=F32)
    start_ref[...] = start_row[:1].astype(jnp.int32)
    meta = jnp.zeros((3 * N_DEV, 128), F32)
    for i in range(NBR):
        mine = sub == owner_ref[i : i + 1, :]
        rank = rank_ref[i : i + 1, :]
        place = (rank + jnp.sum(jnp.where(mine, start, 0.0), axis=0, keepdims=True)).astype(jnp.int32)
        rank = rank.astype(jnp.int32)
        index_ref[i : i + 1, :] = lax.shift_right_logical(place, 8)
        index_ref[NBR + i : NBR + i + 1, :] = lax.bitwise_and(place, 255)
        odd = lax.bitwise_and(owner_ref[i : i + 1, :], 1) * 128
        index_ref[2 * NBR + i : 2 * NBR + i + 1, :] = rank + odd
        rank_hot = (sub == rank).astype(BF16)
        slot = slot_ref[i : i + 1, :] + 1
        parts = (lax.shift_right_logical(slot, 4), lax.bitwise_and(slot, 15), weight_ref[i : i + 1, :])
        left = jnp.concatenate([jnp.where(mine, v.astype(F32), 0.0) for v in parts], axis=0).astype(BF16)
        meta = meta + lax.dot_general(left, rank_hot, NT, preferred_element_type=F32)
    meta_ref[0] = meta[:N_DEV] * 16.0 + meta[N_DEV : 2 * N_DEV]
    meta_ref[1] = meta[2 * N_DEV :]


def route(owner, slot, weight):
    return pl.pallas_call(
        route_kernel,
        name="route",
        out_shape=(
            jax.ShapeDtypeStruct((1, N_DEV), jnp.int32),
            jax.ShapeDtypeStruct((96, 128), jnp.int32),
            jax.ShapeDtypeStruct((2, N_DEV, 128), F32),
        ),
        in_specs=[VMEM] * 3,
        out_specs=[VMEM] * 3,
        scratch_shapes=[pltpu.VMEM((NBR, 128), F32)],
        cost_estimate=pl.CostEstimate(flops=int(4e8), bytes_accessed=200000, transcendentals=0),
    )(owner, slot, weight)


def quad(r):
    x0, y0 = 1.0 - r[0] * r[1], r[0] + r[1]
    x1, y1 = 1.0 - r[2] * r[3], r[2] + r[3]
    return angle(x0 * x1 - y0 * y1, x0 * y1 + x1 * y0)


class Ray:
    def __init__(self, azimuth, step, near, far, inv_base, opening, put):
        self.azimuth, self.step, self.near, self.far = azimuth, step, near, far
        self.inv_base, self.opening, self.put = inv_base, opening, put


def plane_rays(H, it, h0, rays, inv_base, V_old, V, S_ref):
    lane = iota((8, 128), 1)
    rc = lax.shift_right_logical(it, 1)
    p0 = lax.bitwise_and(it, 1) * 4
    block = pl.multiple_of(rc * 8, 8)
    made = []
    for f, (a, sy, sx) in enumerate(rays):
        off = 1 if sx >= 0 else 0
        count = 8 if sx == 0 else 9

        def near(p):
            rows = pl.ds(pl.multiple_of(h0 // 8 + rc * 8, 8), 8)
            return [H[1 + j, p0 + p, rows, :] for j in range(8)]

        def far(p, s, sy=sy, sx=sx, off=off, count=count):
            y = h0 + rc * 64 + p0 + p + sy * s
            plane, i0 = lax.bitwise_and(y, 7), lax.shift_right_logical(y, 3)
            tiles = [H[off + j, plane, pl.ds(i0, 8), :] for j in range(count)]
            if sx == 0:
                return tiles
            amount = 128 - s if sx == 1 else lax.bitwise_and(s, 127)
            keep = lane < (amount if sx == 1 else s)
            rolled = [pltpu.roll(v, amount, 1) for v in tiles]
            return [jnp.where(keep, rolled[j], rolled[j + 1]) for j in range(8)]

        def base(p, sx=sx):
            return 1.0 / pixel_size if sx == 0 else inv_base[p0 + p, pl.ds(block, 8), :]

        def opening(p, j, v, f=f):
            old = V_old if f == 0 else V
            at = (j, p0 + p, pl.ds(block, 8))
            V[at] = v if old is None else old[at] + v

        def put(j, v, f=f):
            S_ref[rc, f, j] += v

        made.append(Ray(a, sy, near, far, base, opening, put))
    return made


def turned_rays(H, it, inv_row, V, S_ref):
    rt = lax.shift_right_logical(it, 2)
    half = lax.bitwise_and(lax.shift_right_logical(it, 1), 1)
    p0 = lax.bitwise_and(it, 1) * 4
    made = []
    for f, (a, sx) in enumerate(((0, 1), (4, -1))):

        def near(p):
            return [H[rt, p0 + p, pl.ds(pl.multiple_of(16 + half * 64 + 8 * j, 8), 8), :] for j in range(8)]

        def far(p, s, sx=sx):
            x = 128 + half * 512 + p0 + p + sx * s
            plane, i0 = lax.bitwise_and(x, 7), lax.shift_right_logical(x, 3)
            return [H[rt, plane, pl.ds(i0 + 8 * j, 8), :] for j in range(8)]

        def base(p):
            return jnp.broadcast_to(inv_row[pl.ds(rt, 1), :], (8, 128))

        def rows(j):
            return pl.ds(pl.multiple_of(half * 64 + 8 * j, 8), 8)

        def opening(p, j, v, f=f):
            at = (rt, p0 + p, rows(j))
            V[at] = v if f == 0 else V[at] + v

        def put(j, v, f=f):
            S_ref[rt, f, rows(j), :] += v

        made.append(Ray(a, sx, near, far, base, opening, put))
    return made


def march(lags, inv_lags, group, rise):
    for p in range(4):
        t = [ray.near(p) for ray in group]
        best = [[None] * 8 for ray in group]
        for k in range(KS):
            for i, ray in enumerate(group):
                inv_lag = inv_lags[ray.azimuth, k]
                got = ray.far(p, lags[ray.azimuth, k])
                for j in range(8):
                    v = (got[j] - t[i][j]) * inv_lag
                    best[i][j] = v if k == 0 else jnp.maximum(best[i][j], v)
        for i, ray in enumerate(group):
            ib = ray.inv_base(p)
            for j in range(8):
                rise[i, p, j] = jnp.minimum(jnp.maximum(best[i][j] * ib, 0.0), 1e8)


def finish(group, rise):
    for i, ray in enumerate(group):
        for j in range(8):
            r = [rise[i, p, j] for p in range(4)]
            for p in range(4):
                ray.opening(p, j, recip(1.0 + r[p] * r[p]))
            ray.put(j, quad(r))


def slanted(southward):
    sy = jnp.where(southward, 1, -1)
    return [(jnp.where(southward, 3, 5), sy, -1), (jnp.where(southward, 2, 6), sy, 0), (jnp.where(southward, 1, 7), sy, 1)]


def copies(pairs, sems):
    made = [pltpu.make_async_copy(a, b, sems.at[i]) for i, (a, b) in enumerate(pairs)]
    for c in made:
        c.start()
    for c in made:
        c.wait()


def cols(j):
    return pl.ds(j * 128, 128)


def inner_kernel(
    lags, inv_lags, own, west, east, inv_base, inv_row, V_ref, S_ref, pooled_ref, Hn, H, Tn, T, VT, ST, X, Xn, rise, sems
):
    copies(
        [(own.at[:, cols(j)], Hn.at[1 + j]) for j in range(8)] + [(west, Hn.at[0]), (east, Hn.at[9])], sems
    )
    for c in range(10):
        for p in range(8):
            H[c, p] = Hn[c, pl.ds(p, 32, stride=8), :]
        for rt in range(2):
            Tn[rt, c * 128 : (c + 1) * 128, :] = Hn[c, rt * 128 : (rt + 1) * 128, :].T
    for rt in range(2):
        for p in range(8):
            T[rt, p] = Tn[rt, pl.ds(p, 160, stride=8), :]
    S_ref[...] = jnp.zeros(S_ref.shape, F32)
    ST[...] = jnp.zeros(ST.shape, F32)

    def step(it, carry):
        left, up, right = plane_rays(H, it, 0, slanted(it < 4), inv_base, None, V_ref, S_ref)
        along, against = turned_rays(T, it, inv_row, VT, ST)
        groups = ((left, along), (right, against), (up,))
        order = (0, 2, 1)
        for n, g in enumerate(groups):
            march(lags, inv_lags, g, rise.at[n])
        for n in order:
            finish(groups[n], rise.at[n])
        return carry

    lax.fori_loop(0, 8, step, 0)
    pool = (iota((16, 128), 0) == lax.shift_right_logical(iota((16, 128), 1), 3)).astype(BF16)
    for rt in range(2):
        for f in range(2):
            hi, lo = split2(ST[rt, f])
            total = lax.dot_general(pool, hi, NT, preferred_element_type=F32)
            pooled_ref[f, rt * 16 : rt * 16 + 16, :] = total + lax.dot_general(pool, lo, NT, preferred_element_type=F32)
        for c in range(8):
            for p in range(8):
                X[rt, c, pl.ds(p, 16, stride=8), :] = VT[rt, p, c * 16 : (c + 1) * 16, :]
    for rt in range(2):
        for c in range(8):
            Xn[rt, c] = X[rt, c].T
    for rt in range(2):
        for c in range(8):
            for p in range(8):
                V_ref[c, p, rt * 16 : rt * 16 + 16, :] += Xn[rt, c, pl.ds(p, 16, stride=8), :]


def inner(*args):
    return pl.pallas_call(
        inner_kernel,
        name="inner",
        out_shape=(
            jax.ShapeDtypeStruct((8, 8, 32, 128), F32),
            jax.ShapeDtypeStruct((4, 3, 8, 8, 128), F32),
            jax.ShapeDtypeStruct((2, NBR, 128), F32),
        ),
        in_specs=[SMEM] * 2 + [ANY] * 3 + [VMEM] * 2,
        out_specs=[VMEM] * 3,
        scratch_shapes=[
            pltpu.VMEM((10, 256, 128), F32),
            pltpu.VMEM((10, 8, 32, 128), F32),
            pltpu.VMEM((2, 1280, 128), F32),
            pltpu.VMEM((2, 8, 160, 128), F32),
            pltpu.VMEM((2, 8, 128, 128), F32),
            pltpu.VMEM((2, 2, 128, 128), F32),
            pltpu.VMEM((2, 8, 128, 128), F32),
            pltpu.VMEM((2, 8, 128, 128), F32),
            pltpu.VMEM((3, 2, 4, 8, 8, 128), F32),
            pltpu.SemaphoreType.DMA((10,)),
        ],
        compiler_params=pltpu.CompilerParams(vmem_limit_bytes=32 * 1024 * 1024),
        cost_estimate=pl.CostEstimate(flops=int(4e8), bytes_accessed=30000000, transcendentals=0),
    )(*args)


def outer_kernel(
    lags, inv_lags, starts, lat, own, north, south, west, east, inv_base, V_in, S_in, pooled, weight, owner, index, meta,
    svf_ref, out_ref, Hn, H, S, V, Vn, R, Z, Y, O, acc, rise, sems,
):
    pairs = [(own.at[:, cols(j)], Hn.at[1 + j, pl.ds(128, 256)]) for j in range(8)]
    pairs += [(west, Hn.at[0, pl.ds(128, 256)]), (east, Hn.at[9, pl.ds(128, 256)])]
    pairs += [(north.at[:, cols(j)], Hn.at[j, pl.ds(0, 128)]) for j in range(10)]
    pairs += [(south.at[:, cols(j)], Hn.at[j, pl.ds(384, 128)]) for j in range(10)]
    copies(pairs, sems)

    @pl.when(lat[0] == 0)
    def _():
        for c in range(10):
            Hn[c, 0:128, :] = jnp.broadcast_to(Hn[c, 128:129, :], (128, 128))

    @pl.when(lat[0] == lat[1] - 1)
    def _():
        for c in range(10):
            Hn[c, 384:512, :] = jnp.broadcast_to(Hn[c, 383:384, :], (128, 128))

    for c in range(10):
        for p in range(8):
            H[c, p] = Hn[c, pl.ds(p, 64, stride=8), :]
    S[...] = jnp.zeros(S.shape, F32)

    def step(it, carry):
        left, up, right = plane_rays(H, it, 128, slanted(it >= 4), inv_base, V_in, V, S)
        groups = ((left, up), (right,))
        for n, g in enumerate(groups):
            march(lags, inv_lags, g, rise.at[n])
        for n, g in enumerate(groups):
            finish(g, rise.at[n])
        return carry

    lax.fori_loop(0, 8, step, 0)
    svf_rows = []
    for j in range(8):
        rows = V[j, 0]
        for p in range(8):
            Vn[j, pl.ds(p, 32, stride=8), :] = V[j, p] * (1.0 / AZ)
            rows = rows if p == 0 else rows + V[j, p]
        svf_rows.append(rows)
    written = [pltpu.make_async_copy(Vn.at[j], svf_ref.at[:, cols(j)], sems.at[30 + j]) for j in range(8)]
    for c in written:
        c.start()

    total = jnp.zeros((224, 128), F32)
    for j in range(8):
        pool = (iota((128, 128), 1) == j * 16 + lax.shift_right_logical(iota((128, 128), 0), 3)).astype(BF16)
        field = []
        for rc in range(4):
            south, north_ = (S_in, S) if rc < 2 else (S, S_in)
            field += [south[rc, 2, j], south[rc, 1, j], south[rc, 0, j], north_[rc, 0, j], north_[rc, 1, j], north_[rc, 2, j]]
            field.append(svf_rows[j][rc * 8 : rc * 8 + 8, :])
        hi, lo = split2(jnp.concatenate(field, axis=0))
        total = total + jnp.dot(hi, pool, preferred_element_type=F32) + jnp.dot(lo, pool, preferred_element_type=F32)
    for rc in range(4):
        part = [total[rc * 56 + 8 * i : rc * 56 + 8 * i + 8] for i in range(7)]
        flat = [pooled[f, rc * 8 : rc * 8 + 8, :] for f in range(2)]
        R[rc * 72 : rc * 72 + 72, :] = jnp.concatenate([flat[0]] + part[:3] + [flat[1]] + part[3:], axis=0)
    lane = iota((8, 128), 1)
    scale = 1.0 / 4096.0
    for rc in range(4):
        for i in range(8):
            b = rc * 8 + i
            Y[b] = R[pl.ds(rc * 72 + i, 8, stride=8), :] * (weight[b : b + 1, :].astype(F32) * scale)
        O[rc * 8 : rc * 8 + 8, :] = R[rc * 72 + 64 : rc * 72 + 72, :] * (weight[rc * 8 : rc * 8 + 8, :].astype(F32) * (scale / AZ))

    acc[...] = jnp.zeros(acc.shape, F32)
    low = iota((256, 512), 0).astype(F32).astype(BF16)
    zero = jnp.zeros((16, 512), BF16)
    none = jnp.zeros((64, 512), BF16)

    def wide(v, row, height):
        v = jnp.concatenate([v[pl.ds(row + i, 1), :] for i in range(4)], axis=1)
        return jnp.broadcast_to(v.astype(F32), (height, 512))

    def sort(g, carry):
        b = g * 4
        v = jnp.concatenate([Y[b + i] for i in range(4)], axis=1)
        v = jnp.concatenate(split2(v), axis=0)
        tile = wide(index, b, 16).astype(BF16)
        left = [jnp.where(tile == BF16(t), v, zero) for t in range(NBR // 2)]
        hot = (low == wide(index, 32 + b, 256).astype(BF16)).astype(BF16)
        acc[0:256, :] += lax.dot_general(jnp.concatenate(left, axis=0), hot, NT, preferred_element_type=F32)
        o_hi, o_lo = split2(wide(O, b, 64))
        mine = low[:64] == jnp.floor(wide(owner, b, 64) * 0.5).astype(BF16)
        hot = (low == wide(index, 64 + b, 256).astype(BF16)).astype(BF16)
        left = [jnp.where(mine, o_hi, none), jnp.where(mine, o_lo, none)]
        acc[256:384, :] += lax.dot_general(jnp.concatenate(left, axis=0), hot, NT, preferred_element_type=F32)
        return carry

    lax.fori_loop(0, NBR // 4, sort, 0, unroll=4)
    for t in range(NBR):
        r, c = t // 2 * 16, t % 2 * 128
        Z[t] = acc[r : r + 8, c : c + 128] + acc[r + 8 : r + 16, c : c + 128]
    Z[32] = jnp.zeros((8, 128), F32)
    Z[33] = jnp.zeros((8, 128), F32)
    for odd in range(2):
        c = odd * 128
        out_ref[pl.ds(8 + 11 * odd, 64, stride=22), :] = acc[256:320, c : c + 128] + acc[320:384, c : c + 128]
    out_ref[pl.ds(9, N_DEV, stride=11), :] = meta[0]
    out_ref[pl.ds(10, N_DEV, stride=11), :] = meta[1]

    def expand(g, carry):
        owners = [g * 16 + i for i in range(16)]
        st = [starts[0, o] for o in owners]
        tile = [lax.shift_right_logical(s, 7) for s in st]
        q = [128 - lax.bitwise_and(s, 127) for s in st]
        a = [pltpu.roll(Z[t], lax.bitwise_and(n, 127), 1) for t, n in zip(tile, q)]
        b = [pltpu.roll(Z[t + 1], lax.bitwise_and(n, 127), 1) for t, n in zip(tile, q)]
        got = [jnp.where(lane < n, u, w) for n, u, w in zip(q, a, b)]
        for o, v in zip(owners, got):
            out_ref[pl.ds(o * 11, 8), :] = v
        return carry

    lax.fori_loop(0, N_DEV // 16, expand, 0)
    for c in written:
        c.wait()


def outer(*args):
    return pl.pallas_call(
        outer_kernel,
        name="outer",
        out_shape=(jax.ShapeDtypeStruct((256, 1024), F32), jax.ShapeDtypeStruct((N_DEV * 11, 128), F32)),
        in_specs=[SMEM] * 4 + [ANY] * 5 + [VMEM] * 8,
        out_specs=[ANY, VMEM],
        scratch_shapes=[
            pltpu.VMEM((10, 512, 128), F32),
            pltpu.VMEM((10, 8, 64, 128), F32),
            pltpu.VMEM((4, 3, 8, 8, 128), F32),
            pltpu.VMEM((8, 8, 32, 128), F32),
            pltpu.VMEM((8, 256, 128), F32),
            pltpu.VMEM((288, 128), F32),
            pltpu.VMEM((34, 8, 128), F32),
            pltpu.VMEM((32, 8, 128), F32),
            pltpu.VMEM((32, 128), F32),
            pltpu.VMEM((384, 256), F32),
            pltpu.VMEM((2, 2, 4, 8, 8, 128), F32),
            pltpu.SemaphoreType.DMA((38,)),
        ],
        compiler_params=pltpu.CompilerParams(vmem_limit_bytes=32 * 1024 * 1024),
        cost_estimate=pl.CostEstimate(flops=int(4e8), bytes_accessed=20000000, transcendentals=0),
    )(*args)


def cells_kernel(got_ref, horizon_ref, svf_ref):
    low = iota((128, 512), 0).astype(F32).astype(BF16)

    def accumulate(t, acc):
        first = jnp.concatenate([got_ref[pl.ds(t * 44 + 11 * i, 8), :] for i in range(4)], axis=1)
        second = jnp.concatenate([got_ref[pl.ds(t * 44 + 11 * i + 3, 8), :] for i in range(4)], axis=1)
        hi, lo = split2(jnp.concatenate([first, second], axis=0))
        cell = second[6:7, :] - 1.0
        upper = jnp.floor(cell * (1.0 / 128.0))
        high = jnp.broadcast_to(upper, (16, 512)).astype(BF16)
        zero = jnp.zeros((16, 512), BF16)
        left = []
        for h in range(4):
            mine = high == BF16(h)
            left += [jnp.where(mine, hi, zero), jnp.where(mine, lo, zero)]
        hot = (low == jnp.broadcast_to(cell - 128.0 * upper, (128, 512)).astype(BF16)).astype(BF16)
        return acc + lax.dot_general(jnp.concatenate(left, axis=0), hot, NT, preferred_element_type=F32)

    acc = lax.fori_loop(0, N_DEV // 4, accumulate, jnp.zeros((128, 128), F32), unroll=8)
    sums = jnp.concatenate([acc[h * 32 : h * 32 + 16] + acc[h * 32 + 16 : h * 32 + 32] for h in range(4)], axis=1)
    area = jnp.maximum(sums[15:16, :] * (1.0 / 64.0), 1.0)
    horizon_ref[...] = sums[0:8] / area
    svf_ref[...] = sums[13:14] / area


def cells(got):
    return pl.pallas_call(
        cells_kernel,
        name="cells",
        out_shape=(jax.ShapeDtypeStruct((AZ, CELLS_DEV), F32), jax.ShapeDtypeStruct((1, CELLS_DEV), F32)),
        in_specs=[VMEM],
        out_specs=[VMEM] * 2,
        compiler_params=pltpu.CompilerParams(vmem_limit_bytes=24 * 1024 * 1024),
    )(got)


def shards(terrain_surface, azimuth_lag_tallies, holder_devices, holder_region_slot, footprint_weight):
    rows, width = terrain_surface.shape
    n_lat = lax.axis_size("lat")
    n_lon = lax.axis_size("lon")
    W = FARTHEST_LAG
    own = terrain_surface
    east_pairs = [((i + 1) % n_lon, i) for i in range(n_lon)]
    west = lax.ppermute(own[:, width - W :], "lon", [(j, i) for i, j in east_pairs])
    east = lax.ppermute(own[:, :W], "lon", east_pairs)
    weight = footprint_weight.reshape(NBR, 128)
    owner = holder_devices.reshape(NBR, 128)
    start, index, meta = route(owner, holder_region_slot.reshape(NBR, 128), weight)
    west, east, start, index, meta = lax.optimization_barrier((west, east, start, index, meta))
    wide = jnp.concatenate([west, own, east], axis=1)
    down = [(i, i + 1) for i in range(n_lat - 1)]
    north = lax.ppermute(wide[rows - W :], "lat", down)
    south = lax.ppermute(wide[:W], "lat", [(j, i) for i, j in down])

    rows_global = (lax.axis_index("lat") * rows + jnp.arange(rows, dtype=jnp.int32)).astype(F32)
    latitude = 47.0 - (rows_global + 0.5) / 1200.0
    coslat = jnp.cos(latitude * jnp.pi / 180.0)
    across = (pixel_size * coslat) ** 2
    inv_row = (1.0 / jnp.sqrt(across)).reshape(2, 128)
    inv_base = 1.0 / jnp.sqrt(pixel_size**2 + across)
    inv_base = jnp.broadcast_to(inv_base.reshape(32, 8).T[:, :, None], (8, 32, 128))
    lat = jnp.stack([lax.axis_index("lat").astype(jnp.int32), jnp.int32(n_lat)])
    inv_lags = 1.0 / azimuth_lag_tallies.astype(F32)
    part, sums, pooled = inner(azimuth_lag_tallies, inv_lags, own, west, east, inv_base, inv_row)
    fine_svf, packed = outer(
        azimuth_lag_tallies, inv_lags, start, lat, own, north, south, west, east, inv_base, part, sums, pooled,
        weight, owner, index, meta,
    )
    packed = packed.reshape(N_DEV, 1, 11 * 128)
    got = lax.all_to_all(packed, ("lat", "lon"), split_axis=0, concat_axis=0, tiled=True)
    got = got.reshape(N_DEV * 11, 128)
    cell_horizon, cell_svf = cells(got)
    return fine_svf, cell_horizon, cell_svf.reshape(CELLS_DEV)


def solution(mesh):
    P = jax.sharding.PartitionSpec
    in_specs = (P("lat", "lon"), P(), P(("lat", "lon"), None), P(("lat", "lon")), P(("lat", "lon")))
    out_specs = (P("lat", "lon"), P(None, ("lat", "lon")), P(("lat", "lon")))
    return jax.shard_map(shards, mesh=mesh, in_specs=in_specs, out_specs=out_specs, check_vma=False)
```

```python
import jax
import jax.numpy as jnp
from jax import lax
from jax.experimental import pallas as pl
from jax.experimental.pallas import tpu as pltpu

FARTHEST_LAG = 128
AZ = 8
KS = 8
pixel_size = 92.6
ATAN = (0.9999999, -0.33331991, 0.19969724, -0.14019481, 0.09914293, -0.05948639, 0.0242524, -0.00469327)
HALF_PI = 1.5707963267948966


def recip(v):
    return pl.reciprocal(v, approx=True)


def angle(x, y):
    ax, ay = jnp.abs(x), jnp.abs(y)
    z = jnp.minimum(ax, ay) * recip(jnp.maximum(ax, ay))
    u = z * z
    p = ATAN[7]
    for c in ATAN[6::-1]:
        p = p * u + c
    p = p * z
    p = jnp.where(ay > ax, HALF_PI - p, p)
    p = jnp.where(x < 0.0, 2.0 * HALF_PI - p, p)
    return jnp.where(y < 0.0, 4.0 * HALF_PI - p, p)


N_DEV = 128
NBR = 32
CELLS_DEV = 512
F32 = jnp.float32
BF16 = jnp.bfloat16
VMEM = pl.BlockSpec(memory_space=pltpu.VMEM)
SMEM = pl.BlockSpec(memory_space=pltpu.SMEM)
ANY = pl.BlockSpec(memory_space=pl.ANY)
NT = (((1,), (1,)), ((), ()))


def split2(v):
    hi = v.astype(BF16)
    return hi, (v - hi.astype(F32)).astype(BF16)


def iota(shape, dim):
    return lax.broadcasted_iota(jnp.int32, shape, dim)


def route_kernel(owner_ref, slot_ref, weight_ref, start_ref, index_ref, meta_ref, rank_ref):
    sub = iota((N_DEV, 128), 0)
    upper = (iota((128, 128), 0) < iota((128, 128), 1)).astype(BF16)
    right = jnp.concatenate([upper, jnp.ones((128, 128), BF16)], axis=1)
    count = jnp.zeros((N_DEV, 128), F32)
    for i in range(NBR):
        mine = sub == owner_ref[i : i + 1, :]
        both = jnp.dot(mine.astype(BF16), right, preferred_element_type=F32)
        rank = jnp.sum(jnp.where(mine, both[:, :128] + count, 0.0), axis=0, keepdims=True)
        rank_ref[i : i + 1, :] = rank
        count = count + both[:, 128:]
    lower = (iota((128, 128), 0) > iota((128, 128), 1)).astype(BF16)
    start = jnp.dot(lower, count.astype(BF16), preferred_element_type=F32)
    start_row = lax.dot_general(count[:, :8].T.astype(BF16), upper, (((1,), (0,)), ((), ())), preferred_element_type=F32)
    start_ref[...] = start_row[:1].astype(jnp.int32)
    meta = jnp.zeros((3 * N_DEV, 128), F32)
    for i in range(NBR):
        mine = sub == owner_ref[i : i + 1, :]
        rank = rank_ref[i : i + 1, :]
        place = (rank + jnp.sum(jnp.where(mine, start, 0.0), axis=0, keepdims=True)).astype(jnp.int32)
        rank = rank.astype(jnp.int32)
        index_ref[i : i + 1, :] = lax.shift_right_logical(place, 8)
        index_ref[NBR + i : NBR + i + 1, :] = lax.bitwise_and(place, 255)
        odd = lax.bitwise_and(owner_ref[i : i + 1, :], 1) * 128
        index_ref[2 * NBR + i : 2 * NBR + i + 1, :] = rank + odd
        rank_hot = (sub == rank).astype(BF16)
        slot = slot_ref[i : i + 1, :] + 1
        parts = (lax.shift_right_logical(slot, 4), lax.bitwise_and(slot, 15), weight_ref[i : i + 1, :])
        left = jnp.concatenate([jnp.where(mine, v.astype(F32), 0.0) for v in parts], axis=0).astype(BF16)
        meta = meta + lax.dot_general(left, rank_hot, NT, preferred_element_type=F32)
    meta_ref[0] = meta[:N_DEV] * 16.0 + meta[N_DEV : 2 * N_DEV]
    meta_ref[1] = meta[2 * N_DEV :]


def route(owner, slot, weight):
    return pl.pallas_call(
        route_kernel,
        name="route",
        out_shape=(
            jax.ShapeDtypeStruct((1, N_DEV), jnp.int32),
            jax.ShapeDtypeStruct((96, 128), jnp.int32),
            jax.ShapeDtypeStruct((2, N_DEV, 128), F32),
        ),
        in_specs=[VMEM] * 3,
        out_specs=[VMEM] * 3,
        scratch_shapes=[pltpu.VMEM((NBR, 128), F32)],
        cost_estimate=pl.CostEstimate(flops=int(4e8), bytes_accessed=200000, transcendentals=0),
    )(owner, slot, weight)


def quad(r):
    x0, y0 = 1.0 - r[0] * r[1], r[0] + r[1]
    x1, y1 = 1.0 - r[2] * r[3], r[2] + r[3]
    return angle(x0 * x1 - y0 * y1, x0 * y1 + x1 * y0)


class Ray:
    def __init__(self, azimuth, near, far, inv_base, opening, put):
        self.azimuth, self.near, self.far = azimuth, near, far
        self.inv_base, self.opening, self.put = inv_base, opening, put


def plane_rays(tile, it, h0, rays, inv_base, V_old, V, S_ref):
    lane = iota((8, 128), 1)
    rc = lax.shift_right_logical(it, 1)
    p0 = lax.bitwise_and(it, 1) * 4
    block = pl.ds(pl.multiple_of(rc * 8, 8), 8)
    made = []
    for f, (a, sy, sx) in enumerate(rays):
        off = 1 if sx >= 0 else 0
        count = 8 if sx == 0 else 9

        def near(p):
            rows = pl.ds(pl.multiple_of(h0 // 8 + rc * 8, 8), 8)
            return [tile(1 + j, p0 + p, rows) for j in range(8)]

        def far(p, s, sy=sy, sx=sx, off=off, count=count):
            y = h0 + rc * 64 + p0 + p + sy * s
            plane, i0 = lax.bitwise_and(y, 7), lax.shift_right_logical(y, 3)
            tiles = [tile(off + j, plane, pl.ds(i0, 8)) for j in range(count)]
            if sx == 0:
                return tiles
            amount = 128 - s if sx == 1 else lax.bitwise_and(s, 127)
            keep = lane < (amount if sx == 1 else s)
            rolled = [pltpu.roll(v, amount, 1) for v in tiles]
            return [jnp.where(keep, rolled[j], rolled[j + 1]) for j in range(8)]

        def base(p, sx=sx):
            return 1.0 / pixel_size if sx == 0 else inv_base[p0 + p, block, :]

        def opening(p, j, v, f=f):
            old = V_old if f == 0 else V
            at = (j, p0 + p, block)
            V[at] = v if old is None else old[at] + v

        def put(j, v, f=f):
            S_ref[rc, f, j] += v

        made.append(Ray(a, near, far, base, opening, put))
    return made


def turned_ray(T, first, it, facing, inv_row, V_old, V, S_ref):
    rt = lax.shift_right_logical(it, 2)
    half = lax.bitwise_and(lax.shift_right_logical(it, 1), 1)
    p0 = lax.bitwise_and(it, 1) * 4
    west = lax.bitwise_xor(half, facing)
    sx = 1 - 2 * west

    def rows(j):
        return pl.ds(pl.multiple_of(half * 64 + 8 * j, 8), 8)

    def near(p):
        return [T[rt, p0 + p, pl.ds(pl.multiple_of(first + half * 64 + 8 * j, 8), 8), :] for j in range(8)]

    def far(p, s):
        x = 8 * first + half * 512 + p0 + p + sx * s
        plane, i0 = lax.bitwise_and(x, 7), lax.shift_right_logical(x, 3)
        return [T[rt, plane, pl.ds(i0 + 8 * j, 8), :] for j in range(8)]

    def base(p):
        return jnp.broadcast_to(inv_row[pl.ds(rt, 1), :], (8, 128))

    def opening(p, j, v):
        at = (rt, p0 + p, rows(j))
        V[at] = v if V_old is None else V_old[at] + v

    def put(j, v):
        S_ref[rt, rows(j), :] += v

    return Ray(4 * west, near, far, base, opening, put)


def march(lags, inv_lags, group, rise):
    for p in range(4):
        t = [ray.near(p) for ray in group]
        best = [[None] * 8 for ray in group]
        for k in range(KS):
            for i, ray in enumerate(group):
                inv_lag = inv_lags[ray.azimuth, k]
                got = ray.far(p, lags[ray.azimuth, k])
                for j in range(8):
                    v = (got[j] - t[i][j]) * inv_lag
                    best[i][j] = v if k == 0 else jnp.maximum(best[i][j], v)
        for i, ray in enumerate(group):
            ib = ray.inv_base(p)
            for j in range(8):
                rise[i, p, j] = jnp.minimum(jnp.maximum(best[i][j] * ib, 0.0), 1e8)


def finish(group, rise):
    for i, ray in enumerate(group):
        for j in range(8):
            r = [rise[i, p, j] for p in range(4)]
            for p in range(4):
                ray.opening(p, j, recip(1.0 + r[p] * r[p]))
            ray.put(j, quad(r))


def slanted(southward):
    sy = jnp.where(southward, 1, -1)
    return [(jnp.where(southward, 3, 5), sy, -1), (jnp.where(southward, 2, 6), sy, 0), (jnp.where(southward, 1, 7), sy, 1)]


def copies(pairs, sems):
    made = [pltpu.make_async_copy(a, b, sems.at[i]) for i, (a, b) in enumerate(pairs)]
    for c in made:
        c.start()
    for c in made:
        c.wait()


def cols(j):
    return pl.ds(j * 128, 128)


def first_kernel(lags, inv_lags, own, inv_row, H, T, V, S_ref, VT, ST, Hn, Tn, rise, sems):
    copies([(own.at[:, cols(j)], Hn.at[j]) for j in range(8)], sems)
    for c in range(8):
        for p in range(8):
            H[c, p] = Hn[c, pl.ds(p, 32, stride=8), :]
        for rt in range(2):
            Tn[rt, c * 128 : (c + 1) * 128, :] = Hn[c, rt * 128 : (rt + 1) * 128, :].T
    for rt in range(2):
        for p in range(8):
            T[rt, p] = Tn[rt, pl.ds(p, 128, stride=8), :]
    S_ref[...] = jnp.zeros(S_ref.shape, F32)
    ST[...] = jnp.zeros(ST.shape, F32)

    def tile(c, p, rows):
        return H[c - 1, p, rows, :]

    def step(it, carry):
        up = plane_rays(tile, it, 0, slanted(it < 4)[1:2], None, None, V, S_ref)
        group = up + [turned_ray(T, 0, it, 0, inv_row, None, VT, ST)]
        march(lags, inv_lags, group, rise)
        finish(group, rise)
        return carry

    lax.fori_loop(0, 8, step, 0)


def first(*args):
    return pl.pallas_call(
        first_kernel,
        name="first",
        out_shape=(
            jax.ShapeDtypeStruct((8, 8, 32, 128), F32),
            jax.ShapeDtypeStruct((2, 8, 128, 128), F32),
            jax.ShapeDtypeStruct((8, 8, 32, 128), F32),
            jax.ShapeDtypeStruct((4, 1, 8, 8, 128), F32),
            jax.ShapeDtypeStruct((2, 8, 128, 128), F32),
            jax.ShapeDtypeStruct((2, 128, 128), F32),
        ),
        in_specs=[SMEM] * 2 + [ANY, VMEM],
        out_specs=[VMEM] * 6,
        scratch_shapes=[
            pltpu.VMEM((8, 256, 128), F32),
            pltpu.VMEM((2, 1024, 128), F32),
            pltpu.VMEM((2, 4, 8, 8, 128), F32),
            pltpu.SemaphoreType.DMA((8,)),
        ],
        compiler_params=pltpu.CompilerParams(vmem_limit_bytes=24 * 1024 * 1024),
        cost_estimate=pl.CostEstimate(flops=int(1e8), bytes_accessed=10000000, transcendentals=0),
    )(*args)


def inner_kernel(
    lags, inv_lags, west, east, inv_base, inv_row, H, T_own, V_old, VT_old, ST_old,
    V_ref, S_ref, pooled_ref, E, Tn, T, VT, ST, X, Xn, rise, sems,
):
    own = pltpu.make_async_copy(T_own, T.at[:, :, pl.ds(16, 128)], sems.at[0])
    own.start()
    for side, edge in enumerate((west, east)):
        for p in range(8):
            E[side, p] = edge[pl.ds(p, 32, stride=8), :]
        for rt in range(2):
            Tn[side, rt] = edge[rt * 128 : (rt + 1) * 128, :].T
            for p in range(8):
                T[rt, p, 144 * side : 144 * side + 16, :] = Tn[side, rt, pl.ds(p, 16, stride=8), :]
    S_ref[...] = jnp.zeros(S_ref.shape, F32)
    ST[...] = jnp.zeros(ST.shape, F32)
    own.wait()

    def tile(c, p, rows):
        return H[c - 1, p, rows, :] if 1 <= c <= 8 else E[c // 9, p, rows, :]

    def step(it, carry):
        left, right = plane_rays(tile, it, 0, slanted(it < 4)[::2], inv_base, V_old, V_ref, S_ref)
        groups = ((left, turned_ray(T, 16, it, 1, inv_row, VT_old, VT, ST)), (right,))
        for n, g in enumerate(groups):
            march(lags, inv_lags, g, rise.at[n])
        for n, g in enumerate(groups):
            finish(g, rise.at[n])
        return carry

    lax.fori_loop(0, 8, step, 0)
    pool = (iota((16, 128), 0) == lax.shift_right_logical(iota((16, 128), 1), 3)).astype(BF16)
    for rt in range(2):
        for f, (lower, upper) in enumerate(((ST_old, ST), (ST, ST_old))):
            hi, lo = split2(jnp.concatenate([lower[rt, 0:64, :], upper[rt, 64:128, :]], axis=0))
            total = lax.dot_general(pool, hi, NT, preferred_element_type=F32)
            pooled_ref[f, rt * 16 : rt * 16 + 16, :] = total + lax.dot_general(pool, lo, NT, preferred_element_type=F32)
        for c in range(8):
            for p in range(8):
                X[rt, c, pl.ds(p, 16, stride=8), :] = VT[rt, p, c * 16 : (c + 1) * 16, :]
    for rt in range(2):
        for c in range(8):
            Xn[rt, c] = X[rt, c].T
    for rt in range(2):
        for c in range(8):
            for p in range(8):
                V_ref[c, p, rt * 16 : rt * 16 + 16, :] += Xn[rt, c, pl.ds(p, 16, stride=8), :]


def inner(*args):
    return pl.pallas_call(
        inner_kernel,
        name="inner",
        out_shape=(
            jax.ShapeDtypeStruct((8, 8, 32, 128), F32),
            jax.ShapeDtypeStruct((4, 2, 8, 8, 128), F32),
            jax.ShapeDtypeStruct((2, NBR, 128), F32),
        ),
        in_specs=[SMEM] * 2 + [VMEM] * 9,
        out_specs=[VMEM] * 3,
        scratch_shapes=[
            pltpu.VMEM((2, 8, 32, 128), F32),
            pltpu.VMEM((2, 2, 128, 128), F32),
            pltpu.VMEM((2, 8, 160, 128), F32),
            pltpu.VMEM((2, 8, 128, 128), F32),
            pltpu.VMEM((2, 128, 128), F32),
            pltpu.VMEM((2, 8, 128, 128), F32),
            pltpu.VMEM((2, 8, 128, 128), F32),
            pltpu.VMEM((2, 2, 4, 8, 8, 128), F32),
            pltpu.SemaphoreType.DMA((1,)),
        ],
        compiler_params=pltpu.CompilerParams(vmem_limit_bytes=32 * 1024 * 1024),
        cost_estimate=pl.CostEstimate(flops=int(4e8), bytes_accessed=30000000, transcendentals=0),
    )(*args)


def outer_kernel(
    lags, inv_lags, starts, lat, own, north, south, west, east, inv_base, V_in, S_in, S_up, pooled, weight, owner, index, meta,
    svf_ref, out_ref, Hn, H, S, V, Vn, R, Z, Y, O, acc, rise, sems,
):
    pairs = [(own.at[:, cols(j)], Hn.at[1 + j, pl.ds(128, 256)]) for j in range(8)]
    pairs += [(west, Hn.at[0, pl.ds(128, 256)]), (east, Hn.at[9, pl.ds(128, 256)])]
    pairs += [(north.at[:, cols(j)], Hn.at[j, pl.ds(0, 128)]) for j in range(10)]
    pairs += [(south.at[:, cols(j)], Hn.at[j, pl.ds(384, 128)]) for j in range(10)]
    copies(pairs, sems)

    @pl.when(lat[0] == 0)
    def _():
        for c in range(10):
            Hn[c, 0:128, :] = jnp.broadcast_to(Hn[c, 128:129, :], (128, 128))

    @pl.when(lat[0] == lat[1] - 1)
    def _():
        for c in range(10):
            Hn[c, 384:512, :] = jnp.broadcast_to(Hn[c, 383:384, :], (128, 128))

    for c in range(10):
        for p in range(8):
            H[c, p] = Hn[c, pl.ds(p, 64, stride=8), :]
    S[...] = jnp.zeros(S.shape, F32)

    def tile(c, p, rows):
        return H[c, p, rows, :]

    def step(it, carry):
        left, up, right = plane_rays(tile, it, 128, slanted(it >= 4), inv_base, V_in, V, S)
        groups = ((left, up), (right,))
        for n, g in enumerate(groups):
            march(lags, inv_lags, g, rise.at[n])
        for n, g in enumerate(groups):
            finish(g, rise.at[n])
        return carry

    lax.fori_loop(0, 8, step, 0)
    svf_rows = []
    for j in range(8):
        rows = V[j, 0]
        for p in range(8):
            Vn[j, pl.ds(p, 32, stride=8), :] = V[j, p] * (1.0 / AZ)
            rows = rows if p == 0 else rows + V[j, p]
        svf_rows.append(rows)
    written = [pltpu.make_async_copy(Vn.at[j], svf_ref.at[:, cols(j)], sems.at[30 + j]) for j in range(8)]
    for c in written:
        c.start()

    total = jnp.zeros((224, 128), F32)
    for j in range(8):
        pool = (iota((128, 128), 1) == j * 16 + lax.shift_right_logical(iota((128, 128), 0), 3)).astype(BF16)
        field = []
        for rc in range(4):
            near = [S_in[rc, 0, j], S_up[rc, 0, j], S_in[rc, 1, j]]
            away = [S[rc, f, j] for f in range(3)]
            field += near[::-1] + away if rc < 2 else away[::-1] + near
            field.append(svf_rows[j][rc * 8 : rc * 8 + 8, :])
        hi, lo = split2(jnp.concatenate(field, axis=0))
        total = total + jnp.dot(hi, pool, preferred_element_type=F32) + jnp.dot(lo, pool, preferred_element_type=F32)
    for rc in range(4):
        part = [total[rc * 56 + 8 * i : rc * 56 + 8 * i + 8] for i in range(7)]
        flat = [pooled[f, rc * 8 : rc * 8 + 8, :] for f in range(2)]
        R[rc * 72 : rc * 72 + 72, :] = jnp.concatenate([flat[0]] + part[:3] + [flat[1]] + part[3:], axis=0)
    lane = iota((8, 128), 1)
    scale = 1.0 / 4096.0
    for rc in range(4):
        for i in range(8):
            b = rc * 8 + i
            Y[b] = R[pl.ds(rc * 72 + i, 8, stride=8), :] * (weight[b : b + 1, :].astype(F32) * scale)
        O[rc * 8 : rc * 8 + 8, :] = R[rc * 72 + 64 : rc * 72 + 72, :] * (weight[rc * 8 : rc * 8 + 8, :].astype(F32) * (scale / AZ))

    acc[...] = jnp.zeros(acc.shape, F32)
    low = iota((256, 512), 0).astype(F32).astype(BF16)
    zero = jnp.zeros((16, 512), BF16)
    none = jnp.zeros((64, 512), BF16)

    def wide(v, row, height):
        v = jnp.concatenate([v[pl.ds(row + i, 1), :] for i in range(4)], axis=1)
        return jnp.broadcast_to(v.astype(F32), (height, 512))

    def sort(g, carry):
        b = g * 4
        v = jnp.concatenate([Y[b + i] for i in range(4)], axis=1)
        v = jnp.concatenate(split2(v), axis=0)
        tile = wide(index, b, 16).astype(BF16)
        left = [jnp.where(tile == BF16(t), v, zero) for t in range(NBR // 2)]
        hot = (low == wide(index, 32 + b, 256).astype(BF16)).astype(BF16)
        acc[0:256, :] += lax.dot_general(jnp.concatenate(left, axis=0), hot, NT, preferred_element_type=F32)
        o_hi, o_lo = split2(wide(O, b, 64))
        mine = low[:64] == jnp.floor(wide(owner, b, 64) * 0.5).astype(BF16)
        hot = (low == wide(index, 64 + b, 256).astype(BF16)).astype(BF16)
        left = [jnp.where(mine, o_hi, none), jnp.where(mine, o_lo, none)]
        acc[256:384, :] += lax.dot_general(jnp.concatenate(left, axis=0), hot, NT, preferred_element_type=F32)
        return carry

    lax.fori_loop(0, NBR // 4, sort, 0, unroll=4)
    for t in range(NBR):
        r, c = t // 2 * 16, t % 2 * 128
        Z[t] = acc[r : r + 8, c : c + 128] + acc[r + 8 : r + 16, c : c + 128]
    Z[32] = jnp.zeros((8, 128), F32)
    Z[33] = jnp.zeros((8, 128), F32)
    for odd in range(2):
        c = odd * 128
        out_ref[pl.ds(8 + 11 * odd, 64, stride=22), :] = acc[256:320, c : c + 128] + acc[320:384, c : c + 128]
    out_ref[pl.ds(9, N_DEV, stride=11), :] = meta[0]
    out_ref[pl.ds(10, N_DEV, stride=11), :] = meta[1]

    def expand(g, carry):
        owners = [g * 16 + i for i in range(16)]
        st = [starts[0, o] for o in owners]
        tile = [lax.shift_right_logical(s, 7) for s in st]
        q = [128 - lax.bitwise_and(s, 127) for s in st]
        a = [pltpu.roll(Z[t], lax.bitwise_and(n, 127), 1) for t, n in zip(tile, q)]
        b = [pltpu.roll(Z[t + 1], lax.bitwise_and(n, 127), 1) for t, n in zip(tile, q)]
        got = [jnp.where(lane < n, u, w) for n, u, w in zip(q, a, b)]
        for o, v in zip(owners, got):
            out_ref[pl.ds(o * 11, 8), :] = v
        return carry

    lax.fori_loop(0, N_DEV // 16, expand, 0)
    for c in written:
        c.wait()


def outer(*args):
    return pl.pallas_call(
        outer_kernel,
        name="outer",
        out_shape=(jax.ShapeDtypeStruct((256, 1024), F32), jax.ShapeDtypeStruct((N_DEV * 11, 128), F32)),
        in_specs=[SMEM] * 4 + [ANY] * 5 + [VMEM] * 9,
        out_specs=[ANY, VMEM],
        scratch_shapes=[
            pltpu.VMEM((10, 512, 128), F32),
            pltpu.VMEM((10, 8, 64, 128), F32),
            pltpu.VMEM((4, 3, 8, 8, 128), F32),
            pltpu.VMEM((8, 8, 32, 128), F32),
            pltpu.VMEM((8, 256, 128), F32),
            pltpu.VMEM((288, 128), F32),
            pltpu.VMEM((34, 8, 128), F32),
            pltpu.VMEM((32, 8, 128), F32),
            pltpu.VMEM((32, 128), F32),
            pltpu.VMEM((384, 256), F32),
            pltpu.VMEM((2, 2, 4, 8, 8, 128), F32),
            pltpu.SemaphoreType.DMA((38,)),
        ],
        compiler_params=pltpu.CompilerParams(vmem_limit_bytes=32 * 1024 * 1024),
        cost_estimate=pl.CostEstimate(flops=int(4e8), bytes_accessed=20000000, transcendentals=0),
    )(*args)


def cells_kernel(got_ref, horizon_ref, svf_ref):
    low = iota((128, 512), 0).astype(F32).astype(BF16)

    def accumulate(t, acc):
        first = jnp.concatenate([got_ref[pl.ds(t * 44 + 11 * i, 8), :] for i in range(4)], axis=1)
        second = jnp.concatenate([got_ref[pl.ds(t * 44 + 11 * i + 3, 8), :] for i in range(4)], axis=1)
        hi, lo = split2(jnp.concatenate([first, second], axis=0))
        cell = second[6:7, :] - 1.0
        upper = jnp.floor(cell * (1.0 / 128.0))
        high = jnp.broadcast_to(upper, (16, 512)).astype(BF16)
        zero = jnp.zeros((16, 512), BF16)
        left = []
        for h in range(4):
            mine = high == BF16(h)
            left += [jnp.where(mine, hi, zero), jnp.where(mine, lo, zero)]
        hot = (low == jnp.broadcast_to(cell - 128.0 * upper, (128, 512)).astype(BF16)).astype(BF16)
        return acc + lax.dot_general(jnp.concatenate(left, axis=0), hot, NT, preferred_element_type=F32)

    acc = lax.fori_loop(0, N_DEV // 4, accumulate, jnp.zeros((128, 128), F32), unroll=8)
    sums = jnp.concatenate([acc[h * 32 : h * 32 + 16] + acc[h * 32 + 16 : h * 32 + 32] for h in range(4)], axis=1)
    area = jnp.maximum(sums[15:16, :] * (1.0 / 64.0), 1.0)
    horizon_ref[...] = sums[0:8] / area
    svf_ref[...] = sums[13:14] / area


def cells(got):
    return pl.pallas_call(
        cells_kernel,
        name="cells",
        out_shape=(jax.ShapeDtypeStruct((AZ, CELLS_DEV), F32), jax.ShapeDtypeStruct((1, CELLS_DEV), F32)),
        in_specs=[VMEM],
        out_specs=[VMEM] * 2,
        compiler_params=pltpu.CompilerParams(vmem_limit_bytes=24 * 1024 * 1024),
    )(got)


def shards(terrain_surface, azimuth_lag_tallies, holder_devices, holder_region_slot, footprint_weight):
    rows, width = terrain_surface.shape
    n_lat = lax.axis_size("lat")
    n_lon = lax.axis_size("lon")
    W = FARTHEST_LAG
    own = terrain_surface
    east_pairs = [((i + 1) % n_lon, i) for i in range(n_lon)]
    west = lax.ppermute(own[:, width - W :], "lon", [(j, i) for i, j in east_pairs])
    east = lax.ppermute(own[:, :W], "lon", east_pairs)
    weight = footprint_weight.reshape(NBR, 128)
    owner = holder_devices.reshape(NBR, 128)
    start, index, meta = route(owner, holder_region_slot.reshape(NBR, 128), weight)
    rows_global = (lax.axis_index("lat") * rows + jnp.arange(rows, dtype=jnp.int32)).astype(F32)
    latitude = 47.0 - (rows_global + 0.5) / 1200.0
    coslat = jnp.cos(latitude * jnp.pi / 180.0)
    across = (pixel_size * coslat) ** 2
    inv_row = (1.0 / jnp.sqrt(across)).reshape(2, 128)
    inv_lags = 1.0 / azimuth_lag_tallies.astype(F32)
    straight, turned, part, up, turned_part, turned_sums = first(azimuth_lag_tallies, inv_lags, own, inv_row)
    west, east, start, index, meta, part = lax.optimization_barrier((west, east, start, index, meta, part))
    wide = jnp.concatenate([west, own, east], axis=1)
    down = [(i, i + 1) for i in range(n_lat - 1)]
    north = lax.ppermute(wide[rows - W :], "lat", down)
    south = lax.ppermute(wide[:W], "lat", [(j, i) for i, j in down])

    inv_base = 1.0 / jnp.sqrt(pixel_size**2 + across)
    inv_base = jnp.broadcast_to(inv_base.reshape(32, 8).T[:, :, None], (8, 32, 128))
    lat = jnp.stack([lax.axis_index("lat").astype(jnp.int32), jnp.int32(n_lat)])
    part, sums, pooled = inner(
        azimuth_lag_tallies, inv_lags, west, east, inv_base, inv_row, straight, turned, part, turned_part, turned_sums
    )
    fine_svf, packed = outer(
        azimuth_lag_tallies, inv_lags, start, lat, own, north, south, west, east, inv_base, part, sums, up, pooled,
        weight, owner, index, meta,
    )
    packed = packed.reshape(N_DEV, 1, 11 * 128)
    got = lax.all_to_all(packed, ("lat", "lon"), split_axis=0, concat_axis=0, tiled=True)
    got = got.reshape(N_DEV * 11, 128)
    cell_horizon, cell_svf = cells(got)
    return fine_svf, cell_horizon, cell_svf.reshape(CELLS_DEV)


def solution(mesh):
    P = jax.sharding.PartitionSpec
    in_specs = (P("lat", "lon"), P(), P(("lat", "lon"), None), P(("lat", "lon")), P(("lat", "lon")))
    out_specs = (P("lat", "lon"), P(None, ("lat", "lon")), P(("lat", "lon")))
    return jax.shard_map(shards, mesh=mesh, in_specs=in_specs, out_specs=out_specs, check_vma=False)
```

```python
import jax
import jax.numpy as jnp
from jax import lax
from jax.experimental import pallas as pl
from jax.experimental.pallas import tpu as pltpu

FARTHEST_LAG = 128
AZ = 8
KS = 8
pixel_size = 92.6
ATAN = (0.9999999, -0.33331991, 0.19969724, -0.14019481, 0.09914293, -0.05948639, 0.0242524, -0.00469327)
HALF_PI = 1.5707963267948966


def recip(v):
    return pl.reciprocal(v, approx=True)


def angle(x, y):
    ax, ay = jnp.abs(x), jnp.abs(y)
    z = jnp.minimum(ax, ay) * recip(jnp.maximum(ax, ay))
    u = z * z
    p = ATAN[7]
    for c in ATAN[6::-1]:
        p = p * u + c
    p = p * z
    p = jnp.where(ay > ax, HALF_PI - p, p)
    p = jnp.where(x < 0.0, 2.0 * HALF_PI - p, p)
    return jnp.where(y < 0.0, 4.0 * HALF_PI - p, p)


N_DEV = 128
NBR = 32
CELLS_DEV = 512
F32 = jnp.float32
BF16 = jnp.bfloat16
VMEM = pl.BlockSpec(memory_space=pltpu.VMEM)
SMEM = pl.BlockSpec(memory_space=pltpu.SMEM)
ANY = pl.BlockSpec(memory_space=pl.ANY)
NT = (((1,), (1,)), ((), ()))


def split2(v):
    hi = v.astype(BF16)
    return hi, (v - hi.astype(F32)).astype(BF16)


def iota(shape, dim):
    return lax.broadcasted_iota(jnp.int32, shape, dim)


def route_kernel(owner_ref, slot_ref, weight_ref, start_ref, index_ref, meta_ref, rank_ref):
    sub = iota((N_DEV, 128), 0)
    upper = (iota((128, 128), 0) < iota((128, 128), 1)).astype(BF16)
    right = jnp.concatenate([upper, jnp.ones((128, 128), BF16)], axis=1)
    count = jnp.zeros((N_DEV, 128), F32)
    for i in range(NBR):
        mine = sub == owner_ref[i : i + 1, :]
        both = jnp.dot(mine.astype(BF16), right, preferred_element_type=F32)
        rank = jnp.sum(jnp.where(mine, both[:, :128] + count, 0.0), axis=0, keepdims=True)
        rank_ref[i : i + 1, :] = rank
        count = count + both[:, 128:]
    lower = (iota((128, 128), 0) > iota((128, 128), 1)).astype(BF16)
    start = jnp.dot(lower, count.astype(BF16), preferred_element_type=F32)
    start_row = lax.dot_general(count[:, :8].T.astype(BF16), upper, (((1,), (0,)), ((), ())), preferred_element_type=F32)
    start_ref[...] = start_row[:1].astype(jnp.int32)
    meta = jnp.zeros((3 * N_DEV, 128), F32)
    for i in range(NBR):
        mine = sub == owner_ref[i : i + 1, :]
        rank = rank_ref[i : i + 1, :]
        place = (rank + jnp.sum(jnp.where(mine, start, 0.0), axis=0, keepdims=True)).astype(jnp.int32)
        rank = rank.astype(jnp.int32)
        index_ref[i : i + 1, :] = lax.shift_right_logical(place, 8)
        index_ref[NBR + i : NBR + i + 1, :] = lax.bitwise_and(place, 255)
        odd = lax.bitwise_and(owner_ref[i : i + 1, :], 1) * 128
        index_ref[2 * NBR + i : 2 * NBR + i + 1, :] = rank + odd
        rank_hot = (sub == rank).astype(BF16)
        slot = slot_ref[i : i + 1, :] + 1
        parts = (lax.shift_right_logical(slot, 4), lax.bitwise_and(slot, 15), weight_ref[i : i + 1, :])
        left = jnp.concatenate([jnp.where(mine, v.astype(F32), 0.0) for v in parts], axis=0).astype(BF16)
        meta = meta + lax.dot_general(left, rank_hot, NT, preferred_element_type=F32)
    meta_ref[0] = meta[:N_DEV] * 16.0 + meta[N_DEV : 2 * N_DEV]
    meta_ref[1] = meta[2 * N_DEV :]


def route(owner, slot, weight):
    return pl.pallas_call(
        route_kernel,
        name="route",
        out_shape=(
            jax.ShapeDtypeStruct((1, N_DEV), jnp.int32),
            jax.ShapeDtypeStruct((96, 128), jnp.int32),
            jax.ShapeDtypeStruct((2, N_DEV, 128), F32),
        ),
        in_specs=[VMEM] * 3,
        out_specs=[VMEM] * 3,
        scratch_shapes=[pltpu.VMEM((NBR, 128), F32)],
        cost_estimate=pl.CostEstimate(flops=int(4e8), bytes_accessed=200000, transcendentals=0),
    )(owner, slot, weight)


def quad(r):
    x0, y0 = 1.0 - r[0] * r[1], r[0] + r[1]
    x1, y1 = 1.0 - r[2] * r[3], r[2] + r[3]
    return angle(x0 * x1 - y0 * y1, x0 * y1 + x1 * y0)


class Ray:
    def __init__(self, azimuth, step, near, far, inv_base, opening, put):
        self.azimuth, self.step, self.near, self.far = azimuth, step, near, far
        self.inv_base, self.opening, self.put = inv_base, opening, put


def plane_rays(H, it, h0, rays, inv_base, V_old, V, S_ref):
    lane = iota((8, 128), 1)
    rc = lax.shift_right_logical(it, 1)
    p0 = lax.bitwise_and(it, 1) * 4
    block = pl.multiple_of(rc * 8, 8)
    made = []
    for f, (a, sy, sx) in enumerate(rays):
        off = 1 if sx >= 0 else 0
        count = 8 if sx == 0 else 9

        def near(p):
            rows = pl.ds(pl.multiple_of(h0 // 8 + rc * 8, 8), 8)
            return [H[1 + j, p0 + p, rows, :] for j in range(8)]

        def far(p, s, sy=sy, sx=sx, off=off, count=count):
            y = h0 + rc * 64 + p0 + p + sy * s
            plane, i0 = lax.bitwise_and(y, 7), lax.shift_right_logical(y, 3)
            tiles = [H[off + j, plane, pl.ds(i0, 8), :] for j in range(count)]
            if sx == 0:
                return tiles
            amount = 128 - s if sx == 1 else lax.bitwise_and(s, 127)
            keep = lane < (amount if sx == 1 else s)
            rolled = [pltpu.roll(v, amount, 1) for v in tiles]
            return [jnp.where(keep, rolled[j], rolled[j + 1]) for j in range(8)]

        def base(p, sx=sx):
            return 1.0 / pixel_size if sx == 0 else inv_base[p0 + p, pl.ds(block, 8), :]

        def opening(p, j, v, f=f):
            old = V_old if f == 0 else V
            at = (j, p0 + p, pl.ds(block, 8))
            V[at] = v if old is None else old[at] + v

        def put(j, v, f=f):
            S_ref[rc, f, j] += v

        made.append(Ray(a, sy, near, far, base, opening, put))
    return made


def turned_rays(H, it, inv_row, V, S_ref):
    rt = lax.shift_right_logical(it, 2)
    half = lax.bitwise_and(lax.shift_right_logical(it, 1), 1)
    p0 = lax.bitwise_and(it, 1) * 4
    made = []
    for f, (a, sx) in enumerate(((0, 1), (4, -1))):

        def near(p):
            return [H[rt, p0 + p, pl.ds(pl.multiple_of(16 + half * 64 + 8 * j, 8), 8), :] for j in range(8)]

        def far(p, s, sx=sx):
            x = 128 + half * 512 + p0 + p + sx * s
            plane, i0 = lax.bitwise_and(x, 7), lax.shift_right_logical(x, 3)
            return [H[rt, plane, pl.ds(i0 + 8 * j, 8), :] for j in range(8)]

        def base(p):
            return jnp.broadcast_to(inv_row[pl.ds(rt, 1), :], (8, 128))

        def rows(j):
            return pl.ds(pl.multiple_of(half * 64 + 8 * j, 8), 8)

        def opening(p, j, v, f=f):
            at = (rt, p0 + p, rows(j))
            V[at] = v if f == 0 else V[at] + v

        def put(j, v, f=f):
            S_ref[rt, f, rows(j), :] += v

        made.append(Ray(a, sx, near, far, base, opening, put))
    return made


def march(lags, inv_lags, group, rise):
    for p in range(4):
        t = [ray.near(p) for ray in group]
        best = [[None] * 8 for ray in group]
        for k in range(KS):
            for i, ray in enumerate(group):
                inv_lag = inv_lags[ray.azimuth, k]
                got = ray.far(p, lags[ray.azimuth, k])
                for j in range(8):
                    v = (got[j] - t[i][j]) * inv_lag
                    best[i][j] = v if k == 0 else jnp.maximum(best[i][j], v)
        for i, ray in enumerate(group):
            ib = ray.inv_base(p)
            for j in range(8):
                rise[i, p, j] = jnp.minimum(jnp.maximum(best[i][j] * ib, 0.0), 1e8)


def finish(group, rise):
    for i, ray in enumerate(group):
        for j in range(8):
            r = [rise[i, p, j] for p in range(4)]
            for p in range(4):
                ray.opening(p, j, recip(1.0 + r[p] * r[p]))
            ray.put(j, quad(r))


def slanted(southward):
    sy = jnp.where(southward, 1, -1)
    return [(jnp.where(southward, 3, 5), sy, -1), (jnp.where(southward, 2, 6), sy, 0), (jnp.where(southward, 1, 7), sy, 1)]


def copies(pairs, sems):
    made = [pltpu.make_async_copy(a, b, sems.at[i]) for i, (a, b) in enumerate(pairs)]
    for c in made:
        c.start()
    for c in made:
        c.wait()


def one_of(flag, yes, no, sems, base):
    @pl.when(flag)
    def _():
        for i, (a, b) in enumerate(yes):
            pltpu.make_async_copy(a, b, sems.at[base + i]).start()

    @pl.when(jnp.logical_not(flag))
    def _():
        for i, (a, b) in enumerate(no):
            pltpu.make_async_copy(a, b, sems.at[base + i]).start()

    return [pltpu.make_async_copy(a, b, sems.at[base + i]) for i, (a, b) in enumerate(yes)]


def cols(j):
    return pl.ds(j * 128, 128)


def inner_kernel(
    lags, inv_lags, place, own, near, far, inv_base, inv_row, V_ref, S_ref, pooled_ref, Hn, H, Tn, T, VT, ST, X, Xn, rise, sems
):
    sides = one_of(place[2] == 1, ((near, Hn.at[0]), (far, Hn.at[9])), ((far, Hn.at[0]), (near, Hn.at[9])), sems, 8)
    copies([(own.at[:, cols(j)], Hn.at[1 + j]) for j in range(8)], sems)
    for c in sides:
        c.wait()
    for c in range(10):
        for p in range(8):
            H[c, p] = Hn[c, pl.ds(p, 32, stride=8), :]
        for rt in range(2):
            Tn[rt, c * 128 : (c + 1) * 128, :] = Hn[c, rt * 128 : (rt + 1) * 128, :].T
    for rt in range(2):
        for p in range(8):
            T[rt, p] = Tn[rt, pl.ds(p, 160, stride=8), :]
    S_ref[...] = jnp.zeros(S_ref.shape, F32)
    ST[...] = jnp.zeros(ST.shape, F32)

    def step(it, carry):
        left, up, right = plane_rays(H, it, 0, slanted(it < 4), inv_base, None, V_ref, S_ref)
        along, against = turned_rays(T, it, inv_row, VT, ST)
        groups = ((left, along), (right, against), (up,))
        order = (0, 2, 1)
        for n, g in enumerate(groups):
            march(lags, inv_lags, g, rise.at[n])
        for n in order:
            finish(groups[n], rise.at[n])
        return carry

    lax.fori_loop(0, 8, step, 0)
    pool = (iota((16, 128), 0) == lax.shift_right_logical(iota((16, 128), 1), 3)).astype(BF16)
    for rt in range(2):
        for f in range(2):
            hi, lo = split2(ST[rt, f])
            total = lax.dot_general(pool, hi, NT, preferred_element_type=F32)
            pooled_ref[f, rt * 16 : rt * 16 + 16, :] = total + lax.dot_general(pool, lo, NT, preferred_element_type=F32)
        for c in range(8):
            for p in range(8):
                X[rt, c, pl.ds(p, 16, stride=8), :] = VT[rt, p, c * 16 : (c + 1) * 16, :]
    for rt in range(2):
        for c in range(8):
            Xn[rt, c] = X[rt, c].T
    for rt in range(2):
        for c in range(8):
            for p in range(8):
                V_ref[c, p, rt * 16 : rt * 16 + 16, :] += Xn[rt, c, pl.ds(p, 16, stride=8), :]


def inner(*args):
    return pl.pallas_call(
        inner_kernel,
        name="inner",
        out_shape=(
            jax.ShapeDtypeStruct((8, 8, 32, 128), F32),
            jax.ShapeDtypeStruct((4, 3, 8, 8, 128), F32),
            jax.ShapeDtypeStruct((2, NBR, 128), F32),
        ),
        in_specs=[SMEM] * 3 + [ANY] * 3 + [VMEM] * 2,
        out_specs=[VMEM] * 3,
        scratch_shapes=[
            pltpu.VMEM((10, 256, 128), F32),
            pltpu.VMEM((10, 8, 32, 128), F32),
            pltpu.VMEM((2, 1280, 128), F32),
            pltpu.VMEM((2, 8, 160, 128), F32),
            pltpu.VMEM((2, 8, 128, 128), F32),
            pltpu.VMEM((2, 2, 128, 128), F32),
            pltpu.VMEM((2, 8, 128, 128), F32),
            pltpu.VMEM((2, 8, 128, 128), F32),
            pltpu.VMEM((3, 2, 4, 8, 8, 128), F32),
            pltpu.SemaphoreType.DMA((10,)),
        ],
        compiler_params=pltpu.CompilerParams(vmem_limit_bytes=32 * 1024 * 1024),
        cost_estimate=pl.CostEstimate(flops=int(4e8), bytes_accessed=30000000, transcendentals=0),
    )(*args)


def outer_kernel(
    lags, inv_lags, starts, place, own, same, other, near, far, inv_base, V_in, S_in, pooled, weight, owner, index, meta,
    svf_ref, out_ref, Hn, H, S, V, Vn, R, Z, Y, O, acc, rise, sems,
):
    def rows(ref, first):
        return [(ref.at[:, cols(j)], Hn.at[j, pl.ds(first, 128)]) for j in range(10)]

    def side(ref, c):
        return (ref, Hn.at[c, pl.ds(128, 256)])

    made = one_of(place[2] == 1, (side(near, 0), side(far, 9)), (side(far, 0), side(near, 9)), sems, 8)
    odd = lax.bitwise_and(place[0], 1) == 1
    made += one_of(odd, rows(same, 0) + rows(other, 384), rows(other, 0) + rows(same, 384), sems, 10)
    copies([(own.at[:, cols(j)], Hn.at[1 + j, pl.ds(128, 256)]) for j in range(8)], sems)
    for c in made:
        c.wait()

    @pl.when(place[0] == 0)
    def _():
        for c in range(10):
            Hn[c, 0:128, :] = jnp.broadcast_to(Hn[c, 128:129, :], (128, 128))

    @pl.when(place[0] == place[1] - 1)
    def _():
        for c in range(10):
            Hn[c, 384:512, :] = jnp.broadcast_to(Hn[c, 383:384, :], (128, 128))

    for c in range(10):
        for p in range(8):
            H[c, p] = Hn[c, pl.ds(p, 64, stride=8), :]
    S[...] = jnp.zeros(S.shape, F32)

    def step(it, carry):
        left, up, right = plane_rays(H, it, 128, slanted(it >= 4), inv_base, V_in, V, S)
        groups = ((left, up), (right,))
        for n, g in enumerate(groups):
            march(lags, inv_lags, g, rise.at[n])
        for n, g in enumerate(groups):
            finish(g, rise.at[n])
        return carry

    lax.fori_loop(0, 8, step, 0)
    svf_rows = []
    for j in range(8):
        rows = V[j, 0]
        for p in range(8):
            Vn[j, pl.ds(p, 32, stride=8), :] = V[j, p] * (1.0 / AZ)
            rows = rows if p == 0 else rows + V[j, p]
        svf_rows.append(rows)
    written = [pltpu.make_async_copy(Vn.at[j], svf_ref.at[:, cols(j)], sems.at[30 + j]) for j in range(8)]
    for c in written:
        c.start()

    total = jnp.zeros((224, 128), F32)
    for j in range(8):
        pool = (iota((128, 128), 1) == j * 16 + lax.shift_right_logical(iota((128, 128), 0), 3)).astype(BF16)
        field = []
        for rc in range(4):
            south, north_ = (S_in, S) if rc < 2 else (S, S_in)
            field += [south[rc, 2, j], south[rc, 1, j], south[rc, 0, j], north_[rc, 0, j], north_[rc, 1, j], north_[rc, 2, j]]
            field.append(svf_rows[j][rc * 8 : rc * 8 + 8, :])
        hi, lo = split2(jnp.concatenate(field, axis=0))
        total = total + jnp.dot(hi, pool, preferred_element_type=F32) + jnp.dot(lo, pool, preferred_element_type=F32)
    for rc in range(4):
        part = [total[rc * 56 + 8 * i : rc * 56 + 8 * i + 8] for i in range(7)]
        flat = [pooled[f, rc * 8 : rc * 8 + 8, :] for f in range(2)]
        R[rc * 72 : rc * 72 + 72, :] = jnp.concatenate([flat[0]] + part[:3] + [flat[1]] + part[3:], axis=0)
    lane = iota((8, 128), 1)
    scale = 1.0 / 4096.0
    for rc in range(4):
        for i in range(8):
            b = rc * 8 + i
            Y[b] = R[pl.ds(rc * 72 + i, 8, stride=8), :] * (weight[b : b + 1, :].astype(F32) * scale)
        O[rc * 8 : rc * 8 + 8, :] = R[rc * 72 + 64 : rc * 72 + 72, :] * (weight[rc * 8 : rc * 8 + 8, :].astype(F32) * (scale / AZ))

    acc[...] = jnp.zeros(acc.shape, F32)
    low = iota((256, 512), 0).astype(F32).astype(BF16)
    zero = jnp.zeros((16, 512), BF16)
    none = jnp.zeros((64, 512), BF16)

    def wide(v, row, height):
        v = jnp.concatenate([v[pl.ds(row + i, 1), :] for i in range(4)], axis=1)
        return jnp.broadcast_to(v.astype(F32), (height, 512))

    def sort(g, carry):
        b = g * 4
        v = jnp.concatenate([Y[b + i] for i in range(4)], axis=1)
        v = jnp.concatenate(split2(v), axis=0)
        tile = wide(index, b, 16).astype(BF16)
        left = [jnp.where(tile == BF16(t), v, zero) for t in range(NBR // 2)]
        hot = (low == wide(index, 32 + b, 256).astype(BF16)).astype(BF16)
        acc[0:256, :] += lax.dot_general(jnp.concatenate(left, axis=0), hot, NT, preferred_element_type=F32)
        o_hi, o_lo = split2(wide(O, b, 64))
        mine = low[:64] == jnp.floor(wide(owner, b, 64) * 0.5).astype(BF16)
        hot = (low == wide(index, 64 + b, 256).astype(BF16)).astype(BF16)
        left = [jnp.where(mine, o_hi, none), jnp.where(mine, o_lo, none)]
        acc[256:384, :] += lax.dot_general(jnp.concatenate(left, axis=0), hot, NT, preferred_element_type=F32)
        return carry

    lax.fori_loop(0, NBR // 4, sort, 0, unroll=4)
    for t in range(NBR):
        r, c = t // 2 * 16, t % 2 * 128
        Z[t] = acc[r : r + 8, c : c + 128] + acc[r + 8 : r + 16, c : c + 128]
    Z[32] = jnp.zeros((8, 128), F32)
    Z[33] = jnp.zeros((8, 128), F32)
    for odd in range(2):
        c = odd * 128
        out_ref[pl.ds(8 + 11 * odd, 64, stride=22), :] = acc[256:320, c : c + 128] + acc[320:384, c : c + 128]
    out_ref[pl.ds(9, N_DEV, stride=11), :] = meta[0]
    out_ref[pl.ds(10, N_DEV, stride=11), :] = meta[1]

    def expand(g, carry):
        owners = [g * 16 + i for i in range(16)]
        st = [starts[0, o] for o in owners]
        tile = [lax.shift_right_logical(s, 7) for s in st]
        q = [128 - lax.bitwise_and(s, 127) for s in st]
        a = [pltpu.roll(Z[t], lax.bitwise_and(n, 127), 1) for t, n in zip(tile, q)]
        b = [pltpu.roll(Z[t + 1], lax.bitwise_and(n, 127), 1) for t, n in zip(tile, q)]
        got = [jnp.where(lane < n, u, w) for n, u, w in zip(q, a, b)]
        for o, v in zip(owners, got):
            out_ref[pl.ds(o * 11, 8), :] = v
        return carry

    lax.fori_loop(0, N_DEV // 16, expand, 0)
    for c in written:
        c.wait()


def outer(*args):
    return pl.pallas_call(
        outer_kernel,
        name="outer",
        out_shape=(jax.ShapeDtypeStruct((256, 1024), F32), jax.ShapeDtypeStruct((N_DEV * 11, 128), F32)),
        in_specs=[SMEM] * 4 + [ANY] * 5 + [VMEM] * 8,
        out_specs=[ANY, VMEM],
        scratch_shapes=[
            pltpu.VMEM((10, 512, 128), F32),
            pltpu.VMEM((10, 8, 64, 128), F32),
            pltpu.VMEM((4, 3, 8, 8, 128), F32),
            pltpu.VMEM((8, 8, 32, 128), F32),
            pltpu.VMEM((8, 256, 128), F32),
            pltpu.VMEM((288, 128), F32),
            pltpu.VMEM((34, 8, 128), F32),
            pltpu.VMEM((32, 8, 128), F32),
            pltpu.VMEM((32, 128), F32),
            pltpu.VMEM((384, 256), F32),
            pltpu.VMEM((2, 2, 4, 8, 8, 128), F32),
            pltpu.SemaphoreType.DMA((38,)),
        ],
        compiler_params=pltpu.CompilerParams(vmem_limit_bytes=32 * 1024 * 1024),
        cost_estimate=pl.CostEstimate(flops=int(4e8), bytes_accessed=20000000, transcendentals=0),
    )(*args)


def cells_kernel(got_ref, horizon_ref, svf_ref):
    low = iota((128, 512), 0).astype(F32).astype(BF16)

    def accumulate(t, acc):
        first = jnp.concatenate([got_ref[pl.ds(t * 44 + 11 * i, 8), :] for i in range(4)], axis=1)
        second = jnp.concatenate([got_ref[pl.ds(t * 44 + 11 * i + 3, 8), :] for i in range(4)], axis=1)
        hi, lo = split2(jnp.concatenate([first, second], axis=0))
        cell = second[6:7, :] - 1.0
        upper = jnp.floor(cell * (1.0 / 128.0))
        high = jnp.broadcast_to(upper, (16, 512)).astype(BF16)
        zero = jnp.zeros((16, 512), BF16)
        left = []
        for h in range(4):
            mine = high == BF16(h)
            left += [jnp.where(mine, hi, zero), jnp.where(mine, lo, zero)]
        hot = (low == jnp.broadcast_to(cell - 128.0 * upper, (128, 512)).astype(BF16)).astype(BF16)
        return acc + lax.dot_general(jnp.concatenate(left, axis=0), hot, NT, preferred_element_type=F32)

    acc = lax.fori_loop(0, N_DEV // 4, accumulate, jnp.zeros((128, 128), F32), unroll=True)
    sums = jnp.concatenate([acc[h * 32 : h * 32 + 16] + acc[h * 32 + 16 : h * 32 + 32] for h in range(4)], axis=1)
    area = jnp.maximum(sums[15:16, :] * (1.0 / 64.0), 1.0)
    horizon_ref[...] = sums[0:8] / area
    svf_ref[...] = sums[13:14] / area


def cells(got):
    return pl.pallas_call(
        cells_kernel,
        name="cells",
        out_shape=(jax.ShapeDtypeStruct((AZ, CELLS_DEV), F32), jax.ShapeDtypeStruct((1, CELLS_DEV), F32)),
        in_specs=[VMEM],
        out_specs=[VMEM] * 2,
        compiler_params=pltpu.CompilerParams(vmem_limit_bytes=24 * 1024 * 1024),
    )(got)


def shards(terrain_surface, azimuth_lag_tallies, holder_devices, holder_region_slot, footprint_weight):
    rows, width = terrain_surface.shape
    n_lat = lax.axis_size("lat")
    n_lon = lax.axis_size("lon")
    W = FARTHEST_LAG
    own = terrain_surface
    lat, lon = lax.axis_index("lat"), lax.axis_index("lon")
    odd = lon % 2

    def exchange(block, axis, size, first, wrap):
        pairs = []
        for i in range(first, size, 2):
            if i + 1 < size or wrap:
                pairs += [(i, (i + 1) % size), ((i + 1) % size, i)]
        return lax.ppermute(block, axis, pairs)

    def edge(block, at_end, dim):
        return lax.dynamic_slice_in_dim(block, jnp.where(at_end, block.shape[dim] - W, 0), W, axis=dim)

    far = exchange(edge(own, odd == 1, 1), "lon", n_lon, 1, True)
    near = exchange(edge(own, odd == 0, 1), "lon", n_lon, 0, True)
    weight = footprint_weight.reshape(NBR, 128)
    owner = holder_devices.reshape(NBR, 128)
    start, index, meta = route(owner, holder_region_slot.reshape(NBR, 128), weight)
    near, far, start, index, meta = lax.optimization_barrier((near, far, start, index, meta))
    west, east = jnp.where(odd == 1, near, far), jnp.where(odd == 1, far, near)

    def wide(at_end):
        return jnp.concatenate([edge(west, at_end, 0), edge(own, at_end, 0), edge(east, at_end, 0)], axis=1)

    other = exchange(wide(lat % 2 == 1), "lat", n_lat, 1, False)
    same = exchange(wide(lat % 2 == 0), "lat", n_lat, 0, False)

    rows_global = (lax.axis_index("lat") * rows + jnp.arange(rows, dtype=jnp.int32)).astype(F32)
    latitude = 47.0 - (rows_global + 0.5) / 1200.0
    coslat = jnp.cos(latitude * jnp.pi / 180.0)
    across = (pixel_size * coslat) ** 2
    inv_row = (1.0 / jnp.sqrt(across)).reshape(2, 128)
    inv_base = 1.0 / jnp.sqrt(pixel_size**2 + across)
    inv_base = jnp.broadcast_to(inv_base.reshape(32, 8).T[:, :, None], (8, 32, 128))
    place = jnp.stack([lat.astype(jnp.int32), jnp.int32(n_lat), odd.astype(jnp.int32)])
    inv_lags = 1.0 / azimuth_lag_tallies.astype(F32)
    part, sums, pooled = inner(azimuth_lag_tallies, inv_lags, place, own, near, far, inv_base, inv_row)
    fine_svf, packed = outer(
        azimuth_lag_tallies, inv_lags, start, place, own, same, other, near, far, inv_base, part, sums, pooled,
        weight, owner, index, meta,
    )
    packed = packed.reshape(N_DEV, 1, 11 * 128)
    got = lax.all_to_all(packed, ("lat", "lon"), split_axis=0, concat_axis=0, tiled=True)
    got = got.reshape(N_DEV * 11, 128)
    cell_horizon, cell_svf = cells(got)
    return fine_svf, cell_horizon, cell_svf.reshape(CELLS_DEV)


def solution(mesh):
    P = jax.sharding.PartitionSpec
    in_specs = (P("lat", "lon"), P(), P(("lat", "lon"), None), P(("lat", "lon")), P(("lat", "lon")))
    out_specs = (P("lat", "lon"), P(None, ("lat", "lon")), P(("lat", "lon")))
    return jax.shard_map(shards, mesh=mesh, in_specs=in_specs, out_specs=out_specs, check_vma=False)
```

```python
import jax
import jax.numpy as jnp
from jax import lax
from jax.experimental import pallas as pl
from jax.experimental.pallas import tpu as pltpu

FARTHEST_LAG = 128
AZ = 8
KS = 8
pixel_size = 92.6
ATAN = (0.9999999, -0.33331991, 0.19969724, -0.14019481, 0.09914293, -0.05948639, 0.0242524, -0.00469327)
HALF_PI = 1.5707963267948966


def recip(v):
    return pl.reciprocal(v, approx=True)


def angle(x, y):
    ax, ay = jnp.abs(x), jnp.abs(y)
    z = jnp.minimum(ax, ay) * recip(jnp.maximum(ax, ay))
    u = z * z
    p = ATAN[7]
    for c in ATAN[6::-1]:
        p = p * u + c
    p = p * z
    p = jnp.where(ay > ax, HALF_PI - p, p)
    p = jnp.where(x < 0.0, 2.0 * HALF_PI - p, p)
    return jnp.where(y < 0.0, 4.0 * HALF_PI - p, p)


N_DEV = 128
NBR = 32
CELLS_DEV = 512
F32 = jnp.float32
BF16 = jnp.bfloat16
VMEM = pl.BlockSpec(memory_space=pltpu.VMEM)
SMEM = pl.BlockSpec(memory_space=pltpu.SMEM)
ANY = pl.BlockSpec(memory_space=pl.ANY)
NT = (((1,), (1,)), ((), ()))


def split2(v):
    hi = v.astype(BF16)
    return hi, (v - hi.astype(F32)).astype(BF16)


def iota(shape, dim):
    return lax.broadcasted_iota(jnp.int32, shape, dim)


def route_kernel(owner_ref, slot_ref, weight_ref, start_ref, index_ref, meta_ref, rank_ref):
    sub = iota((N_DEV, 128), 0)
    upper = (iota((128, 128), 0) < iota((128, 128), 1)).astype(BF16)
    right = jnp.concatenate([upper, jnp.ones((128, 128), BF16)], axis=1)
    count = jnp.zeros((N_DEV, 128), F32)
    for i in range(NBR):
        mine = sub == owner_ref[i : i + 1, :]
        both = jnp.dot(mine.astype(BF16), right, preferred_element_type=F32)
        rank = jnp.sum(jnp.where(mine, both[:, :128] + count, 0.0), axis=0, keepdims=True)
        rank_ref[i : i + 1, :] = rank
        count = count + both[:, 128:]
    lower = (iota((128, 128), 0) > iota((128, 128), 1)).astype(BF16)
    start = jnp.dot(lower, count.astype(BF16), preferred_element_type=F32)
    start_row = lax.dot_general(count[:, :8].T.astype(BF16), upper, (((1,), (0,)), ((), ())), preferred_element_type=F32)
    start_ref[...] = start_row[:1].astype(jnp.int32)
    meta = jnp.zeros((3 * N_DEV, 128), F32)
    for i in range(NBR):
        mine = sub == owner_ref[i : i + 1, :]
        rank = rank_ref[i : i + 1, :]
        place = (rank + jnp.sum(jnp.where(mine, start, 0.0), axis=0, keepdims=True)).astype(jnp.int32)
        rank = rank.astype(jnp.int32)
        index_ref[i : i + 1, :] = lax.shift_right_logical(place, 8)
        index_ref[NBR + i : NBR + i + 1, :] = lax.bitwise_and(place, 255)
        odd = lax.bitwise_and(owner_ref[i : i + 1, :], 1) * 128
        index_ref[2 * NBR + i : 2 * NBR + i + 1, :] = rank + odd
        rank_hot = (sub == rank).astype(BF16)
        slot = slot_ref[i : i + 1, :] + 1
        parts = (lax.shift_right_logical(slot, 4), lax.bitwise_and(slot, 15), weight_ref[i : i + 1, :])
        left = jnp.concatenate([jnp.where(mine, v.astype(F32), 0.0) for v in parts], axis=0).astype(BF16)
        meta = meta + lax.dot_general(left, rank_hot, NT, preferred_element_type=F32)
    meta_ref[0] = meta[:N_DEV] * 16.0 + meta[N_DEV : 2 * N_DEV]
    meta_ref[1] = meta[2 * N_DEV :]


def route(owner, slot, weight):
    return pl.pallas_call(
        route_kernel,
        name="route",
        out_shape=(
            jax.ShapeDtypeStruct((1, N_DEV), jnp.int32),
            jax.ShapeDtypeStruct((96, 128), jnp.int32),
            jax.ShapeDtypeStruct((2, N_DEV, 128), F32),
        ),
        in_specs=[VMEM] * 3,
        out_specs=[VMEM] * 3,
        scratch_shapes=[pltpu.VMEM((NBR, 128), F32)],
        compiler_params=pltpu.CompilerParams(vmem_limit_bytes=8 * 1024 * 1024),
        cost_estimate=pl.CostEstimate(flops=int(4e8), bytes_accessed=200000, transcendentals=0),
    )(owner, slot, weight)


def quad(r):
    x0, y0 = 1.0 - r[0] * r[1], r[0] + r[1]
    x1, y1 = 1.0 - r[2] * r[3], r[2] + r[3]
    return angle(x0 * x1 - y0 * y1, x0 * y1 + x1 * y0)


class Ray:
    def __init__(self, azimuth, step, near, far, inv_base, opening, put):
        self.azimuth, self.step, self.near, self.far = azimuth, step, near, far
        self.inv_base, self.opening, self.put = inv_base, opening, put


def plane_rays(H, it, h0, rays, inv_base, V_old, V, S_ref):
    lane = iota((8, 128), 1)
    rc = lax.shift_right_logical(it, 1)
    p0 = lax.bitwise_and(it, 1) * 4
    block = pl.multiple_of(rc * 8, 8)
    made = []
    for f, (a, sy, sx) in enumerate(rays):
        off = 1 if sx >= 0 else 0
        count = 8 if sx == 0 else 9

        def near(p):
            rows = pl.ds(pl.multiple_of(h0 // 8 + rc * 8, 8), 8)
            return [H[1 + j, p0 + p, rows, :] for j in range(8)]

        def far(p, s, sy=sy, sx=sx, off=off, count=count):
            y = h0 + rc * 64 + p0 + p + sy * s
            plane, i0 = lax.bitwise_and(y, 7), lax.shift_right_logical(y, 3)
            tiles = [H[off + j, plane, pl.ds(i0, 8), :] for j in range(count)]
            if sx == 0:
                return tiles
            amount = 128 - s if sx == 1 else lax.bitwise_and(s, 127)
            keep = lane < (amount if sx == 1 else s)
            rolled = [pltpu.roll(v, amount, 1) for v in tiles]
            return [jnp.where(keep, rolled[j], rolled[j + 1]) for j in range(8)]

        def base(p, sx=sx):
            return 1.0 / pixel_size if sx == 0 else inv_base[p0 + p, pl.ds(block, 8), :]

        def opening(p, j, v, f=f):
            old = V_old if f == 0 else V
            at = (j, p0 + p, pl.ds(block, 8))
            V[at] = v if old is None else old[at] + v

        def put(j, v, f=f):
            S_ref[rc, f, j] += v

        made.append(Ray(a, sy, near, far, base, opening, put))
    return made


def turned_rays(H, it, inv_row, V, S_ref):
    rt = lax.shift_right_logical(it, 2)
    half = lax.bitwise_and(lax.shift_right_logical(it, 1), 1)
    p0 = lax.bitwise_and(it, 1) * 4
    made = []
    for f, (a, sx) in enumerate(((0, 1), (4, -1))):

        def near(p):
            return [H[rt, p0 + p, pl.ds(pl.multiple_of(16 + half * 64 + 8 * j, 8), 8), :] for j in range(8)]

        def far(p, s, sx=sx):
            x = 128 + half * 512 + p0 + p + sx * s
            plane, i0 = lax.bitwise_and(x, 7), lax.shift_right_logical(x, 3)
            return [H[rt, plane, pl.ds(i0 + 8 * j, 8), :] for j in range(8)]

        def base(p):
            return jnp.broadcast_to(inv_row[pl.ds(rt, 1), :], (8, 128))

        def rows(j):
            return pl.ds(pl.multiple_of(half * 64 + 8 * j, 8), 8)

        def opening(p, j, v, f=f):
            at = (rt, p0 + p, rows(j))
            V[at] = v if f == 0 else V[at] + v

        def put(j, v, f=f):
            S_ref[rt, f, rows(j), :] += v

        made.append(Ray(a, sx, near, far, base, opening, put))
    return made


def march(lags, inv_lags, group, rise):
    for p in range(4):
        t = [ray.near(p) for ray in group]
        best = [[None] * 8 for ray in group]
        for k in range(KS):
            for i, ray in enumerate(group):
                inv_lag = inv_lags[ray.azimuth, k]
                got = ray.far(p, lags[ray.azimuth, k])
                for j in range(8):
                    v = (got[j] - t[i][j]) * inv_lag
                    best[i][j] = v if k == 0 else jnp.maximum(best[i][j], v)
        for i, ray in enumerate(group):
            ib = ray.inv_base(p)
            for j in range(8):
                rise[i, p, j] = jnp.minimum(jnp.maximum(best[i][j] * ib, 0.0), 1e8)


def finish(group, rise):
    for i, ray in enumerate(group):
        for j in range(8):
            r = [rise[i, p, j] for p in range(4)]
            for p in range(4):
                ray.opening(p, j, recip(1.0 + r[p] * r[p]))
            ray.put(j, quad(r))


def slanted(southward):
    sy = jnp.where(southward, 1, -1)
    return [(jnp.where(southward, 3, 5), sy, -1), (jnp.where(southward, 2, 6), sy, 0), (jnp.where(southward, 1, 7), sy, 1)]


def copies(pairs, sems):
    made = [pltpu.make_async_copy(a, b, sems.at[i]) for i, (a, b) in enumerate(pairs)]
    for c in made:
        c.start()
    for c in made:
        c.wait()


def one_of(flag, yes, no, sems, base):
    @pl.when(flag)
    def _():
        for i, (a, b) in enumerate(yes):
            pltpu.make_async_copy(a, b, sems.at[base + i]).start()

    @pl.when(jnp.logical_not(flag))
    def _():
        for i, (a, b) in enumerate(no):
            pltpu.make_async_copy(a, b, sems.at[base + i]).start()

    return [pltpu.make_async_copy(a, b, sems.at[base + i]) for i, (a, b) in enumerate(yes)]


def cols(j):
    return pl.ds(j * 128, 128)


def inner_kernel(
    lags, inv_lags, place, own, near, far, inv_base, inv_row, V_ref, S_ref, pooled_ref, Hn, H, Tn, T, VT, ST, X, Xn, rise, sems
):
    sides = one_of(place[2] == 1, ((near, Hn.at[0]), (far, Hn.at[9])), ((far, Hn.at[0]), (near, Hn.at[9])), sems, 8)
    copies([(own.at[:, cols(j)], Hn.at[1 + j]) for j in range(8)], sems)
    for c in sides:
        c.wait()
    for c in range(10):
        for p in range(8):
            H[c, p] = Hn[c, pl.ds(p, 32, stride=8), :]
        for rt in range(2):
            Tn[rt, c * 128 : (c + 1) * 128, :] = Hn[c, rt * 128 : (rt + 1) * 128, :].T
    for rt in range(2):
        for p in range(8):
            T[rt, p] = Tn[rt, pl.ds(p, 160, stride=8), :]
    S_ref[...] = jnp.zeros(S_ref.shape, F32)
    ST[...] = jnp.zeros(ST.shape, F32)

    def step(it, carry):
        left, up, right = plane_rays(H, it, 0, slanted(it < 4), inv_base, None, V_ref, S_ref)
        along, against = turned_rays(T, it, inv_row, VT, ST)
        groups = ((left, along), (right, against), (up,))
        order = (0, 2, 1)
        for n, g in enumerate(groups):
            march(lags, inv_lags, g, rise.at[n])
        for n in order:
            finish(groups[n], rise.at[n])
        return carry

    lax.fori_loop(0, 8, step, 0)
    pool = (iota((16, 128), 0) == lax.shift_right_logical(iota((16, 128), 1), 3)).astype(BF16)
    for rt in range(2):
        for f in range(2):
            hi, lo = split2(ST[rt, f])
            total = lax.dot_general(pool, hi, NT, preferred_element_type=F32)
            pooled_ref[f, rt * 16 : rt * 16 + 16, :] = total + lax.dot_general(pool, lo, NT, preferred_element_type=F32)
        for c in range(8):
            for p in range(8):
                X[rt, c, pl.ds(p, 16, stride=8), :] = VT[rt, p, c * 16 : (c + 1) * 16, :]
    for rt in range(2):
        for c in range(8):
            Xn[rt, c] = X[rt, c].T
    for rt in range(2):
        for c in range(8):
            for p in range(8):
                V_ref[c, p, rt * 16 : rt * 16 + 16, :] += Xn[rt, c, pl.ds(p, 16, stride=8), :]


def inner(*args):
    return pl.pallas_call(
        inner_kernel,
        name="inner",
        out_shape=(
            jax.ShapeDtypeStruct((8, 8, 32, 128), F32),
            jax.ShapeDtypeStruct((4, 3, 8, 8, 128), F32),
            jax.ShapeDtypeStruct((2, NBR, 128), F32),
        ),
        in_specs=[SMEM] * 3 + [ANY] * 3 + [VMEM] * 2,
        out_specs=[VMEM] * 3,
        scratch_shapes=[
            pltpu.VMEM((10, 256, 128), F32),
            pltpu.VMEM((10, 8, 32, 128), F32),
            pltpu.VMEM((2, 1280, 128), F32),
            pltpu.VMEM((2, 8, 160, 128), F32),
            pltpu.VMEM((2, 8, 128, 128), F32),
            pltpu.VMEM((2, 2, 128, 128), F32),
            pltpu.VMEM((2, 8, 128, 128), F32),
            pltpu.VMEM((2, 8, 128, 128), F32),
            pltpu.VMEM((3, 2, 4, 8, 8, 128), F32),
            pltpu.SemaphoreType.DMA((10,)),
        ],
        compiler_params=pltpu.CompilerParams(vmem_limit_bytes=20 * 1024 * 1024),
        cost_estimate=pl.CostEstimate(flops=int(4e8), bytes_accessed=30000000, transcendentals=0),
    )(*args)


def outer_kernel(
    lags, inv_lags, starts, place, own, same, other, near, far, inv_base, V_in, S_in, pooled, weight, owner, index, meta,
    svf_ref, out_ref, Hn, H, S, V, Vn, R, Z, Y, O, acc, rise, sems,
):
    def rows(ref, first):
        return [(ref.at[:, cols(j)], Hn.at[j, pl.ds(first, 128)]) for j in range(10)]

    def side(ref, c):
        return (ref, Hn.at[c, pl.ds(128, 256)])

    made = one_of(place[2] == 1, (side(near, 0), side(far, 9)), (side(far, 0), side(near, 9)), sems, 8)
    odd = lax.bitwise_and(place[0], 1) == 1
    made += one_of(odd, rows(same, 0) + rows(other, 384), rows(other, 0) + rows(same, 384), sems, 10)
    copies([(own.at[:, cols(j)], Hn.at[1 + j, pl.ds(128, 256)]) for j in range(8)], sems)
    for c in made:
        c.wait()

    @pl.when(place[0] == 0)
    def _():
        for c in range(10):
            Hn[c, 0:128, :] = jnp.broadcast_to(Hn[c, 128:129, :], (128, 128))

    @pl.when(place[0] == place[1] - 1)
    def _():
        for c in range(10):
            Hn[c, 384:512, :] = jnp.broadcast_to(Hn[c, 383:384, :], (128, 128))

    for c in range(10):
        for p in range(8):
            H[c, p] = Hn[c, pl.ds(p, 64, stride=8), :]
    S[...] = jnp.zeros(S.shape, F32)

    def step(it, carry):
        left, up, right = plane_rays(H, it, 128, slanted(it >= 4), inv_base, V_in, V, S)
        groups = ((left, up), (right,))
        for n, g in enumerate(groups):
            march(lags, inv_lags, g, rise.at[n])
        for n, g in enumerate(groups):
            finish(g, rise.at[n])
        return carry

    lax.fori_loop(0, 8, step, 0)
    svf_rows = []
    for j in range(8):
        rows = V[j, 0]
        for p in range(8):
            Vn[j, pl.ds(p, 32, stride=8), :] = V[j, p] * (1.0 / AZ)
            rows = rows if p == 0 else rows + V[j, p]
        svf_rows.append(rows)
    written = [pltpu.make_async_copy(Vn.at[j], svf_ref.at[:, cols(j)], sems.at[30 + j]) for j in range(8)]
    for c in written:
        c.start()

    total = jnp.zeros((224, 128), F32)
    for j in range(8):
        pool = (iota((128, 128), 1) == j * 16 + lax.shift_right_logical(iota((128, 128), 0), 3)).astype(BF16)
        field = []
        for rc in range(4):
            south, north_ = (S_in, S) if rc < 2 else (S, S_in)
            field += [south[rc, 2, j], south[rc, 1, j], south[rc, 0, j], north_[rc, 0, j], north_[rc, 1, j], north_[rc, 2, j]]
            field.append(svf_rows[j][rc * 8 : rc * 8 + 8, :])
        hi, lo = split2(jnp.concatenate(field, axis=0))
        total = total + jnp.dot(hi, pool, preferred_element_type=F32) + jnp.dot(lo, pool, preferred_element_type=F32)
    for rc in range(4):
        part = [total[rc * 56 + 8 * i : rc * 56 + 8 * i + 8] for i in range(7)]
        flat = [pooled[f, rc * 8 : rc * 8 + 8, :] for f in range(2)]
        R[rc * 72 : rc * 72 + 72, :] = jnp.concatenate([flat[0]] + part[:3] + [flat[1]] + part[3:], axis=0)
    lane = iota((8, 128), 1)
    scale = 1.0 / 4096.0
    for rc in range(4):
        for i in range(8):
            b = rc * 8 + i
            Y[b] = R[pl.ds(rc * 72 + i, 8, stride=8), :] * (weight[b : b + 1, :].astype(F32) * scale)
        O[rc * 8 : rc * 8 + 8, :] = R[rc * 72 + 64 : rc * 72 + 72, :] * (weight[rc * 8 : rc * 8 + 8, :].astype(F32) * (scale / AZ))

    acc[...] = jnp.zeros(acc.shape, F32)
    low = iota((256, 512), 0).astype(F32).astype(BF16)
    zero = jnp.zeros((16, 512), BF16)
    none = jnp.zeros((64, 512), BF16)

    def wide(v, row, height):
        v = jnp.concatenate([v[pl.ds(row + i, 1), :] for i in range(4)], axis=1)
        return jnp.broadcast_to(v.astype(F32), (height, 512))

    def sort(g, carry):
        b = g * 4
        v = jnp.concatenate([Y[b + i] for i in range(4)], axis=1)
        v = jnp.concatenate(split2(v), axis=0)
        tile = wide(index, b, 16).astype(BF16)
        left = [jnp.where(tile == BF16(t), v, zero) for t in range(NBR // 2)]
        hot = (low == wide(index, 32 + b, 256).astype(BF16)).astype(BF16)
        acc[0:256, :] += lax.dot_general(jnp.concatenate(left, axis=0), hot, NT, preferred_element_type=F32)
        o_hi, o_lo = split2(wide(O, b, 64))
        mine = low[:64] == jnp.floor(wide(owner, b, 64) * 0.5).astype(BF16)
        hot = (low == wide(index, 64 + b, 256).astype(BF16)).astype(BF16)
        left = [jnp.where(mine, o_hi, none), jnp.where(mine, o_lo, none)]
        acc[256:384, :] += lax.dot_general(jnp.concatenate(left, axis=0), hot, NT, preferred_element_type=F32)
        return carry

    lax.fori_loop(0, NBR // 4, sort, 0, unroll=4)
    for t in range(NBR):
        r, c = t // 2 * 16, t % 2 * 128
        Z[t] = acc[r : r + 8, c : c + 128] + acc[r + 8 : r + 16, c : c + 128]
    Z[32] = jnp.zeros((8, 128), F32)
    Z[33] = jnp.zeros((8, 128), F32)
    for odd in range(2):
        c = odd * 128
        out_ref[pl.ds(8 + 11 * odd, 64, stride=22), :] = acc[256:320, c : c + 128] + acc[320:384, c : c + 128]
    out_ref[pl.ds(9, N_DEV, stride=11), :] = meta[0]
    out_ref[pl.ds(10, N_DEV, stride=11), :] = meta[1]

    def expand(g, carry):
        owners = [g * 16 + i for i in range(16)]
        st = [starts[0, o] for o in owners]
        tile = [lax.shift_right_logical(s, 7) for s in st]
        q = [128 - lax.bitwise_and(s, 127) for s in st]
        a = [pltpu.roll(Z[t], lax.bitwise_and(n, 127), 1) for t, n in zip(tile, q)]
        b = [pltpu.roll(Z[t + 1], lax.bitwise_and(n, 127), 1) for t, n in zip(tile, q)]
        got = [jnp.where(lane < n, u, w) for n, u, w in zip(q, a, b)]
        for o, v in zip(owners, got):
            out_ref[pl.ds(o * 11, 8), :] = v
        return carry

    lax.fori_loop(0, N_DEV // 16, expand, 0)
    for c in written:
        c.wait()


def outer(*args):
    return pl.pallas_call(
        outer_kernel,
        name="outer",
        out_shape=(jax.ShapeDtypeStruct((256, 1024), F32), jax.ShapeDtypeStruct((N_DEV * 11, 128), F32)),
        in_specs=[SMEM] * 4 + [ANY] * 5 + [VMEM] * 8,
        out_specs=[ANY, VMEM],
        scratch_shapes=[
            pltpu.VMEM((10, 512, 128), F32),
            pltpu.VMEM((10, 8, 64, 128), F32),
            pltpu.VMEM((4, 3, 8, 8, 128), F32),
            pltpu.VMEM((8, 8, 32, 128), F32),
            pltpu.VMEM((8, 256, 128), F32),
            pltpu.VMEM((288, 128), F32),
            pltpu.VMEM((34, 8, 128), F32),
            pltpu.VMEM((32, 8, 128), F32),
            pltpu.VMEM((32, 128), F32),
            pltpu.VMEM((384, 256), F32),
            pltpu.VMEM((2, 2, 4, 8, 8, 128), F32),
            pltpu.SemaphoreType.DMA((38,)),
        ],
        compiler_params=pltpu.CompilerParams(vmem_limit_bytes=20 * 1024 * 1024),
        cost_estimate=pl.CostEstimate(flops=int(4e8), bytes_accessed=20000000, transcendentals=0),
    )(*args)


def cells_kernel(got_ref, horizon_ref, svf_ref):
    low = iota((128, 512), 0).astype(F32).astype(BF16)

    def accumulate(t, acc):
        first = jnp.concatenate([got_ref[pl.ds(t * 44 + 11 * i, 8), :] for i in range(4)], axis=1)
        second = jnp.concatenate([got_ref[pl.ds(t * 44 + 11 * i + 3, 8), :] for i in range(4)], axis=1)
        hi, lo = split2(jnp.concatenate([first, second], axis=0))
        cell = second[6:7, :] - 1.0
        upper = jnp.floor(cell * (1.0 / 128.0))
        high = jnp.broadcast_to(upper, (16, 512)).astype(BF16)
        zero = jnp.zeros((16, 512), BF16)
        left = []
        for h in range(4):
            mine = high == BF16(h)
            left += [jnp.where(mine, hi, zero), jnp.where(mine, lo, zero)]
        hot = (low == jnp.broadcast_to(cell - 128.0 * upper, (128, 512)).astype(BF16)).astype(BF16)
        return acc + lax.dot_general(jnp.concatenate(left, axis=0), hot, NT, preferred_element_type=F32)

    acc = lax.fori_loop(0, N_DEV // 4, accumulate, jnp.zeros((128, 128), F32), unroll=True)
    sums = jnp.concatenate([acc[h * 32 : h * 32 + 16] + acc[h * 32 + 16 : h * 32 + 32] for h in range(4)], axis=1)
    area = jnp.maximum(sums[15:16, :] * (1.0 / 64.0), 1.0)
    horizon_ref[...] = sums[0:8] / area
    svf_ref[...] = sums[13:14] / area


def cells(got):
    return pl.pallas_call(
        cells_kernel,
        name="cells",
        out_shape=(jax.ShapeDtypeStruct((AZ, CELLS_DEV), F32), jax.ShapeDtypeStruct((1, CELLS_DEV), F32)),
        in_specs=[VMEM],
        out_specs=[VMEM] * 2,
        compiler_params=pltpu.CompilerParams(vmem_limit_bytes=8 * 1024 * 1024),
    )(got)


def shards(terrain_surface, azimuth_lag_tallies, holder_devices, holder_region_slot, footprint_weight):
    rows, width = terrain_surface.shape
    n_lat = lax.axis_size("lat")
    n_lon = lax.axis_size("lon")
    W = FARTHEST_LAG
    own = terrain_surface
    lat, lon = lax.axis_index("lat"), lax.axis_index("lon")
    odd = lon % 2

    def exchange(block, axis, size, first, wrap):
        pairs = []
        for i in range(first, size, 2):
            if i + 1 < size or wrap:
                pairs += [(i, (i + 1) % size), ((i + 1) % size, i)]
        return lax.ppermute(block, axis, pairs)

    def edge(block, at_end, dim):
        return lax.dynamic_slice_in_dim(block, jnp.where(at_end, block.shape[dim] - W, 0), W, axis=dim)

    far = exchange(edge(own, odd == 1, 1), "lon", n_lon, 1, True)
    near = exchange(edge(own, odd == 0, 1), "lon", n_lon, 0, True)
    weight = footprint_weight.reshape(NBR, 128)
    owner = holder_devices.reshape(NBR, 128)
    start, index, meta = route(owner, holder_region_slot.reshape(NBR, 128), weight)
    inv_lags = 1.0 / azimuth_lag_tallies.astype(F32)
    near, far, start, inv_lags = lax.optimization_barrier((near, far, start, inv_lags))
    west, east = jnp.where(odd == 1, near, far), jnp.where(odd == 1, far, near)

    def wide(at_end):
        return jnp.concatenate([edge(west, at_end, 0), edge(own, at_end, 0), edge(east, at_end, 0)], axis=1)

    other = exchange(wide(lat % 2 == 1), "lat", n_lat, 1, False)
    same = exchange(wide(lat % 2 == 0), "lat", n_lat, 0, False)

    rows_global = (lax.axis_index("lat") * rows + jnp.arange(rows, dtype=jnp.int32)).astype(F32)
    latitude = 47.0 - (rows_global + 0.5) / 1200.0
    coslat = jnp.cos(latitude * jnp.pi / 180.0)
    across = (pixel_size * coslat) ** 2
    inv_row = (1.0 / jnp.sqrt(across)).reshape(2, 128)
    inv_base = 1.0 / jnp.sqrt(pixel_size**2 + across)
    inv_base = jnp.broadcast_to(inv_base.reshape(32, 8).T[:, :, None], (8, 32, 128))
    place = jnp.stack([lat.astype(jnp.int32), jnp.int32(n_lat), odd.astype(jnp.int32)])
    part, sums, pooled = inner(azimuth_lag_tallies, inv_lags, place, own, near, far, inv_base, inv_row)
    fine_svf, packed = outer(
        azimuth_lag_tallies, inv_lags, start, place, own, same, other, near, far, inv_base, part, sums, pooled,
        weight, owner, index, meta,
    )
    packed = packed.reshape(N_DEV, 1, 11 * 128)
    got = lax.all_to_all(packed, ("lat", "lon"), split_axis=0, concat_axis=0, tiled=True)
    got = got.reshape(N_DEV * 11, 128)
    cell_horizon, cell_svf = cells(got)
    return fine_svf, cell_horizon, cell_svf.reshape(CELLS_DEV)


def solution(mesh):
    P = jax.sharding.PartitionSpec
    in_specs = (P("lat", "lon"), P(), P(("lat", "lon"), None), P(("lat", "lon")), P(("lat", "lon")))
    out_specs = (P("lat", "lon"), P(None, ("lat", "lon")), P(("lat", "lon")))
    return jax.shard_map(shards, mesh=mesh, in_specs=in_specs, out_specs=out_specs, check_vma=False)
```
